256 devices in a mesh: sec: 4 (over x_lo, core), gy: 64 (over x_hi, z, y).
Axes of the slice: x: 4 (x_hi: 2, x_lo: 2; x = x_hi * 2 + x_lo), y: 4, z: 8, core: 2. Of those that a mesh axis runs over, the one named last changes fastest.
Arguments:
- fluid_dist: float32 [19, 8, 64, 8192], P(None, None, 'sec', 'gy'), may hold values from 0.02 to 0.1
- order_dist: float32 [19, 8, 64, 8192], P(None, None, 'sec', 'gy'), may hold values from -0.12 to 0.12
- plane_offset: int32 [2, 4], replicated, may hold values from 0 to 2097151, as said below
- plane_speed: int32 [4], replicated, may hold values from 1 to 32
Outputs:
- fluid_next: float32 [19, 8, 64, 8192], P(None, None, 'sec', 'gy')
- order_next: float32 [19, 8, 64, 8192], P(None, None, 'sec', 'gy')
The draws below stay inside these ranges and needn't reach their ends.
Inputs may be any that keep to these rules, and one draw needn't show every extreme that they name: plane_offset[t, s] is the displacement along y, in 1/256 of a cell, of section s - 1 as seen from section s in step t. plane_speed[s] is the plane's sliding speed in 1/256 of a cell per step.
All inputs are finite; a program needn't handle non-finite values.
Results may differ from the reference program's by a relative error of at most 0.0001.
Values sent between devices are 32-bit elements; how exact they have to be, the bound alone decides.
A program may use at most 128 MiB of HBM per device.

```python
import jax
import jax.numpy as jnp
from jax import lax

LX = 16
LY = 128
NZ = 8
STEPS = 2
NX = 64
NY = 8192
N_SEC = 4


def draw_plane_offset(key, part):
    key = jax.random.fold_in(key, 11)
    key_base, key_half, key_pick, key_back, key_other = jax.random.split(key, 5)
    spread = jax.random.randint(key_base, (STEPS, N_SEC), 0, NY * 256, dtype=jnp.int32)
    halfway = NY // 2 * 256 + jax.random.randint(key_half, (STEPS, N_SEC), 0, LY * 256, dtype=jnp.int32)
    backward = (NY - LY) * 256 + jax.random.randint(key_back, (STEPS, N_SEC), 0, LY * 256, dtype=jnp.int32)
    picked = jax.random.randint(key_pick, (STEPS, 1), 0, N_SEC, dtype=jnp.int32)
    other = (picked + 1 + jax.random.randint(key_other, (STEPS, 1), 0, N_SEC - 1, dtype=jnp.int32)) % N_SEC
    sections = jnp.arange(N_SEC, dtype=jnp.int32)[None, :]
    result = jnp.where(sections == picked, halfway, spread)
    result = jnp.where(sections == other, backward, result)
    return result.astype(jnp.int32)


def place_ends(values, stream_key, smallest, largest):
    shape = values.shape
    index_at = [jax.random.randint(jax.random.fold_in(stream_key, axis), (), 0, shape[axis]) for axis in range(len(shape))]
    values = values.at[tuple(index_at)].set(smallest)
    longest = shape.index(max(shape))
    index_at[longest] = (index_at[longest] + 1) % shape[longest]
    return values.at[tuple(index_at)].set(largest)


def levels(own_key, dims, pieces, low, largest):
    gain, own = 1.0, jax.random.fold_in(own_key, 6)
    for position, blocks in pieces:
        draws = jnp.exp(jax.random.uniform(jax.random.fold_in(own, position), (blocks,), jnp.float32, low / len(pieces), largest / len(pieces)))
        gain = gain * jnp.repeat(draws, dims[position] // blocks).reshape([-1 if axis == position else 1 for axis in range(len(dims))])
    return gain


def setup_inputs(seed: int = 0) -> dict:
    key_list = jax.random.split(jax.random.key(seed), 5)
    fluid_dist = jnp.clip(0.02 + 0.08 * jax.random.uniform(key_list[0], (19, NZ, NX, NY), jnp.float32) ** levels(key_list[0], (19, NZ, NX, NY), ((2, 4), (3, 64)), -0.2, 0.2), 0.02, 0.1)
    order_dist = jnp.clip(jax.random.uniform(key_list[1], (19, NZ, NX, NY), jnp.float32, -0.12, 0.12) * levels(key_list[1], (19, NZ, NX, NY), ((2, 4), (3, 64)), -0.4, 0.0), -0.12, 0.12)
    plane_offset = draw_plane_offset(jax.random.fold_in(key_list[4], 71), 0)
    plane_speed = place_ends(jax.random.randint(key_list[3], (N_SEC,), 1, 33), jax.random.fold_in(key_list[3], 1), 1, 32).astype(jnp.int32)
    return dict(fluid_dist=fluid_dist, order_dist=order_dist, plane_offset=plane_offset, plane_speed=plane_speed)


VELOCITY = ((0, 0, 0), (1, 0, 0), (-1, 0, 0), (0, 1, 0), (0, -1, 0), (0, 0, 1), (0, 0, -1),
            (1, 1, 0), (-1, -1, 0), (1, -1, 0), (-1, 1, 0), (1, 0, 1), (-1, 0, -1), (1, 0, -1),
            (-1, 0, 1), (0, 1, 1), (0, -1, -1), (0, 1, -1), (0, -1, 1))
WEIGHTS = (1.0 / 3.0,) + (1.0 / 18.0,) * 6 + (1.0 / 36.0,) * 12
ALONG_X = tuple(vector[0] for vector in VELOCITY)
ALONG_Y = tuple(vector[1] for vector in VELOCITY)
ALONG_Z = tuple(vector[2] for vector in VELOCITY)
UPWARD = (1, 7, 9, 11, 13)
DOWNWARD = (2, 8, 10, 12, 14)
EVERY_ROW = tuple(range(19))
COEF_A = -0.0625
COEF_B = 0.0625
KAPPA_GRAD = 0.04
MOBILITY = 1.0
TAU_FLUID = 0.8
TAU_ORDER = 0.9


def column(values):
    return jnp.asarray(values, jnp.float32)[:, None, None, None]


def moment(field, values):
    return jnp.tensordot(jnp.asarray(values, jnp.float32), field, axes=1, precision=lax.Precision.HIGHEST)


def projected(rows, vel_x, vel_y, vel_z):
    along = (column([ALONG_X[entry] for entry in rows]) * vel_x
             + column([ALONG_Y[entry] for entry in rows]) * vel_y
             + column([ALONG_Z[entry] for entry in rows]) * vel_z)
    square = vel_x * vel_x + vel_y * vel_y + vel_z * vel_z
    return along, 3.0 * along + 4.5 * along * along - 1.5 * square


def collide(fluid, order, density, order_field, potential, force):
    force_x, force_y, force_z = force
    vel_x = (moment(fluid, ALONG_X) + 0.5 * force_x) / density
    vel_y = (moment(fluid, ALONG_Y) + 0.5 * force_y) / density
    vel_z = (moment(fluid, ALONG_Z) + 0.5 * force_z) / density
    along, shape = projected(EVERY_ROW, vel_x, vel_y, vel_z)
    weight = column(WEIGHTS)
    fluid_eq = weight * density * (1.0 + shape)
    pushed = column(ALONG_X) * force_x + column(ALONG_Y) * force_y + column(ALONG_Z) * force_z
    drift = vel_x * force_x + vel_y * force_y + vel_z * force_z
    source = (1.0 - 0.5 / TAU_FLUID) * weight * (3.0 * (pushed - drift) + 9.0 * along * pushed)
    fluid_post = fluid - (fluid - fluid_eq) / TAU_FLUID + source
    order_eq = weight * (3.0 * MOBILITY * potential + order_field * shape)
    resting = order_field - jnp.sum(order_eq[1:], axis=0)
    order_eq = jnp.concatenate([resting[None], order_eq[1:]], axis=0)
    order_post = order - (order - order_eq) / TAU_ORDER
    return fluid_post, order_post, (vel_x, vel_y, vel_z)


def frame_shift(fluid_post, order_post, density, order_field, velocity, layer, rows, jump):
    layer_cut = slice(layer, layer + 1)
    vel_x, vel_y, vel_z = [component[:, layer_cut, :] for component in velocity]
    before = projected(rows, vel_x, vel_y, vel_z)[1]
    after = projected(rows, vel_x, vel_y + jump, vel_z)[1]
    change = column([WEIGHTS[entry] for entry in rows]) * (after - before)
    fluid_rows = jnp.stack([fluid_post[entry, :, layer_cut, :] for entry in rows])
    order_rows = jnp.stack([order_post[entry, :, layer_cut, :] for entry in rows])
    return jnp.concatenate([fluid_rows + density[:, layer_cut, :] * change,
                            order_rows + order_field[:, layer_cut, :] * change], axis=0)


def slide(plane, units):
    whole = units // 256
    frac = (units % 256).astype(jnp.float32) / 256.0
    return (1.0 - frac) * jnp.roll(plane, -whole, axis=-1) + frac * jnp.roll(plane, -whole - 1, axis=-1)


def moved_row(post, row, lower_ghost, upper_ghost):
    base = row % 19
    shift_x, shift_y, shift_z = VELOCITY[base]
    lift = 5 if row >= 19 else 0
    if shift_x == 1:
        post = jnp.concatenate([lower_ghost[UPWARD.index(base) + lift], post[:, :-1, :]], axis=1)
    elif shift_x == -1:
        post = jnp.concatenate([post[:, 1:, :], upper_ghost[DOWNWARD.index(base) + lift]], axis=1)
    return jnp.roll(jnp.roll(post, shift_y, axis=2), shift_z, axis=0)


def section_part(array, section):
    return array[..., section * LX:(section + 1) * LX, :]


def advance(fluid, order, offsets, speeds):
    span = NY * 256
    order_field = jnp.sum(order, axis=0)
    density = jnp.sum(fluid, axis=0)
    rates = speeds.astype(jnp.float32) / 256.0
    sent_up = []
    sent_down = []
    posts = []
    for section in range(N_SEC):
        below = (section - 1) % N_SEC
        above = (section + 1) % N_SEC
        order_here = section_part(order_field, section)
        lower = slide(section_part(order_field, below)[:, LX - 2:, :], offsets[section])
        upper = slide(section_part(order_field, above)[:, :2, :], (span - offsets[above]) % span)
        extended = jnp.concatenate([lower, order_here, upper], axis=1)
        center = extended[:, 1:-1, :]
        laplace = (extended[:, 2:, :] + extended[:, :-2, :] + jnp.roll(center, -1, 2) + jnp.roll(center, 1, 2)
                   + jnp.roll(center, 1, 0) + jnp.roll(center, -1, 0) - 6.0 * center)
        potential = COEF_A * center + COEF_B * center * center * center - KAPPA_GRAD * laplace
        inner = potential[:, 1:-1, :]
        gradient = ((potential[:, 2:, :] - potential[:, :-2, :]) * 0.5,
                    (jnp.roll(inner, -1, 2) - jnp.roll(inner, 1, 2)) * 0.5,
                    (jnp.roll(inner, -1, 0) - jnp.roll(inner, 1, 0)) * 0.5)
        force = tuple(-order_here * entry for entry in gradient)
        density_here = section_part(density, section)
        fluid_post, order_post, velocity = collide(section_part(fluid, section), section_part(order, section),
                                                   density_here, order_here, inner, force)
        sent_down.append(frame_shift(fluid_post, order_post, density_here, order_here, velocity, 0, DOWNWARD,
                                     rates[section]))
        sent_up.append(frame_shift(fluid_post, order_post, density_here, order_here, velocity, LX - 1, UPWARD,
                                   -rates[above]))
        posts.append(jnp.concatenate([fluid_post, order_post], axis=0))
    fluid_parts = []
    order_parts = []
    for section in range(N_SEC):
        below = (section - 1) % N_SEC
        above = (section + 1) % N_SEC
        lower_ghost = slide(sent_up[below], offsets[section])
        upper_ghost = slide(sent_down[above], (span - offsets[above]) % span)
        rows_out = [moved_row(posts[section][row], row, lower_ghost, upper_ghost) for row in range(38)]
        fluid_parts.append(jnp.stack(rows_out[:19]))
        order_parts.append(jnp.stack(rows_out[19:]))
    return jnp.concatenate(fluid_parts, axis=2), jnp.concatenate(order_parts, axis=2)


def reference(fluid_dist, order_dist, plane_offset, plane_speed):
    fluid, order = fluid_dist, order_dist
    for step in range(STEPS):
        fluid, order = advance(fluid, order, plane_offset[step], plane_speed)
    return fluid, order
```

```python
import jax
import jax.numpy as jnp
from jax import lax
from jax.experimental import pallas as pl
from jax.experimental.pallas import tpu as pltpu
from jax.sharding import PartitionSpec as P

STEPS = 2
VELOCITY = (
    (0, 0, 0),
    (1, 0, 0),
    (-1, 0, 0),
    (0, 1, 0),
    (0, -1, 0),
    (0, 0, 1),
    (0, 0, -1),
    (1, 1, 0),
    (-1, -1, 0),
    (1, -1, 0),
    (-1, 1, 0),
    (1, 0, 1),
    (-1, 0, -1),
    (1, 0, -1),
    (-1, 0, 1),
    (0, 1, 1),
    (0, -1, -1),
    (0, 1, -1),
    (0, -1, 1),
)
WEIGHTS = (1.0 / 3.0,) + (1.0 / 18.0,) * 6 + (1.0 / 36.0,) * 12
UPWARD = (1, 7, 9, 11, 13)
DOWNWARD = (2, 8, 10, 12, 14)
Y_PLUS = (3, 7, 10, 15, 17)
Y_MINUS = (4, 8, 9, 16, 18)
COEF_A = -0.0625
COEF_B = 0.0625
KAPPA_GRAD = 0.04
MOBILITY = 1.0
TAU_FLUID = 0.8
TAU_ORDER = 0.9
NZ = 8
LX = 16
LY = 128
N_SEC = 4
N_GY = 64
SPAN = LY * N_GY * 256
ROLES = 20
MESH = pl.DeviceIdType.MESH


def lanes(shape):
    return lax.broadcasted_iota(jnp.int32, shape, len(shape) - 1)


def turn(value, shift):
    return pltpu.roll(value, shift, value.ndim - 1)


def signed_sum(terms, signs):
    total = None
    for term, sign in zip(terms, signs):
        if sign == 0:
            continue
        if total is None:
            total = term if sign > 0 else -term
        else:
            total = total + term if sign > 0 else total - term
    return total


def wait_bytes(ref, sem):
    pltpu.make_async_copy(ref, ref, sem).wait()


def slid_block(land, slot, block, offset):
    offset = offset & (LY * N_GY - 1)
    first = block + (offset >> 7)
    inside = offset & (LY - 1)
    here = land[slot, first & (N_GY - 1)]
    beyond = land[slot, (first + 1) & (N_GY - 1)]
    shift = (LY - inside) & (LY - 1)
    return jnp.where(lanes(here.shape) < LY - inside, turn(here, shift), turn(beyond, shift))


def kernel(
    fluid_in, order_in, offsets, speeds, fluid_out, order_out,
    state, post, field, pot, mom, face,
    a_up, a_down, a_edge, a_land, a_slid, a_ghost, a_near,
    b_send, b_edge, b_land, b_slid, b_ghost, b_near,
    in_sem, out_sem, send_sem, recv_sem,
):
    sec = lax.axis_index("sec")
    gy = lax.axis_index("gy")
    above = (sec + 1) & (N_SEC - 1)
    below = (sec + N_SEC - 1) & (N_SEC - 1)
    left = (gy + N_GY - 1) & (N_GY - 1)
    right = (gy + 1) & (N_GY - 1)
    is_down = gy & 1
    owner = gy >> 1
    a_z = owner & 7
    a_part = owner >> 3
    b_role = (5 * owner + 7) >> 3
    is_owner = jnp.logical_and((8 * b_role) // 5 == owner, b_role < ROLES)

    load_order = pltpu.make_async_copy(order_in, state.at[pl.ds(19, 19)], in_sem.at[0])
    load_order.start()
    load_fluid = pltpu.make_async_copy(fluid_in, state.at[pl.ds(0, 19)], in_sem.at[1])
    load_fluid.start()

    barrier = pltpu.get_barrier_semaphore()
    source_sec = jnp.where(is_down == 0, below, above)

    def greet_source(j, carry):
        pl.semaphore_signal(
            barrier, inc=1, device_id=(source_sec, (gy + j) & (N_GY - 1)), device_id_type=MESH
        )
        return carry

    def greet_own(j, carry):
        pl.semaphore_signal(
            barrier, inc=1, device_id=(sec, (gy + j) & (N_GY - 1)), device_id_type=MESH
        )
        return carry

    lax.fori_loop(0, N_GY, greet_source, 0, unroll=8)
    lax.fori_loop(1, N_GY, greet_own, 0, unroll=7)

    plane = (LX, LY)
    lane = lanes(plane)
    row = lax.broadcasted_iota(jnp.int32, plane, 0)
    field[...] = jnp.zeros_like(field)

    def order_pass():
        def one(z, carry):
            to_left, to_right = carry
            phi = state[19, z]
            for i in range(1, 19):
                phi = phi + state[19 + i, z]
            field[z, pl.ds(8, LX), pl.ds(0, LY)] = phi
            a_up[z] = phi[LX - 2 :]
            a_down[z] = phi[:2]
            mine = (lane >> 1) == z
            to_left = jnp.where(mine, turn(phi, 2 * z), to_left)
            to_right = jnp.where(mine, turn(phi, 2 * z + 2), to_right)
            return to_left, to_right

        zero = jnp.zeros(plane, jnp.float32)
        to_left, to_right = lax.fori_loop(0, NZ, one, (zero, zero))
        a_edge[0] = to_left
        a_edge[1] = to_right

    def send(src, dst, which, slot, to_sec, to_gy):
        pltpu.make_async_remote_copy(
            src_ref=src,
            dst_ref=dst,
            send_sem=send_sem.at[which],
            recv_sem=recv_sem.at[which, slot],
            device_id=(to_sec, to_gy),
            device_id_type=MESH,
        ).start()

    load_order.wait()
    order_pass()
    load_fluid.wait()
    pl.semaphore_wait(barrier, 2 * N_GY - 1)

    def step_body(step, carry):
        here_units = offsets[step, sec]
        next_units = offsets[step, above]
        units = jnp.where(is_down == 0, here_units, (SPAN - next_units) & (SPAN - 1))
        whole = units >> 8
        frac = (units & 255).astype(jnp.float32) * (1.0 / 256.0)
        keep = 1.0 - frac

        def send_order(j, carry):
            z = (j + gy) & (NZ - 1)
            for k in range(4):
                target = 2 * (8 * ((k + (gy >> 4)) & 3) + z)
                send(a_up.at[z], a_land.at[step, gy], 0, step, above, target)
                send(a_down.at[z], a_land.at[step, gy], 0, step, below, target + 1)
            return carry

        lax.fori_loop(0, NZ, send_order, 0, unroll=2)
        send(a_edge.at[0], a_near.at[step, 1], 1, step, sec, left)
        send(a_edge.at[1], a_near.at[step, 0], 1, step, sec, right)

        def moments(z, carry):
            tiles = [state[i, z] for i in range(19)]
            mom[0, z] = signed_sum(tiles, (1,) * 19)
            for axis in range(3):
                mom[1 + axis, z] = signed_sum(tiles, [vector[axis] for vector in VELOCITY])
            return carry

        lax.fori_loop(0, NZ, moments, 0)

        wait_bytes(a_land.at[step], recv_sem.at[0, step])

        def slide_order(block):
            values = [slid_block(a_land, step, block, whole + shift) for shift in (-1, 0, 1, 2)]
            for k in range(3):
                a_slid[block & 15, k] = keep * values[k] + frac * values[k + 1]

        a_role = 8 * is_down + a_z
        slide_order(gy)
        pltpu.make_async_copy(
            a_slid.at[gy & 15], a_ghost.at[step, a_role], recv_sem.at[2, step]
        ).start()

        def send_slid_order(j, carry):
            block = 16 * a_part + ((gy + j) & 15)
            slide_order(block)
            send(a_slid.at[block & 15], a_ghost.at[step, a_role], 2, step, sec, block)
            return carry

        lax.fori_loop(1, 16, send_slid_order, 0, unroll=5)

        wait_bytes(a_near.at[step], recv_sem.at[1, step])
        from_left = a_near[step, 0]
        from_right = a_near[step, 1]

        def put_columns(z, carry):
            field[z, pl.ds(8, LX), pl.ds(LY, LY)] = jnp.where(
                lane < 2,
                turn(from_right, (LY - 2 * z) & (LY - 1)),
                jnp.where(lane >= LY - 2, turn(from_left, (LY - 2 - 2 * z) & (LY - 1)), 0.0),
            )
            return carry

        lax.fori_loop(0, NZ, put_columns, 0)

        wait_bytes(a_ghost.at[step], recv_sem.at[2, step])
        pair = lanes((2, LY))

        def put_ghosts(z, carry):
            for side, start in ((0, 6), (1, 24)):
                rows = [a_ghost[step, 8 * side + z, k] for k in range(3)]
                field[z, pl.ds(start, 2), pl.ds(0, LY)] = rows[1]
                field[z, pl.ds(start, 2), pl.ds(LY, LY)] = jnp.where(
                    pair == 0, turn(rows[2], 1), jnp.where(pair == LY - 1, turn(rows[0], LY - 1), 0.0)
                )
            return carry

        lax.fori_loop(0, NZ, put_ghosts, 0)

        def potentials(z, carry):
            tall = lanes((32, LY))
            tiles = [field[z, :, pl.ds(0, LY)], field[z, :, pl.ds(LY, LY)]]
            ahead = [turn(tile, LY - 1) for tile in tiles]
            behind = [turn(tile, 1) for tile in tiles]
            for k in range(2):
                tile = tiles[k]
                cut = pl.ds(k * LY, LY)
                lap = (
                    pltpu.roll(tile, 1, 0)
                    + pltpu.roll(tile, 31, 0)
                    + jnp.where(tall == LY - 1, ahead[1 - k], ahead[k])
                    + jnp.where(tall == 0, behind[1 - k], behind[k])
                    + field[(z + 1) & 7, :, cut]
                    + field[(z + 7) & 7, :, cut]
                    - 6.0 * tile
                )
                pot[z, :, cut] = tile * (COEF_A + COEF_B * tile * tile) - KAPPA_GRAD * lap
            return carry

        lax.fori_loop(0, NZ, potentials, 0)

        def collide(z, carry):
            to_left, to_right = carry
            own = pl.ds(0, LY)
            inner = pot[z, pl.ds(8, LX), own]
            halo = pot[z, pl.ds(8, LX), pl.ds(LY, LY)]
            phi = field[z, pl.ds(8, LX), own]
            half = -0.5 * phi
            force = (
                half * (pot[z, pl.ds(9, LX), own] - pot[z, pl.ds(7, LX), own]),
                half
                * (
                    jnp.where(lane == LY - 1, turn(halo, LY - 1), turn(inner, LY - 1))
                    - jnp.where(lane == 0, turn(halo, 1), turn(inner, 1))
                ),
                half * (pot[(z + 1) & 7, pl.ds(8, LX), own] - pot[(z + 7) & 7, pl.ds(8, LX), own]),
            )
            density = mom[0, z]
            inverse = 1.0 / density
            vel = tuple((mom[1 + k, z] + 0.5 * force[k]) * inverse for k in range(3))
            square = vel[0] * vel[0] + vel[1] * vel[1] + vel[2] * vel[2]
            drift = vel[0] * force[0] + vel[1] * force[1] + vel[2] * force[2]
            kick = 1.0 - 0.5 / TAU_FLUID
            scaled = density * (1.0 / TAU_FLUID)
            base = scaled * (1.0 - 1.5 * square) - (3.0 * kick) * drift
            square_phi = phi * (1.0 / TAU_ORDER)
            base_phi = (3.0 * MOBILITY / TAU_ORDER) * inner - 1.5 * square_phi * square
            left_f = 1.0 - 1.0 / TAU_FLUID
            left_g = 1.0 - 1.0 / TAU_ORDER
            fluid = [None] * 19
            order = [None] * 19
            fluid[0] = left_f * state[0, z] + WEIGHTS[0] * base
            order[0] = left_g * state[19, z] + (
                square_phi * (1.0 - 0.5 * square) - (2.0 * MOBILITY / TAU_ORDER) * inner
            )
            for i in range(1, 19, 2):
                vector = VELOCITY[i]
                along = signed_sum(vel, vector)
                pushed = signed_sum(force, vector)
                weight = WEIGHTS[i]
                even = weight * (base + along * (4.5 * scaled * along + (9.0 * kick) * pushed))
                odd = weight * (3.0 * scaled * along + (3.0 * kick) * pushed)
                fluid[i] = left_f * state[i, z] + (even + odd)
                fluid[i + 1] = left_f * state[i + 1, z] + (even - odd)
                carried = square_phi * along
                even = weight * (base_phi + 4.5 * carried * along)
                odd = (3.0 * weight) * carried
                order[i] = left_g * state[19 + i, z] + (even + odd)
                order[i + 1] = left_g * state[20 + i, z] + (even - odd)
            for i in range(19):
                post[i, z] = fluid[i]
                post[19 + i, z] = order[i]
            for side, members, x in ((0, UPWARD, LX - 1), (1, DOWNWARD, 0)):
                rows = [fluid[i] for i in members] + [order[i] for i in members]
                rows += [density, phi, vel[0], vel[1], vel[2]]
                for k, tile in enumerate(rows):
                    face[side, k, pl.ds(z, 1), :] = tile[x : x + 1, :]
            going_left = jnp.zeros(plane, jnp.float32)
            going_right = jnp.zeros(plane, jnp.float32)
            for k in range(10):
                part = fluid if k < 5 else order
                going_right = jnp.where(
                    lane == 8 * k, turn(part[Y_PLUS[k % 5]], 8 * k + 1), going_right
                )
                going_left = jnp.where(
                    lane == 8 * k, turn(part[Y_MINUS[k % 5]], 8 * k), going_left
                )
            mine = (lane & 7) == z
            to_left = jnp.where(mine, turn(going_left, z), to_left)
            to_right = jnp.where(mine, turn(going_right, z), to_right)
            return to_left, to_right

        zero = jnp.zeros(plane, jnp.float32)
        to_left, to_right = lax.fori_loop(0, NZ, collide, (zero, zero))
        b_edge[0] = to_left
        b_edge[1] = to_right

        jump_up = speeds[above].astype(jnp.float32) * (-1.0 / 256.0)
        jump_down = speeds[sec].astype(jnp.float32) * (1.0 / 256.0)
        for side, members, jump in ((0, UPWARD, jump_up), (1, DOWNWARD, jump_down)):
            density, phi, vel_x, vel_y, vel_z = [face[side, 10 + k] for k in range(5)]
            moved = vel_y + jump
            change_square = 1.5 * (moved * moved - vel_y * vel_y)
            for k, i in enumerate(members):
                vector = VELOCITY[i]
                before = signed_sum((vel_x, vel_y, vel_z), vector)
                after = signed_sum((vel_x, moved, vel_z), vector)
                change = WEIGHTS[i] * (
                    3.0 * (after - before) + 4.5 * (after * after - before * before) - change_square
                )
                for lift, mass in ((0, density), (5, phi)):
                    value = face[side, k + lift] + mass * change
                    b_send[side, 2 * (k + lift)] = value[:4]
                    b_send[side, 2 * (k + lift) + 1] = value[4:]

        def send_ghost(j, carry):
            role = lax.rem(j + gy, ROLES)
            target = 2 * ((8 * role) // 5)
            send(b_send.at[0, role], b_land.at[step, gy], 3, step, above, target)
            send(b_send.at[1, role], b_land.at[step, gy], 3, step, below, target + 1)
            return carry

        lax.fori_loop(0, ROLES, send_ghost, 0, unroll=5)
        send(b_edge.at[0], b_near.at[step, 1], 4, step, sec, left)
        send(b_edge.at[1], b_near.at[step, 0], 4, step, sec, right)

        @pl.when(is_owner)
        def _():
            wait_bytes(b_land.at[step], recv_sem.at[3, step])
            member = lax.rem(b_role >> 1, 5)
            along_y = jnp.where(member == 1, 1, jnp.where(member == 2, -1, 0)) * (1 - 2 * is_down)
            start = whole - along_y
            b_slot = ROLES * is_down + b_role

            def slide_ghost(block):
                b_slid[block] = keep * slid_block(b_land, step, block, start) + frac * slid_block(
                    b_land, step, block, start + 1
                )

            slide_ghost(gy)
            pltpu.make_async_copy(
                b_slid.at[gy], b_ghost.at[step, b_slot], recv_sem.at[5, step]
            ).start()

            def send_slid_ghost(j, carry):
                block = (gy + j) & (N_GY - 1)
                slide_ghost(block)
                send(b_slid.at[block], b_ghost.at[step, b_slot], 5, step, sec, block)
                return carry

            lax.fori_loop(1, N_GY, send_slid_ghost, 0, unroll=7)

        wait_bytes(b_near.at[step], recv_sem.at[4, step])
        near_left = b_near[step, 0]
        near_right = b_near[step, 1]

        def stream(z, carry):
            columns = {}
            for shift_z in (-1, 0, 1):
                source = (z - shift_z) & 7
                back = (LY - source) & (LY - 1)
                columns[1, shift_z] = turn(near_left, back)
                columns[-1, shift_z] = turn(near_right, back)
            for which in range(38):
                i = which % 19
                shift_x, shift_y, shift_z = VELOCITY[i]
                tile = post[which, (z - shift_z) & 7]
                if shift_y == 1:
                    k = Y_PLUS.index(i) + (5 if which >= 19 else 0)
                    outer = turn(columns[1, shift_z], (LY - 8 * k) % LY)
                    tile = jnp.where(lane == 0, outer, turn(tile, 1))
                elif shift_y == -1:
                    k = Y_MINUS.index(i) + (5 if which >= 19 else 0)
                    outer = turn(columns[-1, shift_z], (LY - 1 - 8 * k) % LY)
                    tile = jnp.where(lane == LY - 1, outer, turn(tile, LY - 1))
                if shift_x:
                    tile = pltpu.roll(tile, shift_x % LX, 0)
                state[which, z] = tile
            return carry

        lax.fori_loop(0, NZ, stream, 0)

        wait_bytes(a_land.at[step], send_sem.at[0])
        wait_bytes(a_edge, send_sem.at[1])
        wait_bytes(a_slid.at[pl.ds(0, 15)], send_sem.at[2])
        wait_bytes(b_send, send_sem.at[3])
        wait_bytes(b_edge, send_sem.at[4])

        @pl.when(is_owner)
        def _():
            wait_bytes(b_slid.at[pl.ds(0, N_GY - 1)], send_sem.at[5])

        wait_bytes(b_ghost.at[step], recv_sem.at[5, step])
        for side, members, x in ((0, UPWARD, 0), (1, DOWNWARD, LX - 1)):
            for k in range(10):
                i = members[k % 5]
                which = i + (19 if k >= 5 else 0)
                for z in range(NZ):
                    source = (z - VELOCITY[i][2]) % NZ
                    slot = ROLES * side + 2 * k + source // 4
                    state[which, z, pl.ds(x, 1), :] = b_ghost[step, slot, pl.ds(source % 4, 1), :]

        @pl.when(step < STEPS - 1)
        def _():
            order_pass()

        return carry

    lax.fori_loop(0, STEPS, step_body, 0)
    store_fluid = pltpu.make_async_copy(state.at[pl.ds(0, 19)], fluid_out, out_sem.at[0])
    store_order = pltpu.make_async_copy(state.at[pl.ds(19, 19)], order_out, out_sem.at[1])
    store_fluid.start()
    store_order.start()
    store_fluid.wait()
    store_order.wait()


def per_device(fluid_dist, order_dist, plane_offset, plane_speed):
    shape = jax.ShapeDtypeStruct((19, NZ, LX, LY), jnp.float32)

    def scratch(*dims):
        return pltpu.VMEM(dims, jnp.float32)

    return pl.pallas_call(
        kernel,
        out_shape=(shape, shape),
        in_specs=[
            pl.BlockSpec(memory_space=pl.ANY),
            pl.BlockSpec(memory_space=pl.ANY),
            pl.BlockSpec(memory_space=pltpu.SMEM),
            pl.BlockSpec(memory_space=pltpu.SMEM),
        ],
        out_specs=(pl.BlockSpec(memory_space=pl.ANY), pl.BlockSpec(memory_space=pl.ANY)),
        scratch_shapes=[
            scratch(38, NZ, LX, LY),
            scratch(38, NZ, LX, LY),
            scratch(NZ, 32, 2 * LY),
            scratch(NZ, 32, 2 * LY),
            scratch(4, NZ, LX, LY),
            scratch(2, 15, NZ, LY),
            scratch(NZ, 2, LY),
            scratch(NZ, 2, LY),
            scratch(2, LX, LY),
            scratch(STEPS, N_GY, 2, LY),
            scratch(16, 3, 2, LY),
            scratch(STEPS, 16, 3, 2, LY),
            scratch(STEPS, 2, LX, LY),
            scratch(2, ROLES, 4, LY),
            scratch(2, LX, LY),
            scratch(STEPS, N_GY, 4, LY),
            scratch(N_GY, 4, LY),
            scratch(STEPS, 2 * ROLES, 4, LY),
            scratch(STEPS, 2, LX, LY),
            pltpu.SemaphoreType.DMA((2,)),
            pltpu.SemaphoreType.DMA((2,)),
            pltpu.SemaphoreType.DMA((6,)),
            pltpu.SemaphoreType.DMA((6, STEPS)),
        ],
        compiler_params=pltpu.CompilerParams(
            collective_id=0, has_side_effects=True, vmem_limit_bytes=40 * 1024 * 1024
        ),
    )(fluid_dist, order_dist, plane_offset, plane_speed)


def solution(mesh):
    split = P(None, None, "sec", "gy")
    return jax.shard_map(
        per_device,
        mesh=mesh,
        in_specs=(split, split, P(), P()),
        out_specs=(split, split),
        check_vma=False,
    )
```

```python
import jax
import jax.numpy as jnp
from jax import lax
from jax.experimental import pallas as pl
from jax.experimental.pallas import tpu as pltpu
from jax.sharding import PartitionSpec as P

STEPS = 2
VELOCITY = (
    (0, 0, 0),
    (1, 0, 0),
    (-1, 0, 0),
    (0, 1, 0),
    (0, -1, 0),
    (0, 0, 1),
    (0, 0, -1),
    (1, 1, 0),
    (-1, -1, 0),
    (1, -1, 0),
    (-1, 1, 0),
    (1, 0, 1),
    (-1, 0, -1),
    (1, 0, -1),
    (-1, 0, 1),
    (0, 1, 1),
    (0, -1, -1),
    (0, 1, -1),
    (0, -1, 1),
)
WEIGHTS = (1.0 / 3.0,) + (1.0 / 18.0,) * 6 + (1.0 / 36.0,) * 12
UPWARD = (1, 7, 9, 11, 13)
DOWNWARD = (2, 8, 10, 12, 14)
Y_PLUS = (3, 7, 10, 15, 17)
Y_MINUS = (4, 8, 9, 16, 18)
COEF_A = -0.0625
COEF_B = 0.0625
KAPPA_GRAD = 0.04
MOBILITY = 1.0
TAU_FLUID = 0.8
TAU_ORDER = 0.9
NZ = 8
LX = 16
LY = 128
N_SEC = 4
N_GY = 64
SPAN = LY * N_GY * 256
ROLES = 20
MESH = pl.DeviceIdType.MESH
ACROSS = ((1, 2), (1, 1), (1, 3), (0, 2), (1, 0), (0, 1), (0, 3), (0, 0))


def lanes(shape):
    return lax.broadcasted_iota(jnp.int32, shape, len(shape) - 1)


def turn(value, shift):
    return pltpu.roll(value, shift, value.ndim - 1)


def ring_z(gy, k):
    half = (k + 1) >> 1
    return ((gy >> 2) + 4 + jnp.where((k & 1) == 1, -half, half)) & 7


def far_first(gy, k, m):
    across, along = ACROSS[m]
    return (((gy >> 5) ^ across) << 5) + (ring_z(gy, k) << 2) + ((gy + along) & 3)


def signed_sum(terms, signs):
    total = None
    for term, sign in zip(terms, signs):
        if sign == 0:
            continue
        if total is None:
            total = term if sign > 0 else -term
        else:
            total = total + term if sign > 0 else total - term
    return total


def wait_bytes(ref, sem):
    pltpu.make_async_copy(ref, ref, sem).wait()


def slid_block(land, slot, block, offset):
    offset = offset & (LY * N_GY - 1)
    first = block + (offset >> 7)
    inside = offset & (LY - 1)
    here = land[slot, first & (N_GY - 1)]
    beyond = land[slot, (first + 1) & (N_GY - 1)]
    shift = (LY - inside) & (LY - 1)
    return jnp.where(lanes(here.shape) < LY - inside, turn(here, shift), turn(beyond, shift))


def kernel(
    fluid_in, order_in, offsets_in, speeds_in, fluid_out, order_out,
    offsets, speeds, state, post, field, pot, mom,
    a_up, a_down, a_edge, a_land, a_slid, a_ghost, a_near,
    b_send, b_edge, b_land, b_slid, b_ghost, b_near,
    in_sem, out_sem, send_sem, recv_sem,
):
    sec = lax.axis_index("sec")
    gy = lax.axis_index("gy")
    above = (sec + 1) & (N_SEC - 1)
    below = (sec + N_SEC - 1) & (N_SEC - 1)
    left = (gy + N_GY - 1) & (N_GY - 1)
    right = (gy + 1) & (N_GY - 1)
    is_down = gy & 1
    owner = gy >> 1
    a_z = owner & 7
    a_part = owner >> 3
    b_role = (5 * owner + 7) >> 3
    is_owner = jnp.logical_and((8 * b_role) // 5 == owner, b_role < ROLES)

    load_order = pltpu.make_async_copy(order_in, state.at[pl.ds(19, 19)], in_sem.at[0])
    load_order.start()
    load_offsets = pltpu.make_async_copy(offsets_in, offsets, in_sem.at[2])
    load_offsets.start()
    load_speeds = pltpu.make_async_copy(speeds_in, speeds, in_sem.at[3])
    load_speeds.start()
    load_fluid = pltpu.make_async_copy(fluid_in, state.at[pl.ds(0, 19)], in_sem.at[1])
    load_fluid.start()

    barrier = pltpu.get_barrier_semaphore()
    source_sec = jnp.where(is_down == 0, below, above)

    def greet(k, carry):
        for m in range(8):
            other = far_first(gy, k, m)
            pl.semaphore_signal(
                barrier, inc=1, device_id=(source_sec, other), device_id_type=MESH
            )
            if m < 7:
                pl.semaphore_signal(barrier, inc=1, device_id=(sec, other), device_id_type=MESH)
        return carry

    def greet_rest(k, carry):
        pl.semaphore_signal(
            barrier, inc=1, device_id=(sec, far_first(gy, k, 7)), device_id_type=MESH
        )
        return carry

    lax.fori_loop(0, 8, greet, 0)
    lax.fori_loop(0, 7, greet_rest, 0)

    plane = (LX, LY)
    lane = lanes(plane)
    row = lax.broadcasted_iota(jnp.int32, plane, 0)
    field[...] = jnp.zeros_like(field)

    def order_pass():
        def one(z, carry):
            phi = state[19, z]
            for i in range(1, 19):
                phi = phi + state[19 + i, z]
            field[z, pl.ds(8, LX), pl.ds(0, LY)] = phi
            return carry

        lax.fori_loop(0, NZ, one, 0)

    def pack_order():
        for j in range(2):
            a_up[:, j, :] = field[:, 8 + LX - 2 + j, pl.ds(0, LY)]
            a_down[:, j, :] = field[:, 8 + j, pl.ds(0, LY)]
        to_left = jnp.zeros(plane, jnp.float32)
        to_right = to_left
        for z in range(NZ):
            phi = field[z, pl.ds(8, LX), pl.ds(0, LY)]
            mine = (lane >> 1) == z
            to_left = jnp.where(mine, turn(phi, 2 * z), to_left)
            to_right = jnp.where(mine, turn(phi, 2 * z + 2), to_right)
        a_edge[0] = to_left
        a_edge[1] = to_right

    def next_y(near, far):
        tile = lanes(near.shape)
        return jnp.where(tile == LY - 1, turn(far, LY - 1), turn(near, LY - 1))

    def last_y(near, far):
        tile = lanes(near.shape)
        return jnp.where(tile == 0, turn(far, 1), turn(near, 1))

    def face_potential(x, half):
        cut = pl.ds(half * LY, LY)
        tile = field[:, 8 + x, cut]
        other = field[:, 8 + x, pl.ds((1 - half) * LY, LY)]
        lap = (
            field[:, 9 + x, cut]
            + field[:, 7 + x, cut]
            + next_y(tile, other)
            + last_y(tile, other)
            + pltpu.roll(tile, 1, 0)
            + pltpu.roll(tile, NZ - 1, 0)
            - 6.0 * tile
        )
        return tile * (COEF_A + COEF_B * tile * tile) - KAPPA_GRAD * lap

    def face_collide(side, members, x, jump):
        phi = field[:, 8 + x, pl.ds(0, LY)]
        middle = face_potential(x, 0)
        beyond = face_potential(x, 1)
        half = -0.5 * phi
        force = (
            half * (face_potential(x + 1, 0) - face_potential(x - 1, 0)),
            half * (next_y(middle, beyond) - last_y(middle, beyond)),
            half * (pltpu.roll(middle, NZ - 1, 0) - pltpu.roll(middle, 1, 0)),
        )
        density = mom[0, :, x, :]
        inverse = 1.0 / density
        vel = tuple((mom[1 + k, :, x, :] + 0.5 * force[k]) * inverse for k in range(3))
        square = vel[0] * vel[0] + vel[1] * vel[1] + vel[2] * vel[2]
        drift = vel[0] * force[0] + vel[1] * force[1] + vel[2] * force[2]
        kick = 1.0 - 0.5 / TAU_FLUID
        scaled = density * (1.0 / TAU_FLUID)
        base = scaled * (1.0 - 1.5 * square) - (3.0 * kick) * drift
        square_phi = phi * (1.0 / TAU_ORDER)
        base_phi = (3.0 * MOBILITY / TAU_ORDER) * middle - 1.5 * square_phi * square
        moved = vel[1] + jump
        change_square = 1.5 * (moved * moved - vel[1] * vel[1])
        for k, i in enumerate(members):
            vector = VELOCITY[i]
            weight = WEIGHTS[i]
            along = signed_sum(vel, vector)
            pushed = signed_sum(force, vector)
            after = signed_sum((vel[0], moved, vel[2]), vector)
            change = weight * (
                3.0 * (after - along) + 4.5 * (after * after - along * along) - change_square
            )
            fluid = (1.0 - 1.0 / TAU_FLUID) * state[i, :, x, :] + weight * (
                base
                + along * (4.5 * scaled * along + (9.0 * kick) * pushed)
                + (3.0 * scaled * along + (3.0 * kick) * pushed)
            )
            carried = square_phi * along
            order = (1.0 - 1.0 / TAU_ORDER) * state[19 + i, :, x, :] + weight * (
                base_phi + 4.5 * carried * along + 3.0 * carried
            )
            for lift, value in ((0, fluid + density * change), (5, order + phi * change)):
                b_send[side, 2 * (k + lift)] = value[:4]
                b_send[side, 2 * (k + lift) + 1] = value[4:]

    def send(src, dst, which, slot, to_sec, to_gy):
        pltpu.make_async_remote_copy(
            src_ref=src,
            dst_ref=dst,
            send_sem=send_sem.at[which],
            recv_sem=recv_sem.at[which, slot],
            device_id=(to_sec, to_gy),
            device_id_type=MESH,
        ).start()

    load_order.wait()
    order_pass()
    pack_order()
    load_fluid.wait()
    load_offsets.wait()
    load_speeds.wait()
    pl.semaphore_wait(barrier, 2 * N_GY - 1)

    def step_body(step, carry):
        here_units = offsets[step, sec]
        next_units = offsets[step, above]
        units = jnp.where(is_down == 0, here_units, (SPAN - next_units) & (SPAN - 1))
        whole = units >> 8
        frac = (units & 255).astype(jnp.float32) * (1.0 / 256.0)
        keep = 1.0 - frac

        def send_order(k, carry):
            for across, along in ((1, 1), (1, 0), (0, 1), (0, 0)):
                target = (
                    (((gy >> 5) ^ across) << 5) + (ring_z(gy, k) << 2) + ((gy & 2) ^ (2 * along))
                )
                z = (target >> 1) & 7
                send(a_up.at[z], a_land.at[step, gy], 0, step, above, target)
                send(a_down.at[z], a_land.at[step, gy], 0, step, below, target + 1)
            return carry

        lax.fori_loop(0, 8, send_order, 0, unroll=2)
        send(a_edge.at[0], a_near.at[step, 1], 1, step, sec, left)
        send(a_edge.at[1], a_near.at[step, 0], 1, step, sec, right)

        def moments(z, carry):
            tiles = [state[i, z] for i in range(19)]
            mom[0, z] = signed_sum(tiles, (1,) * 19)
            for axis in range(3):
                mom[1 + axis, z] = signed_sum(tiles, [vector[axis] for vector in VELOCITY])
            return carry

        lax.fori_loop(0, NZ, moments, 0)

        wait_bytes(a_land.at[step], recv_sem.at[0, step])

        def slide_order(block):
            values = [slid_block(a_land, step, block, whole + shift) for shift in (-1, 0, 1, 2)]
            for k in range(3):
                a_slid[block & 15, k] = keep * values[k] + frac * values[k + 1]

        a_role = 8 * is_down + a_z
        slide_order(gy)
        pltpu.make_async_copy(
            a_slid.at[gy & 15], a_ghost.at[step, a_role], recv_sem.at[2, step]
        ).start()

        def send_slid_order(j, carry):
            block = gy ^ (16 - j)
            slide_order(block)
            send(a_slid.at[block & 15], a_ghost.at[step, a_role], 2, step, sec, block)
            return carry

        lax.fori_loop(1, 16, send_slid_order, 0, unroll=5)

        wait_bytes(a_near.at[step], recv_sem.at[1, step])
        from_left = a_near[step, 0]
        from_right = a_near[step, 1]

        def put_columns(z, carry):
            field[z, pl.ds(8, LX), pl.ds(LY, LY)] = jnp.where(
                lane < 2,
                turn(from_right, (LY - 2 * z) & (LY - 1)),
                jnp.where(lane >= LY - 2, turn(from_left, (LY - 2 - 2 * z) & (LY - 1)), 0.0),
            )
            return carry

        lax.fori_loop(0, NZ, put_columns, 0)

        wait_bytes(a_ghost.at[step], recv_sem.at[2, step])
        rim = lanes((NZ, LY))
        for side, near_x, far_x in ((0, -1, -2), (1, LX, LX + 1)):
            roles = pl.ds(8 * side, 8)
            place = 1 - side
            field[:, 8 + near_x, pl.ds(0, LY)] = a_ghost[step, roles, 1, place, :]
            field[:, 8 + far_x, pl.ds(0, LY)] = a_ghost[step, roles, 1, 1 - place, :]
            field[:, 8 + near_x, pl.ds(LY, LY)] = jnp.where(
                rim == 0,
                turn(a_ghost[step, roles, 2, place, :], 1),
                jnp.where(rim == LY - 1, turn(a_ghost[step, roles, 0, place, :], LY - 1), 0.0),
            )

        jump_up = speeds[above].astype(jnp.float32) * (-1.0 / 256.0)
        jump_down = speeds[sec].astype(jnp.float32) * (1.0 / 256.0)
        face_collide(0, UPWARD, LX - 1, jump_up)
        face_collide(1, DOWNWARD, 0, jump_down)

        def send_ghost(j, carry):
            role = lax.rem(j + gy, ROLES)
            target = 2 * ((8 * role) // 5)
            send(b_send.at[0, role], b_land.at[step, gy], 3, step, above, target)
            send(b_send.at[1, role], b_land.at[step, gy], 3, step, below, target + 1)
            return carry

        lax.fori_loop(0, ROLES, send_ghost, 0, unroll=5)

        def potentials(z, carry):
            tall = lanes((32, LY))
            tiles = [field[z, :, pl.ds(0, LY)], field[z, :, pl.ds(LY, LY)]]
            ahead = [turn(tile, LY - 1) for tile in tiles]
            behind = [turn(tile, 1) for tile in tiles]
            for k in range(2):
                tile = tiles[k]
                cut = pl.ds(k * LY, LY)
                lap = (
                    pltpu.roll(tile, 1, 0)
                    + pltpu.roll(tile, 31, 0)
                    + jnp.where(tall == LY - 1, ahead[1 - k], ahead[k])
                    + jnp.where(tall == 0, behind[1 - k], behind[k])
                    + field[(z + 1) & 7, :, cut]
                    + field[(z + 7) & 7, :, cut]
                    - 6.0 * tile
                )
                pot[z, :, cut] = tile * (COEF_A + COEF_B * tile * tile) - KAPPA_GRAD * lap
            return carry

        lax.fori_loop(0, NZ, potentials, 0)

        def collide(z, carry):
            to_left, to_right = carry
            own = pl.ds(0, LY)
            inner = pot[z, pl.ds(8, LX), own]
            halo = pot[z, pl.ds(8, LX), pl.ds(LY, LY)]
            phi = field[z, pl.ds(8, LX), own]
            half = -0.5 * phi
            force = (
                half * (pot[z, pl.ds(9, LX), own] - pot[z, pl.ds(7, LX), own]),
                half
                * (
                    jnp.where(lane == LY - 1, turn(halo, LY - 1), turn(inner, LY - 1))
                    - jnp.where(lane == 0, turn(halo, 1), turn(inner, 1))
                ),
                half * (pot[(z + 1) & 7, pl.ds(8, LX), own] - pot[(z + 7) & 7, pl.ds(8, LX), own]),
            )
            density = mom[0, z]
            inverse = 1.0 / density
            vel = tuple((mom[1 + k, z] + 0.5 * force[k]) * inverse for k in range(3))
            square = vel[0] * vel[0] + vel[1] * vel[1] + vel[2] * vel[2]
            drift = vel[0] * force[0] + vel[1] * force[1] + vel[2] * force[2]
            kick = 1.0 - 0.5 / TAU_FLUID
            scaled = density * (1.0 / TAU_FLUID)
            base = scaled * (1.0 - 1.5 * square) - (3.0 * kick) * drift
            square_phi = phi * (1.0 / TAU_ORDER)
            base_phi = (3.0 * MOBILITY / TAU_ORDER) * inner - 1.5 * square_phi * square
            left_f = 1.0 - 1.0 / TAU_FLUID
            left_g = 1.0 - 1.0 / TAU_ORDER
            fluid = [None] * 19
            order = [None] * 19
            fluid[0] = left_f * state[0, z] + WEIGHTS[0] * base
            order[0] = left_g * state[19, z] + (
                square_phi * (1.0 - 0.5 * square) - (2.0 * MOBILITY / TAU_ORDER) * inner
            )
            for i in range(1, 19, 2):
                vector = VELOCITY[i]
                along = signed_sum(vel, vector)
                pushed = signed_sum(force, vector)
                weight = WEIGHTS[i]
                even = weight * (base + along * (4.5 * scaled * along + (9.0 * kick) * pushed))
                odd = weight * (3.0 * scaled * along + (3.0 * kick) * pushed)
                fluid[i] = left_f * state[i, z] + (even + odd)
                fluid[i + 1] = left_f * state[i + 1, z] + (even - odd)
                carried = square_phi * along
                even = weight * (base_phi + 4.5 * carried * along)
                odd = (3.0 * weight) * carried
                order[i] = left_g * state[19 + i, z] + (even + odd)
                order[i + 1] = left_g * state[20 + i, z] + (even - odd)
            for i in range(19):
                post[i, z] = fluid[i]
                post[19 + i, z] = order[i]
            going_left = jnp.zeros(plane, jnp.float32)
            going_right = jnp.zeros(plane, jnp.float32)
            for k in range(10):
                part = fluid if k < 5 else order
                going_right = jnp.where(
                    lane == 8 * k, turn(part[Y_PLUS[k % 5]], 8 * k + 1), going_right
                )
                going_left = jnp.where(
                    lane == 8 * k, turn(part[Y_MINUS[k % 5]], 8 * k), going_left
                )
            mine = (lane & 7) == z
            to_left = jnp.where(mine, turn(going_left, z), to_left)
            to_right = jnp.where(mine, turn(going_right, z), to_right)
            return to_left, to_right

        zero = jnp.zeros(plane, jnp.float32)
        to_left, to_right = lax.fori_loop(0, NZ, collide, (zero, zero))
        b_edge[0] = to_left
        b_edge[1] = to_right

        send(b_edge.at[0], b_near.at[step, 1], 4, step, sec, left)
        send(b_edge.at[1], b_near.at[step, 0], 4, step, sec, right)

        @pl.when(is_owner)
        def _():
            wait_bytes(b_land.at[step], recv_sem.at[3, step])
            member = lax.rem(b_role >> 1, 5)
            along_y = jnp.where(member == 1, 1, jnp.where(member == 2, -1, 0)) * (1 - 2 * is_down)
            start = whole - along_y
            b_slot = ROLES * is_down + b_role

            def slide_ghost(block):
                b_slid[block] = keep * slid_block(b_land, step, block, start) + frac * slid_block(
                    b_land, step, block, start + 1
                )

            slide_ghost(gy)
            pltpu.make_async_copy(
                b_slid.at[gy], b_ghost.at[step, b_slot], recv_sem.at[5, step]
            ).start()

            def send_slid_ghost(k, m):
                block = far_first(gy, k, m)
                slide_ghost(block)
                send(b_slid.at[block], b_ghost.at[step, b_slot], 5, step, sec, block)

            def send_slid_ghosts(k, carry):
                for m in range(8):
                    send_slid_ghost(k, m)
                return carry

            lax.fori_loop(0, 7, send_slid_ghosts, 0)
            for m in range(7):
                send_slid_ghost(7, m)

        wait_bytes(b_near.at[step], recv_sem.at[4, step])
        near_left = b_near[step, 0]
        near_right = b_near[step, 1]

        def stream(z, carry):
            columns = {}
            for shift_z in (-1, 0, 1):
                source = (z - shift_z) & 7
                back = (LY - source) & (LY - 1)
                columns[1, shift_z] = turn(near_left, back)
                columns[-1, shift_z] = turn(near_right, back)
            for which in range(38):
                i = which % 19
                shift_x, shift_y, shift_z = VELOCITY[i]
                tile = post[which, (z - shift_z) & 7]
                if shift_y == 1:
                    k = Y_PLUS.index(i) + (5 if which >= 19 else 0)
                    outer = turn(columns[1, shift_z], (LY - 8 * k) % LY)
                    tile = jnp.where(lane == 0, outer, turn(tile, 1))
                elif shift_y == -1:
                    k = Y_MINUS.index(i) + (5 if which >= 19 else 0)
                    outer = turn(columns[-1, shift_z], (LY - 1 - 8 * k) % LY)
                    tile = jnp.where(lane == LY - 1, outer, turn(tile, LY - 1))
                if shift_x:
                    tile = pltpu.roll(tile, shift_x % LX, 0)
                state[which, z] = tile
            return carry

        lax.fori_loop(0, NZ, stream, 0)

        incoming = ((0, UPWARD, 0), (1, DOWNWARD, LX - 1))

        @pl.when(step < STEPS - 1)
        def _():
            for side, members, x in incoming:
                for i in members:
                    state[19 + i, :, x, :] = jnp.zeros((NZ, LY), jnp.float32)
            order_pass()

        wait_bytes(a_land.at[step], send_sem.at[0])
        wait_bytes(a_edge, send_sem.at[1])
        wait_bytes(a_slid.at[pl.ds(0, 15)], send_sem.at[2])
        wait_bytes(b_send, send_sem.at[3])
        wait_bytes(b_edge, send_sem.at[4])

        @pl.when(is_owner)
        def _():
            wait_bytes(b_slid.at[pl.ds(0, N_GY - 1)], send_sem.at[5])

        wait_bytes(b_ghost.at[step], recv_sem.at[5, step])
        for side, members, x in incoming:
            total = None
            for k in range(10):
                i = members[k % 5]
                rows = b_ghost[step, pl.ds(ROLES * side + 2 * k, 2)].reshape(NZ, LY)
                if VELOCITY[i][2]:
                    rows = pltpu.roll(rows, VELOCITY[i][2] % NZ, 0)
                state[i + (19 if k >= 5 else 0), :, x, :] = rows
                if k >= 5:
                    total = rows if total is None else total + rows
            cut = pl.ds(0, LY)
            field[:, 8 + x, cut] = field[:, 8 + x, cut] + total

        @pl.when(step < STEPS - 1)
        def _():
            pack_order()

        return carry

    lax.fori_loop(0, STEPS, step_body, 0)
    store_fluid = pltpu.make_async_copy(state.at[pl.ds(0, 19)], fluid_out, out_sem.at[0])
    store_order = pltpu.make_async_copy(state.at[pl.ds(19, 19)], order_out, out_sem.at[1])
    store_fluid.start()
    store_order.start()
    store_fluid.wait()
    store_order.wait()


def copy_out(fluid_in, order_in, fluid_out, order_out, held, in_sem, out_sem):
    parts = [(0, 5), (5, 5), (10, 5), (15, 4)]
    loads, stores = [], []
    for start, size in parts:
        for half, src, dst in ((0, fluid_in, fluid_out), (19, order_in, order_out)):
            k = len(loads)
            here = held.at[pl.ds(half + start, size)]
            cut = pl.ds(start, size)
            loads.append(pltpu.make_async_copy(src.at[cut], here, in_sem.at[k]))
            stores.append(pltpu.make_async_copy(here, dst.at[cut], out_sem.at[k]))
    for load in loads:
        load.start()
    for load, store in zip(loads, stores):
        load.wait()
        store.start()
    for store in stores:
        store.wait()


def per_device(fluid_dist, order_dist, plane_offset, plane_speed):
    shape = jax.ShapeDtypeStruct((19, NZ, LX, LY), jnp.float32)

    def scratch(*dims):
        return pltpu.VMEM(dims, jnp.float32)

    hbm = pl.BlockSpec(memory_space=pl.ANY)
    results = pl.pallas_call(
        kernel,
        out_shape=(shape, shape),
        in_specs=[
            pl.BlockSpec(memory_space=pl.ANY),
            pl.BlockSpec(memory_space=pl.ANY),
            pl.BlockSpec(memory_space=pl.ANY),
            pl.BlockSpec(memory_space=pl.ANY),
        ],
        out_specs=(pl.BlockSpec(memory_space=pl.ANY), pl.BlockSpec(memory_space=pl.ANY)),
        scratch_shapes=[
            pltpu.SMEM((STEPS, N_SEC), jnp.int32),
            pltpu.SMEM((N_SEC,), jnp.int32),
            scratch(38, NZ, LX, LY),
            scratch(38, NZ, LX, LY),
            scratch(NZ, 32, 2 * LY),
            scratch(NZ, 32, 2 * LY),
            scratch(4, NZ, LX, LY),
            scratch(NZ, 2, LY),
            scratch(NZ, 2, LY),
            scratch(2, LX, LY),
            scratch(STEPS, N_GY, 2, LY),
            scratch(16, 3, 2, LY),
            scratch(STEPS, 16, 3, 2, LY),
            scratch(STEPS, 2, LX, LY),
            scratch(2, ROLES, 4, LY),
            scratch(2, LX, LY),
            scratch(STEPS, N_GY, 4, LY),
            scratch(N_GY, 4, LY),
            scratch(STEPS, 2 * ROLES, 4, LY),
            scratch(STEPS, 2, LX, LY),
            pltpu.SemaphoreType.DMA((4,)),
            pltpu.SemaphoreType.DMA((2,)),
            pltpu.SemaphoreType.DMA((6,)),
            pltpu.SemaphoreType.DMA((6, STEPS)),
        ],
        compiler_params=pltpu.CompilerParams(
            collective_id=0, has_side_effects=True, vmem_limit_bytes=60 * 1024 * 1024
        ),
    )(fluid_dist, order_dist, plane_offset, plane_speed)
    return pl.pallas_call(
        copy_out,
        out_shape=(shape, shape),
        in_specs=[hbm, hbm],
        out_specs=(hbm, hbm),
        scratch_shapes=[
            scratch(38, NZ, LX, LY),
            pltpu.SemaphoreType.DMA((8,)),
            pltpu.SemaphoreType.DMA((8,)),
        ],
        compiler_params=pltpu.CompilerParams(vmem_limit_bytes=60 * 1024 * 1024),
    )(*results)


def solution(mesh):
    split = P(None, None, "sec", "gy")
    return jax.shard_map(
        per_device,
        mesh=mesh,
        in_specs=(split, split, P(), P()),
        out_specs=(split, split),
        check_vma=False,
    )
```

```python
import jax
import jax.numpy as jnp
from jax import lax
from jax.experimental import pallas as pl
from jax.experimental.pallas import tpu as pltpu
from jax.sharding import PartitionSpec as P

STEPS = 2
VELOCITY = (
    (0, 0, 0),
    (1, 0, 0),
    (-1, 0, 0),
    (0, 1, 0),
    (0, -1, 0),
    (0, 0, 1),
    (0, 0, -1),
    (1, 1, 0),
    (-1, -1, 0),
    (1, -1, 0),
    (-1, 1, 0),
    (1, 0, 1),
    (-1, 0, -1),
    (1, 0, -1),
    (-1, 0, 1),
    (0, 1, 1),
    (0, -1, -1),
    (0, 1, -1),
    (0, -1, 1),
)
WEIGHTS = (1.0 / 3.0,) + (1.0 / 18.0,) * 6 + (1.0 / 36.0,) * 12
UPWARD = (1, 7, 9, 11, 13)
DOWNWARD = (2, 8, 10, 12, 14)
Y_PLUS = (3, 7, 10, 15, 17)
Y_MINUS = (4, 8, 9, 16, 18)
COEF_A = -0.0625
COEF_B = 0.0625
KAPPA_GRAD = 0.04
MOBILITY = 1.0
TAU_FLUID = 0.8
TAU_ORDER = 0.9
NZ = 8
LX = 16
LY = 128
N_SEC = 4
N_GY = 64
SPAN = LY * N_GY * 256
ROLES = 20
GHOSTS = 2 * ROLES
MESH = pl.DeviceIdType.MESH
ACROSS = ((1, 2), (1, 1), (1, 3), (0, 2), (1, 0), (0, 1), (0, 3), (0, 0))


def lanes(shape):
    return lax.broadcasted_iota(jnp.int32, shape, len(shape) - 1)


def turn(value, shift):
    return pltpu.roll(value, shift, value.ndim - 1)


def ring_z(gy, k):
    half = (k + 1) >> 1
    return ((gy >> 2) + 4 + jnp.where((k & 1) == 1, -half, half)) & 7


def far_first(gy, k, m):
    across, along = ACROSS[m]
    return (((gy >> 5) ^ across) << 5) + (ring_z(gy, k) << 2) + ((gy + along) & 3)


def signed_sum(terms, signs):
    total = None
    for term, sign in zip(terms, signs):
        if sign == 0:
            continue
        if total is None:
            total = term if sign > 0 else -term
        else:
            total = total + term if sign > 0 else total - term
    return total


def wait_bytes(ref, sem):
    pltpu.make_async_copy(ref, ref, sem).wait()


def slid_block(load, block, offset):
    offset = offset & (LY * N_GY - 1)
    first = block + (offset >> 7)
    inside = offset & (LY - 1)
    here = load(first & (N_GY - 1))
    beyond = load((first + 1) & (N_GY - 1))
    shift = (LY - inside) & (LY - 1)
    return jnp.where(lanes(here.shape) < LY - inside, turn(here, shift), turn(beyond, shift))


def parts_of(units):
    frac = (units & 255).astype(jnp.float32) * (1.0 / 256.0)
    return units >> 8, 1.0 - frac, frac


def slide(load, block, parts, along_y=0):
    whole, keep, frac = parts
    start = whole + along_y
    return keep * slid_block(load, block, start) + frac * slid_block(load, block, start + 1)


def kernel(
    fluid_in, order_in, offsets_in, speeds_in, fluid_out, order_out, ghosts_out,
    offsets, speeds, state, post, field, pot, mom,
    a_up, a_down, a_edge, a_land, a_slid, a_ghost, a_near,
    b_send, b_part, b_own, b_edge, b_land_0, b_land_1, b_back, b_full, b_line, b_turned, b_slid, b_ghost, b_near,
    in_sem, out_sem, send_sem, recv_sem,
):
    b_lands = (b_land_0, b_land_1)
    sec = lax.axis_index("sec")
    gy = lax.axis_index("gy")
    above = (sec + 1) & (N_SEC - 1)
    below = (sec + N_SEC - 1) & (N_SEC - 1)
    left = (gy + N_GY - 1) & (N_GY - 1)
    right = (gy + 1) & (N_GY - 1)
    is_down = gy & 1
    owner = gy >> 1
    a_z = owner & 7
    a_part = owner >> 3
    place = owner & 3
    b_role = 8 * place + (owner >> 2)
    is_owner = b_role < ROLES
    is_phi = place == 3
    phi_z = owner >> 2

    load_order = pltpu.make_async_copy(order_in, state.at[pl.ds(19, 19)], in_sem.at[0])
    load_order.start()
    load_offsets = pltpu.make_async_copy(offsets_in, offsets, in_sem.at[2])
    load_offsets.start()
    load_speeds = pltpu.make_async_copy(speeds_in, speeds, in_sem.at[3])
    load_speeds.start()
    load_fluid = pltpu.make_async_copy(fluid_in, state.at[pl.ds(0, 19)], in_sem.at[1])
    load_fluid.start()

    barrier = pltpu.get_barrier_semaphore()
    source_sec = jnp.where(is_down == 0, below, above)

    def greet(k, carry):
        for m in range(8):
            other = far_first(gy, k, m)
            pl.semaphore_signal(
                barrier, inc=1, device_id=(source_sec, other), device_id_type=MESH
            )
            if m < 7:
                pl.semaphore_signal(barrier, inc=1, device_id=(sec, other), device_id_type=MESH)
        return carry

    def greet_rest(k, carry):
        pl.semaphore_signal(
            barrier, inc=1, device_id=(sec, far_first(gy, k, 7)), device_id_type=MESH
        )
        return carry

    lax.fori_loop(0, 8, greet, 0)
    lax.fori_loop(0, 7, greet_rest, 0)

    plane = (LX, LY)
    lane = lanes(plane)
    field[...] = jnp.zeros_like(field)

    def order_pass():
        def one(z, carry):
            phi = state[19, z]
            for i in range(1, 19):
                phi = phi + state[19 + i, z]
            field[z, pl.ds(8, LX), pl.ds(0, LY)] = phi
            return carry

        lax.fori_loop(0, NZ, one, 0)

    def pack_faces():
        for j in range(2):
            a_up[:, j, :] = field[:, 8 + LX - 2 + j, pl.ds(0, LY)]
            a_down[:, j, :] = field[:, 8 + j, pl.ds(0, LY)]

    def pack_columns():
        to_left = jnp.zeros(plane, jnp.float32)
        to_right = to_left
        for z in range(NZ):
            phi = field[z, pl.ds(8, LX), pl.ds(0, LY)]
            mine = (lane >> 1) == z
            to_left = jnp.where(mine, turn(phi, 2 * z), to_left)
            to_right = jnp.where(mine, turn(phi, 2 * z + 2), to_right)
        a_edge[0] = to_left
        a_edge[1] = to_right

    def next_y(near, far):
        tile = lanes(near.shape)
        return jnp.where(tile == LY - 1, turn(far, LY - 1), turn(near, LY - 1))

    def last_y(near, far):
        tile = lanes(near.shape)
        return jnp.where(tile == 0, turn(far, 1), turn(near, 1))

    def face_potential(x, half):
        cut = pl.ds(half * LY, LY)
        tile = field[:, 8 + x, cut]
        other = field[:, 8 + x, pl.ds((1 - half) * LY, LY)]
        lap = (
            field[:, 9 + x, cut]
            + field[:, 7 + x, cut]
            + next_y(tile, other)
            + last_y(tile, other)
            + pltpu.roll(tile, 1, 0)
            + pltpu.roll(tile, NZ - 1, 0)
            - 6.0 * tile
        )
        return tile * (COEF_A + COEF_B * tile * tile) - KAPPA_GRAD * lap

    left_f = 1.0 - 1.0 / TAU_FLUID
    left_g = 1.0 - 1.0 / TAU_ORDER
    kick = 1.0 - 0.5 / TAU_FLUID
    rim = lanes((NZ, LY))

    def face_layer(x, potential):
        phi = field[:, 8 + x, pl.ds(0, LY)]
        middle = potential(x, 0)
        beyond = potential(x, 1)
        half = -0.5 * phi
        force = (
            half * (potential(x + 1, 0) - potential(x - 1, 0)),
            half * (next_y(middle, beyond) - last_y(middle, beyond)),
            half * (pltpu.roll(middle, NZ - 1, 0) - pltpu.roll(middle, 1, 0)),
        )
        density = mom[0, :, x, :]
        inverse = 1.0 / density
        vel = tuple((mom[1 + k, :, x, :] + 0.5 * force[k]) * inverse for k in range(3))
        square = vel[0] * vel[0] + vel[1] * vel[1] + vel[2] * vel[2]
        square_phi = phi * (1.0 / TAU_ORDER)
        base_phi = (3.0 * MOBILITY / TAU_ORDER) * middle - 1.5 * square_phi * square
        return phi, middle, force, density, vel, square, square_phi, base_phi

    def face_order(x, i, layer):
        _, middle, _, _, vel, square, square_phi, base_phi = layer
        kept = left_g * state[19 + i, :, x, :]
        if i == 0:
            return kept + (
                square_phi * (1.0 - 0.5 * square) - (2.0 * MOBILITY / TAU_ORDER) * middle
            )
        along = signed_sum(vel, VELOCITY[i])
        carried = square_phi * along
        return kept + WEIGHTS[i] * (base_phi + 4.5 * carried * along + 3.0 * carried)

    def streamed_sum(terms):
        groups = {0: None, 1: None, -1: None}
        for i, tile in terms:
            _, shift_y, shift_z = VELOCITY[i]
            if shift_z:
                tile = pltpu.roll(tile, shift_z % NZ, 0)
            held = groups[shift_y]
            groups[shift_y] = tile if held is None else held + tile
        total = (
            groups[0]
            + jnp.where(rim == 0, 0.0, turn(groups[1], 1))
            + jnp.where(rim == LY - 1, 0.0, turn(groups[-1], LY - 1))
        )
        return total, groups[1], groups[-1]

    def crossing(sums):
        result = jnp.zeros((NZ, LY), jnp.float32)
        for j, (_, forward, back) in enumerate(sums):
            result = jnp.where(rim == j, turn(forward, 1 + j), result)
            result = jnp.where(rim == LY - 1 - j, turn(back, LY - 1 - j), result)
        return result

    def face_collide(side, jump):
        members, others, x, inward = ((UPWARD, DOWNWARD, LX - 1, -1), (DOWNWARD, UPWARD, 0, 1))[side]
        made = {}

        def potential(layer_x, half):
            if (layer_x, half) not in made:
                made[layer_x, half] = face_potential(layer_x, half)
            return made[layer_x, half]

        layer = face_layer(x, potential)
        phi, middle, force, density, vel, square, square_phi, base_phi = layer
        drift = vel[0] * force[0] + vel[1] * force[1] + vel[2] * force[2]
        scaled = density * (1.0 / TAU_FLUID)
        base = scaled * (1.0 - 1.5 * square) - (3.0 * kick) * drift
        moved = vel[1] + jump
        change_square = 1.5 * (moved * moved - vel[1] * vel[1])
        leaving = []
        for k, i in enumerate(members):
            vector = VELOCITY[i]
            weight = WEIGHTS[i]
            along = signed_sum(vel, vector)
            pushed = signed_sum(force, vector)
            after = signed_sum((vel[0], moved, vel[2]), vector)
            change = weight * (
                3.0 * (after - along) + 4.5 * (after * after - along * along) - change_square
            )
            fluid = left_f * state[i, :, x, :] + weight * (
                base
                + along * (4.5 * scaled * along + (9.0 * kick) * pushed)
                + (3.0 * scaled * along + (3.0 * kick) * pushed)
            )
            order = face_order(x, i, layer) + phi * change
            leaving.append((i, order))
            for lift, value in ((0, fluid + density * change), (5, order)):
                b_send[side, 2 * (k + lift)] = value[:4]
                b_send[side, 2 * (k + lift) + 1] = value[4:]

        def make_parts():
            second = x + inward
            third = second + inward
            layers = {x: layer}
            for layer_x in (second, third):
                layers[layer_x] = face_layer(layer_x, potential)
            still = [i for i in range(19) if VELOCITY[i][0] == 0]

            def terms(layer_x, rows):
                return [(i, face_order(layer_x, i, layers[layer_x])) for i in rows]

            sums = [
                streamed_sum(terms(x, still) + terms(second, members)),
                streamed_sum(terms(second, still) + terms(third, members) + terms(x, others)),
                streamed_sum(leaving),
            ]
            for j in range(3):
                b_part[side, :, j, :] = sums[j][0]
            b_part[side, :, 3, :] = crossing(sums)
            b_own[side, :, 0, :] = sums[2][0]
            b_own[side, :, 1, :] = crossing(sums[2:])

        return make_parts

    def send(src, dst, which, slot, to_sec, to_gy):
        pltpu.make_async_remote_copy(
            src_ref=src,
            dst_ref=dst,
            send_sem=send_sem.at[which],
            recv_sem=recv_sem.at[which, slot],
            device_id=(to_sec, to_gy),
            device_id_type=MESH,
        ).start()

    load_order.wait()
    order_pass()
    pack_faces()
    pack_columns()
    load_offsets.wait()
    load_speeds.wait()
    pl.semaphore_wait(barrier, 2 * N_GY - 1)

    own = pl.ds(0, LY)
    halo = pl.ds(LY, LY)
    incoming = ((0, UPWARD, 0), (1, DOWNWARD, LX - 1))
    outside = ((0, -1, -2), (1, LX, LX + 1))

    def units_of(step):
        return jnp.where(
            is_down == 0, offsets[step, sec], (SPAN - offsets[step, above]) & (SPAN - 1)
        )

    def send_columns(step):
        send(a_edge.at[0], a_near.at[step, 1], 1, step, sec, left)
        send(a_edge.at[1], a_near.at[step, 0], 1, step, sec, right)

    def put_columns(step):
        wait_bytes(a_near.at[step], recv_sem.at[1, step])
        from_left = a_near[step, 0]
        from_right = a_near[step, 1]

        def one(z, carry):
            field[z, pl.ds(8, LX), halo] = jnp.where(
                lane < 2,
                turn(from_right, (LY - 2 * z) & (LY - 1)),
                jnp.where(lane >= LY - 2, turn(from_left, (LY - 2 - 2 * z) & (LY - 1)), 0.0),
            )
            return carry

        lax.fori_loop(0, NZ, one, 0)

    def moments():
        def one(z, carry):
            tiles = [state[i, z] for i in range(19)]
            mom[0, z] = signed_sum(tiles, (1,) * 19)
            for axis in range(3):
                mom[1 + axis, z] = signed_sum(tiles, [vector[axis] for vector in VELOCITY])
            return carry

        lax.fori_loop(0, NZ, one, 0)

    def exchange_order():
        def send_order(k, carry):
            for across, along in ((1, 1), (1, 0), (0, 1), (0, 0)):
                target = (
                    (((gy >> 5) ^ across) << 5) + (ring_z(gy, k) << 2) + ((gy & 2) ^ (2 * along))
                )
                z = (target >> 1) & 7
                send(a_up.at[z], a_land.at[gy], 0, 0, above, target)
                send(a_down.at[z], a_land.at[gy], 0, 0, below, target + 1)
            return carry

        lax.fori_loop(0, 8, send_order, 0, unroll=2)
        send_columns(0)
        load_fluid.wait()
        moments()
        parts = parts_of(units_of(0))
        whole, keep, frac = parts
        wait_bytes(a_land, recv_sem.at[0, 0])

        def slide_order(block):
            values = [
                slid_block(lambda i: a_land[i], block, whole + shift) for shift in (-1, 0, 1, 2)
            ]
            for k in range(3):
                a_slid[block & 15, k] = keep * values[k] + frac * values[k + 1]

        a_role = 8 * is_down + a_z
        slide_order(gy)
        pltpu.make_async_copy(
            a_slid.at[gy & 15], a_ghost.at[a_role], recv_sem.at[2, 0]
        ).start()

        def send_slid_order(j, carry):
            block = gy ^ (16 - j)
            slide_order(block)
            send(a_slid.at[block & 15], a_ghost.at[a_role], 2, 0, sec, block)
            return carry

        lax.fori_loop(1, 16, send_slid_order, 0, unroll=5)
        put_columns(0)
        wait_bytes(a_ghost, recv_sem.at[2, 0])
        for side, near_x, far_x in outside:
            roles = pl.ds(8 * side, 8)
            first = 1 - side
            field[:, 8 + near_x, own] = a_ghost[roles, 1, first, :]
            field[:, 8 + far_x, own] = a_ghost[roles, 1, 1 - first, :]
            field[:, 8 + near_x, halo] = jnp.where(
                rim == 0,
                turn(a_ghost[roles, 2, first, :], 1),
                jnp.where(rim == LY - 1, turn(a_ghost[roles, 0, first, :], LY - 1), 0.0),
            )
        wait_bytes(a_land, send_sem.at[0])
        wait_bytes(a_slid.at[pl.ds(0, 15)], send_sem.at[2])

    def potentials(z, carry):
        tall = lanes((32, LY))
        tiles = [field[z, :, own], field[z, :, halo]]
        ahead = [turn(tile, LY - 1) for tile in tiles]
        behind = [turn(tile, 1) for tile in tiles]
        for k in range(2):
            tile = tiles[k]
            cut = pl.ds(k * LY, LY)
            lap = (
                pltpu.roll(tile, 1, 0)
                + pltpu.roll(tile, 31, 0)
                + jnp.where(tall == LY - 1, ahead[1 - k], ahead[k])
                + jnp.where(tall == 0, behind[1 - k], behind[k])
                + field[(z + 1) & 7, :, cut]
                + field[(z + 7) & 7, :, cut]
                - 6.0 * tile
            )
            pot[z, :, cut] = tile * (COEF_A + COEF_B * tile * tile) - KAPPA_GRAD * lap
        return carry

    def collide(z, carry):
        to_left, to_right = carry
        rows = pl.ds(8, LX)
        inner = pot[z, rows, own]
        beyond = pot[z, rows, halo]
        phi = field[z, rows, own]
        half = -0.5 * phi
        force = (
            half * (pot[z, pl.ds(9, LX), own] - pot[z, pl.ds(7, LX), own]),
            half * (next_y(inner, beyond) - last_y(inner, beyond)),
            half * (pot[(z + 1) & 7, rows, own] - pot[(z + 7) & 7, rows, own]),
        )
        density = mom[0, z]
        inverse = 1.0 / density
        vel = tuple((mom[1 + k, z] + 0.5 * force[k]) * inverse for k in range(3))
        square = vel[0] * vel[0] + vel[1] * vel[1] + vel[2] * vel[2]
        drift = vel[0] * force[0] + vel[1] * force[1] + vel[2] * force[2]
        scaled = density * (1.0 / TAU_FLUID)
        base = scaled * (1.0 - 1.5 * square) - (3.0 * kick) * drift
        square_phi = phi * (1.0 / TAU_ORDER)
        base_phi = (3.0 * MOBILITY / TAU_ORDER) * inner - 1.5 * square_phi * square
        fluid = [None] * 19
        order = [None] * 19
        fluid[0] = left_f * state[0, z] + WEIGHTS[0] * base
        order[0] = left_g * state[19, z] + (
            square_phi * (1.0 - 0.5 * square) - (2.0 * MOBILITY / TAU_ORDER) * inner
        )
        for i in range(1, 19, 2):
            vector = VELOCITY[i]
            along = signed_sum(vel, vector)
            pushed = signed_sum(force, vector)
            weight = WEIGHTS[i]
            even = weight * (base + along * (4.5 * scaled * along + (9.0 * kick) * pushed))
            odd = weight * (3.0 * scaled * along + (3.0 * kick) * pushed)
            fluid[i] = left_f * state[i, z] + (even + odd)
            fluid[i + 1] = left_f * state[i + 1, z] + (even - odd)
            carried = square_phi * along
            even = weight * (base_phi + 4.5 * carried * along)
            odd = (3.0 * weight) * carried
            order[i] = left_g * state[19 + i, z] + (even + odd)
            order[i + 1] = left_g * state[20 + i, z] + (even - odd)
        for i in range(19):
            post[i, z] = fluid[i]
            post[19 + i, z] = order[i]
        going_left = jnp.zeros(plane, jnp.float32)
        going_right = jnp.zeros(plane, jnp.float32)
        for k in range(10):
            part = fluid if k < 5 else order
            going_right = jnp.where(
                lane == 8 * k, turn(part[Y_PLUS[k % 5]], 8 * k + 1), going_right
            )
            going_left = jnp.where(lane == 8 * k, turn(part[Y_MINUS[k % 5]], 8 * k), going_left)
        mine = (lane & 7) == z
        to_left = jnp.where(mine, turn(going_left, z), to_left)
        to_right = jnp.where(mine, turn(going_right, z), to_right)
        return to_left, to_right

    def pass_ghosts(step):
        member = lax.rem(b_role >> 1, 5)
        along_y = jnp.where(member == 1, -1, jnp.where(member == 2, 1, 0)) * (1 - 2 * is_down)
        parts = parts_of(units_of(step))
        slot = ROLES * is_down + b_role
        wait_bytes(b_lands[step], recv_sem.at[3, step])

        def make(block):
            b_slid[block] = slide(lambda i: b_lands[step][i], block, parts, along_y)

        pass_on(step, slot, make)

    def pass_on(step, slot, make):
        make(gy)
        pltpu.make_async_copy(
            b_slid.at[gy], b_ghost.at[step, slot], recv_sem.at[5, step]
        ).start()

        def one(k, m):
            block = far_first(gy, k, m)
            make(block)
            send(b_slid.at[block], b_ghost.at[step, slot], 5, step, sec, block)

        def several(k, carry):
            for m in range(8):
                one(k, m)
            return carry

        lax.fori_loop(0, 7, several, 0)
        for m in range(7):
            one(7, m)

    def pass_order(step):
        units = units_of(step)
        parts = parts_of(units)
        parts_back = parts_of((SPAN - units) & (SPAN - 1))
        parts_next = parts_of(units_of(step + 1))
        wait_bytes(b_lands[step], recv_sem.at[6, step])
        wait_bytes(b_back, recv_sem.at[7, step])
        four = lanes((4, LY))
        which = lax.broadcasted_iota(jnp.int32, (4, LY), 0)
        line = lanes((1, LY))

        def complete(block, carry):
            before = (block + N_GY - 1) & (N_GY - 1)
            after = (block + 1) & (N_GY - 1)
            forward = jnp.broadcast_to(b_lands[step][before, pl.ds(3, 1), :], (4, LY))
            back = jnp.broadcast_to(b_lands[step][after, pl.ds(3, 1), :], (4, LY))
            for j in (1, 2):
                forward = jnp.where(which == j, turn(forward, LY - j), forward)
                back = jnp.where(which == j, turn(back, j), back)
            b_full[block] = (
                b_lands[step][block]
                + jnp.where(four == 0, forward, 0.0)
                + jnp.where(four == LY - 1, back, 0.0)
            )
            b_line[block] = (
                b_back[block, pl.ds(0, 1), :]
                + jnp.where(line == 0, b_back[before, pl.ds(1, 1), :], 0.0)
                + jnp.where(line == LY - 1, b_back[after, pl.ds(1, 1), :], 0.0)
            )
            return carry

        lax.fori_loop(0, N_GY, complete, 0, unroll=4)

        def add_own(block, carry):
            b_full[block, pl.ds(0, 1), :] = b_full[block, pl.ds(0, 1), :] + slide(
                lambda i: b_line[i], block, parts_back
            )
            return carry

        lax.fori_loop(0, N_GY, add_own, 0, unroll=4)

        def turn_all(block, carry):
            ahead = slide(lambda i: b_full[i], block, parts_next)
            now = slide(lambda i: b_full[i], block, parts)
            b_turned[block] = jnp.where(which == 2, now, ahead)
            return carry

        lax.fori_loop(0, N_GY, turn_all, 0, unroll=4)

        def make(block):
            before = (block + N_GY - 1) & (N_GY - 1)
            after = (block + 1) & (N_GY - 1)
            b_slid[block, pl.ds(0, 2), :] = b_turned[block, pl.ds(0, 2), :]
            b_slid[block, pl.ds(2, 1), :] = jnp.where(
                line == 0,
                b_turned[after, pl.ds(0, 1), :],
                jnp.where(line == LY - 1, b_turned[before, pl.ds(0, 1), :], 0.0),
            )
            b_slid[block, pl.ds(3, 1), :] = jnp.where(
                line < 2,
                b_turned[after, pl.ds(2, 1), :],
                jnp.where(line >= LY - 2, b_turned[before, pl.ds(2, 1), :], 0.0),
            )

        pass_on(step, GHOSTS + 8 * is_down + phi_z, make)

    def stream(z, carry):
        near_left, near_right = carry
        columns = {}
        for shift_z in (-1, 0, 1):
            source = (z - shift_z) & 7
            back = (LY - source) & (LY - 1)
            columns[1, shift_z] = turn(near_left, back)
            columns[-1, shift_z] = turn(near_right, back)
        for which in range(38):
            i = which % 19
            shift_x, shift_y, shift_z = VELOCITY[i]
            tile = post[which, (z - shift_z) & 7]
            if shift_y == 1:
                k = Y_PLUS.index(i) + (5 if which >= 19 else 0)
                outer = turn(columns[1, shift_z], (LY - 8 * k) % LY)
                tile = jnp.where(lane == 0, outer, turn(tile, 1))
            elif shift_y == -1:
                k = Y_MINUS.index(i) + (5 if which >= 19 else 0)
                outer = turn(columns[-1, shift_z], (LY - 1 - 8 * k) % LY)
                tile = jnp.where(lane == LY - 1, outer, turn(tile, LY - 1))
            if shift_x:
                tile = pltpu.roll(tile, shift_x % LX, 0)
            state[which, z] = tile
        return carry

    def take_ghosts(step):
        for side, members, x in incoming:
            order_sum = None
            tiles = []
            for k in range(10):
                i = members[k % 5]
                rows = b_ghost[step, pl.ds(ROLES * side + 2 * k, 2)].reshape(NZ, LY)
                if VELOCITY[i][2]:
                    rows = pltpu.roll(rows, VELOCITY[i][2] % NZ, 0)
                state[i + (19 if k >= 5 else 0), :, x, :] = rows
                if k >= 5:
                    order_sum = rows if order_sum is None else order_sum + rows
                else:
                    tiles.append(rows)
            field[:, 8 + x, own] = field[:, 8 + x, own] + order_sum
            mom[0, :, x, :] = mom[0, :, x, :] + signed_sum(tiles, (1,) * 5)
            for axis in range(3):
                mom[1 + axis, :, x, :] = mom[1 + axis, :, x, :] + signed_sum(
                    tiles, [VELOCITY[i][axis] for i in members]
                )
        for side, near_x, far_x in outside:
            roles = pl.ds(GHOSTS + 8 * side, 8)
            x = 0 if side == 0 else LX - 1
            field[:, 8 + near_x, own] = b_ghost[step, roles, 0, :]
            field[:, 8 + far_x, own] = b_ghost[step, roles, 1, :]
            field[:, 8 + near_x, halo] = b_ghost[step, roles, 2, :]
            field[:, 8 + x, halo] = field[:, 8 + x, halo] + b_ghost[step, roles, 3, :]

    def send_ghosts(step):
        def one(j, carry):
            role = lax.rem(j + gy, ROLES)
            target = 2 * (4 * (role & 7) + (role >> 3))
            send(b_send.at[0, role], b_lands[step].at[gy], 3, step, above, target)
            send(b_send.at[1, role], b_lands[step].at[gy], 3, step, below, target + 1)
            return carry

        lax.fori_loop(0, ROLES, one, 0, unroll=5)

    def send_parts(step):
        def one(j, carry):
            z = (j + (gy >> 3)) & 7
            target = 8 * z + 6
            send(b_part.at[0, z], b_lands[step].at[gy], 6, step, above, target)
            send(b_part.at[1, z], b_lands[step].at[gy], 6, step, below, target + 1)
            for side in (0, 1):
                to = target + 1 - side

                @pl.when(to != gy)
                def _():
                    send(b_own.at[side, z], b_back.at[gy], 7, step, sec, to)

            return carry

        lax.fori_loop(0, 8, one, 0)

        @pl.when(is_phi)
        def _():
            pltpu.make_async_copy(
                b_own.at[1 - is_down, phi_z], b_back.at[gy], recv_sem.at[7, step]
            ).start()

    exchange_order()
    for step in range(STEPS):
        last = step == STEPS - 1
        jump_up = speeds[above].astype(jnp.float32) * (-1.0 / 256.0)
        jump_down = speeds[sec].astype(jnp.float32) * (1.0 / 256.0)
        make_parts = [face_collide(0, jump_up), face_collide(1, jump_down)]
        send_ghosts(step)
        if not last:
            for make in make_parts:
                make()
            send_parts(step)

        lax.fori_loop(0, NZ, potentials, 0)
        zero = jnp.zeros(plane, jnp.float32)
        to_left, to_right = lax.fori_loop(0, NZ, collide, (zero, zero))
        b_edge[0] = to_left
        b_edge[1] = to_right
        send(b_edge.at[0], b_near.at[step, 1], 4, step, sec, left)
        send(b_edge.at[1], b_near.at[step, 0], 4, step, sec, right)

        if step > 0:
            @pl.when(jnp.logical_or(is_owner, is_phi))
            def _():
                wait_bytes(b_slid.at[pl.ds(0, N_GY - 1)], send_sem.at[5])

        @pl.when(is_owner)
        def _():
            pass_ghosts(step)

        if not last:

            @pl.when(is_phi)
            def _():
                pass_order(step)

        wait_bytes(b_near.at[step], recv_sem.at[4, step])
        lax.fori_loop(0, NZ, stream, (b_near[step, 0], b_near[step, 1]))
        wait_bytes(a_edge, send_sem.at[1])
        if last:
            store_fluid = pltpu.make_async_copy(state.at[pl.ds(0, 19)], fluid_out, out_sem.at[0])
            store_order = pltpu.make_async_copy(state.at[pl.ds(19, 19)], order_out, out_sem.at[1])
            store_fluid.start()
            store_order.start()
        else:
            for side, members, x in incoming:
                for i in members:
                    state[i, :, x, :] = jnp.zeros((NZ, LY), jnp.float32)
                    state[19 + i, :, x, :] = jnp.zeros((NZ, LY), jnp.float32)
            order_pass()
            pack_columns()
            send_columns(step + 1)
            moments()
            put_columns(step + 1)

        wait_bytes(b_send, send_sem.at[3])
        wait_bytes(b_edge, send_sem.at[4])
        if last:
            wait_bytes(b_ghost.at[step, pl.ds(0, GHOSTS)], recv_sem.at[5, step])
            store_ghosts = pltpu.make_async_copy(
                b_ghost.at[step, pl.ds(0, GHOSTS)], ghosts_out, out_sem.at[2]
            )
            store_ghosts.start()

            @pl.when(is_owner)
            def _():
                wait_bytes(b_slid.at[pl.ds(0, N_GY - 1)], send_sem.at[5])

            store_fluid.wait()
            store_order.wait()
            store_ghosts.wait()
        else:
            wait_bytes(b_part, send_sem.at[6])
            wait_bytes(b_ghost.at[step], recv_sem.at[5, step])
            take_ghosts(step)

            @pl.when(is_phi)
            def _():
                wait_bytes(b_own.at[:, pl.ds(0, 7)], send_sem.at[7])
                wait_bytes(b_own.at[0, 0], send_sem.at[7])

            @pl.when(jnp.logical_not(is_phi))
            def _():
                wait_bytes(b_own, send_sem.at[7])


def finish(
    fluid_in, order_in, ghosts_in, fluid_out, order_out, held, ghosts, in_sem, out_sem, ghost_sem
):
    load_ghosts = pltpu.make_async_copy(ghosts_in, ghosts, ghost_sem)
    load_ghosts.start()
    loads, stores, firsts = [], [], []
    for start, size in ((0, 5), (5, 5), (10, 5), (15, 4)):
        for half, src, dst in ((0, fluid_in, fluid_out), (19, order_in, order_out)):
            k = len(loads)
            here = held.at[pl.ds(half + start, size)]
            cut = pl.ds(start, size)
            loads.append(pltpu.make_async_copy(src.at[cut], here, in_sem.at[k]))
            stores.append(pltpu.make_async_copy(here, dst.at[cut], out_sem.at[k]))
            firsts.append((half + start, size))
    for load in loads:
        load.start()
    load_ghosts.wait()
    for load, store, (first, size) in zip(loads, stores, firsts):
        load.wait()
        for side, members, x in ((0, UPWARD, 0), (1, DOWNWARD, LX - 1)):
            for k in range(10):
                i = members[k % 5]
                which = i + (19 if k >= 5 else 0)
                if first <= which < first + size:
                    rows = ghosts[pl.ds(ROLES * side + 2 * k, 2)].reshape(NZ, LY)
                    if VELOCITY[i][2]:
                        rows = pltpu.roll(rows, VELOCITY[i][2] % NZ, 0)
                    held[which, :, x, :] = rows
        store.start()
    for store in stores:
        store.wait()


def per_device(fluid_dist, order_dist, plane_offset, plane_speed):
    shape = jax.ShapeDtypeStruct((19, NZ, LX, LY), jnp.float32)
    ghosts = jax.ShapeDtypeStruct((GHOSTS, 4, LY), jnp.float32)
    hbm = pl.BlockSpec(memory_space=pl.ANY)
    dma = pltpu.SemaphoreType.DMA

    def scratch(*dims):
        return pltpu.VMEM(dims, jnp.float32)

    results = pl.pallas_call(
        kernel,
        out_shape=(shape, shape, ghosts),
        in_specs=[hbm] * 4,
        out_specs=(hbm, hbm, hbm),
        scratch_shapes=[
            pltpu.SMEM((STEPS, N_SEC), jnp.int32),
            pltpu.SMEM((N_SEC,), jnp.int32),
            scratch(38, NZ, LX, LY),
            scratch(38, NZ, LX, LY),
            scratch(NZ, 32, 2 * LY),
            scratch(NZ, 32, 2 * LY),
            scratch(4, NZ, LX, LY),
            scratch(NZ, 2, LY),
            scratch(NZ, 2, LY),
            scratch(2, LX, LY),
            scratch(N_GY, 2, LY),
            scratch(16, 3, 2, LY),
            scratch(16, 3, 2, LY),
            scratch(STEPS, 2, LX, LY),
            scratch(2, ROLES, 4, LY),
            scratch(2, NZ, 4, LY),
            scratch(2, NZ, 2, LY),
            scratch(2, LX, LY),
            scratch(N_GY, 4, LY),
            scratch(N_GY, 4, LY),
            scratch(N_GY, 2, LY),
            scratch(N_GY, 4, LY),
            scratch(N_GY, 1, LY),
            scratch(N_GY, 4, LY),
            scratch(N_GY, 4, LY),
            scratch(STEPS, GHOSTS + 16, 4, LY),
            scratch(STEPS, 2, LX, LY),
            dma((4,)),
            dma((3,)),
            dma((8,)),
            dma((8, STEPS)),
        ],
        compiler_params=pltpu.CompilerParams(
            collective_id=0, has_side_effects=True, vmem_limit_bytes=60 * 1024 * 1024
        ),
    )(fluid_dist, order_dist, plane_offset, plane_speed)
    return pl.pallas_call(
        finish,
        out_shape=(shape, shape),
        in_specs=[hbm] * 3,
        out_specs=(hbm, hbm),
        scratch_shapes=[
            scratch(38, NZ, LX, LY),
            scratch(GHOSTS, 4, LY),
            dma((8,)),
            dma((8,)),
            dma,
        ],
        compiler_params=pltpu.CompilerParams(vmem_limit_bytes=60 * 1024 * 1024),
    )(*results)


def solution(mesh):
    split = P(None, None, "sec", "gy")
    return jax.shard_map(
        per_device,
        mesh=mesh,
        in_specs=(split, split, P(), P()),
        out_specs=(split, split),
        check_vma=False,
    )
```

```python
import jax
import jax.numpy as jnp
from jax import lax
from jax.experimental import pallas as pl
from jax.experimental.pallas import tpu as pltpu
from jax.sharding import PartitionSpec as P

STEPS = 2
VELOCITY = (
    (0, 0, 0),
    (1, 0, 0),
    (-1, 0, 0),
    (0, 1, 0),
    (0, -1, 0),
    (0, 0, 1),
    (0, 0, -1),
    (1, 1, 0),
    (-1, -1, 0),
    (1, -1, 0),
    (-1, 1, 0),
    (1, 0, 1),
    (-1, 0, -1),
    (1, 0, -1),
    (-1, 0, 1),
    (0, 1, 1),
    (0, -1, -1),
    (0, 1, -1),
    (0, -1, 1),
)
WEIGHTS = (1.0 / 3.0,) + (1.0 / 18.0,) * 6 + (1.0 / 36.0,) * 12
UPWARD = (1, 7, 9, 11, 13)
DOWNWARD = (2, 8, 10, 12, 14)
Y_PLUS = (3, 7, 10, 15, 17)
Y_MINUS = (4, 8, 9, 16, 18)
COEF_A = -0.0625
COEF_B = 0.0625
KAPPA_GRAD = 0.04
MOBILITY = 1.0
TAU_FLUID = 0.8
TAU_ORDER = 0.9
NZ = 8
LX = 16
LY = 128
N_SEC = 4
N_GY = 64
SPAN = LY * N_GY * 256
ROLES = 20
GHOSTS = 2 * ROLES
MESH = pl.DeviceIdType.MESH
FAR_GROUPS = (6, 5, 7, 2, 4, 1, 3, 0)
ACROSS = ((1, 2), (1, 1), (1, 3), (0, 2), (1, 0), (0, 1), (0, 3), (0, 0))


def lanes(shape):
    return lax.broadcasted_iota(jnp.int32, shape, len(shape) - 1)


def turn(value, shift):
    return pltpu.roll(value, shift, value.ndim - 1)


def ring_z(gy, k):
    half = (k + 1) >> 1
    return ((gy >> 2) + 4 + jnp.where((k & 1) == 1, -half, half)) & 7


def far_first(gy, k, m):
    across, along = ACROSS[m]
    return (((gy >> 5) ^ across) << 5) + (ring_z(gy, k) << 2) + ((gy + along) & 3)


def signed_sum(terms, signs):
    total = None
    for term, sign in zip(terms, signs):
        if sign == 0:
            continue
        if total is None:
            total = term if sign > 0 else -term
        else:
            total = total + term if sign > 0 else total - term
    return total


def wait_bytes(ref, sem):
    pltpu.make_async_copy(ref, ref, sem).wait()


def parts_of(units):
    frac = (units & 255).astype(jnp.float32) * (1.0 / 256.0)
    return units >> 8, 1.0 - frac, frac


def rows_after(value):
    return pltpu.roll(value, N_GY - 1, 0)


def rows_before(value):
    return pltpu.roll(value, 1, 0)


def slide(value, parts, along_y=0):
    whole, keep, frac = parts
    whole = (whole + along_y) & (LY * N_GY - 1)
    inside = whole & (LY - 1)
    tile = lanes(value.shape)
    first = turn(value, LY - 1)
    value = keep * value + frac * jnp.where(tile == LY - 1, rows_after(first), first)
    value = turn(value, (LY - inside) & (LY - 1))
    value = jnp.where(tile < LY - inside, value, rows_after(value))
    return pltpu.roll(value, (N_GY - (whole >> 7)) & (N_GY - 1), 0)


def rim_of(value, width):
    tile = lanes(value.shape)
    return jnp.where(
        tile < width,
        rows_after(value),
        jnp.where(tile >= LY - width, rows_before(value), 0.0),
    )


def kernel(
    fluid_in, order_in, offsets_in, speeds_in, fluid_out, order_out, ghosts_out,
    offsets, speeds, state, post, field, pot, mom,
    a_up, a_down, a_edge, a_land, a_slid, a_ghost, a_near,
    b_send, b_part, b_own, b_edge, b_land_0, b_land_1, b_back, b_slid, b_ghost, b_near,
    in_sem, out_sem, send_sem, recv_sem,
):
    b_lands = (b_land_0, b_land_1)
    sec = lax.axis_index("sec")
    gy = lax.axis_index("gy")
    above = (sec + 1) & (N_SEC - 1)
    below = (sec + N_SEC - 1) & (N_SEC - 1)
    left = (gy + N_GY - 1) & (N_GY - 1)
    right = (gy + 1) & (N_GY - 1)
    is_down = gy & 1
    owner = gy >> 1
    a_z = owner & 7
    a_part = owner >> 3
    place = owner & 3
    group = owner >> 2
    b_role = jnp.where(place == 2, 16 + (group >> 1), 8 * place + group)
    is_owner = jnp.logical_or(place < 2, jnp.logical_and(place == 2, (group & 1) == 0))
    is_phi = place == 3

    load_order = pltpu.make_async_copy(order_in, state.at[pl.ds(19, 19)], in_sem.at[0])
    load_order.start()
    load_offsets = pltpu.make_async_copy(offsets_in, offsets, in_sem.at[2])
    load_offsets.start()
    load_speeds = pltpu.make_async_copy(speeds_in, speeds, in_sem.at[3])
    load_speeds.start()
    load_fluid = pltpu.make_async_copy(fluid_in, state.at[pl.ds(0, 19)], in_sem.at[1])
    load_fluid.start()

    barrier = pltpu.get_barrier_semaphore()
    source_sec = jnp.where(is_down == 0, below, above)

    def greet(k, carry):
        for m in range(8):
            other = far_first(gy, k, m)
            pl.semaphore_signal(
                barrier, inc=1, device_id=(source_sec, other), device_id_type=MESH
            )
            if m < 7:
                pl.semaphore_signal(barrier, inc=1, device_id=(sec, other), device_id_type=MESH)
        return carry

    def greet_rest(k, carry):
        pl.semaphore_signal(
            barrier, inc=1, device_id=(sec, far_first(gy, k, 7)), device_id_type=MESH
        )
        return carry

    lax.fori_loop(0, 8, greet, 0)
    lax.fori_loop(0, 7, greet_rest, 0)

    plane = (LX, LY)
    lane = lanes(plane)
    field[...] = jnp.zeros_like(field)

    def order_pass():
        def one(z, carry):
            phi = state[19, z]
            for i in range(1, 19):
                phi = phi + state[19 + i, z]
            field[z, pl.ds(8, LX), pl.ds(0, LY)] = phi
            return carry

        lax.fori_loop(0, NZ, one, 0)

    def pack_faces():
        for j in range(2):
            a_up[:, j, :] = field[:, 8 + LX - 1 - j, pl.ds(0, LY)]
            a_down[:, j, :] = field[:, 8 + j, pl.ds(0, LY)]

    def pack_columns():
        to_left = jnp.zeros(plane, jnp.float32)
        to_right = to_left
        for z in range(NZ):
            phi = field[z, pl.ds(8, LX), pl.ds(0, LY)]
            mine = (lane >> 1) == z
            to_left = jnp.where(mine, turn(phi, 2 * z), to_left)
            to_right = jnp.where(mine, turn(phi, 2 * z + 2), to_right)
        a_edge[0] = to_left
        a_edge[1] = to_right

    def next_y(near, far):
        tile = lanes(near.shape)
        return jnp.where(tile == LY - 1, turn(far, LY - 1), turn(near, LY - 1))

    def last_y(near, far):
        tile = lanes(near.shape)
        return jnp.where(tile == 0, turn(far, 1), turn(near, 1))

    def face_potential(x, half):
        cut = pl.ds(half * LY, LY)
        tile = field[:, 8 + x, cut]
        other = field[:, 8 + x, pl.ds((1 - half) * LY, LY)]
        lap = (
            field[:, 9 + x, cut]
            + field[:, 7 + x, cut]
            + next_y(tile, other)
            + last_y(tile, other)
            + pltpu.roll(tile, 1, 0)
            + pltpu.roll(tile, NZ - 1, 0)
            - 6.0 * tile
        )
        return tile * (COEF_A + COEF_B * tile * tile) - KAPPA_GRAD * lap

    left_f = 1.0 - 1.0 / TAU_FLUID
    left_g = 1.0 - 1.0 / TAU_ORDER
    kick = 1.0 - 0.5 / TAU_FLUID
    rim = lanes((NZ, LY))

    def face_layer(x, potential):
        phi = field[:, 8 + x, pl.ds(0, LY)]
        middle = potential(x, 0)
        beyond = potential(x, 1)
        half = -0.5 * phi
        force = (
            half * (potential(x + 1, 0) - potential(x - 1, 0)),
            half * (next_y(middle, beyond) - last_y(middle, beyond)),
            half * (pltpu.roll(middle, NZ - 1, 0) - pltpu.roll(middle, 1, 0)),
        )
        density = mom[0, :, x, :]
        inverse = 1.0 / density
        vel = tuple((mom[1 + k, :, x, :] + 0.5 * force[k]) * inverse for k in range(3))
        square = vel[0] * vel[0] + vel[1] * vel[1] + vel[2] * vel[2]
        square_phi = phi * (1.0 / TAU_ORDER)
        base_phi = (3.0 * MOBILITY / TAU_ORDER) * middle - 1.5 * square_phi * square
        return phi, middle, force, density, vel, square, square_phi, base_phi

    def face_order(x, i, layer):
        _, middle, _, _, vel, square, square_phi, base_phi = layer
        kept = left_g * state[19 + i, :, x, :]
        if i == 0:
            return kept + (
                square_phi * (1.0 - 0.5 * square) - (2.0 * MOBILITY / TAU_ORDER) * middle
            )
        along = signed_sum(vel, VELOCITY[i])
        carried = square_phi * along
        return kept + WEIGHTS[i] * (base_phi + 4.5 * carried * along + 3.0 * carried)

    def streamed_sum(terms):
        groups = {0: None, 1: None, -1: None}
        for i, tile in terms:
            _, shift_y, shift_z = VELOCITY[i]
            if shift_z:
                tile = pltpu.roll(tile, shift_z % NZ, 0)
            held = groups[shift_y]
            groups[shift_y] = tile if held is None else held + tile
        total = (
            groups[0]
            + jnp.where(rim == 0, 0.0, turn(groups[1], 1))
            + jnp.where(rim == LY - 1, 0.0, turn(groups[-1], LY - 1))
        )
        return total, groups[1], groups[-1]

    def crossing(sums):
        result = jnp.zeros((NZ, LY), jnp.float32)
        for j, (_, forward, back) in enumerate(sums):
            result = jnp.where(rim == j, turn(forward, 1 + j), result)
            result = jnp.where(rim == LY - 1 - j, turn(back, LY - 1 - j), result)
        return result

    def face_collide(side, jump):
        members, others, x, inward = ((UPWARD, DOWNWARD, LX - 1, -1), (DOWNWARD, UPWARD, 0, 1))[side]
        made = {}

        def potential(layer_x, half):
            if (layer_x, half) not in made:
                made[layer_x, half] = face_potential(layer_x, half)
            return made[layer_x, half]

        layer = face_layer(x, potential)
        phi, middle, force, density, vel, square, square_phi, base_phi = layer
        drift = vel[0] * force[0] + vel[1] * force[1] + vel[2] * force[2]
        scaled = density * (1.0 / TAU_FLUID)
        base = scaled * (1.0 - 1.5 * square) - (3.0 * kick) * drift
        moved = vel[1] + jump
        change_square = 1.5 * (moved * moved - vel[1] * vel[1])
        leaving = []
        for k, i in enumerate(members):
            vector = VELOCITY[i]
            weight = WEIGHTS[i]
            along = signed_sum(vel, vector)
            pushed = signed_sum(force, vector)
            after = signed_sum((vel[0], moved, vel[2]), vector)
            change = weight * (
                3.0 * (after - along) + 4.5 * (after * after - along * along) - change_square
            )
            fluid = left_f * state[i, :, x, :] + weight * (
                base
                + along * (4.5 * scaled * along + (9.0 * kick) * pushed)
                + (3.0 * scaled * along + (3.0 * kick) * pushed)
            )
            order = face_order(x, i, layer) + phi * change
            leaving.append((i, order))
            for lift, value in ((0, fluid + density * change), (5, order)):
                b_send[side, 2 * (k + lift)] = value[:4]
                b_send[side, 2 * (k + lift) + 1] = value[4:]

        def make_parts():
            second = x + inward
            third = second + inward
            layers = {x: layer}
            for layer_x in (second, third):
                layers[layer_x] = face_layer(layer_x, potential)
            still = [i for i in range(19) if VELOCITY[i][0] == 0]

            def terms(layer_x, rows):
                return [(i, face_order(layer_x, i, layers[layer_x])) for i in rows]

            sums = [
                streamed_sum(terms(x, still) + terms(second, members)),
                streamed_sum(terms(second, still) + terms(third, members) + terms(x, others)),
                streamed_sum(leaving),
            ]
            for j in range(3):
                b_part[side, :, j, :] = sums[j][0]
            b_part[side, :, 3, :] = crossing(sums)
            b_own[side, :, 0, :] = sums[2][0]
            b_own[side, :, 1, :] = crossing(sums[2:])

        return make_parts

    def send(src, dst, which, slot, to_sec, to_gy):
        pltpu.make_async_remote_copy(
            src_ref=src,
            dst_ref=dst,
            send_sem=send_sem.at[which],
            recv_sem=recv_sem.at[which, slot],
            device_id=(to_sec, to_gy),
            device_id_type=MESH,
        ).start()

    load_order.wait()
    order_pass()
    pack_faces()
    pack_columns()
    load_offsets.wait()
    load_speeds.wait()
    pl.semaphore_wait(barrier, 2 * N_GY - 1)

    own = pl.ds(0, LY)
    halo = pl.ds(LY, LY)
    incoming = ((0, UPWARD, 0), (1, DOWNWARD, LX - 1))
    outside = ((0, -1, -2), (1, LX, LX + 1))

    def units_of(step):
        return jnp.where(
            is_down == 0, offsets[step, sec], (SPAN - offsets[step, above]) & (SPAN - 1)
        )

    def send_columns(step):
        send(a_edge.at[0], a_near.at[step, 1], 1, step, sec, left)
        send(a_edge.at[1], a_near.at[step, 0], 1, step, sec, right)

    def put_columns(step):
        wait_bytes(a_near.at[step], recv_sem.at[1, step])
        from_left = a_near[step, 0]
        from_right = a_near[step, 1]

        def one(z, carry):
            field[z, pl.ds(8, LX), halo] = jnp.where(
                lane < 2,
                turn(from_right, (LY - 2 * z) & (LY - 1)),
                jnp.where(lane >= LY - 2, turn(from_left, (LY - 2 - 2 * z) & (LY - 1)), 0.0),
            )
            return carry

        lax.fori_loop(0, NZ, one, 0)

    def moments():
        def one(z, carry):
            tiles = [state[i, z] for i in range(19)]
            mom[0, z] = signed_sum(tiles, (1,) * 19)
            for axis in range(3):
                mom[1 + axis, z] = signed_sum(tiles, [vector[axis] for vector in VELOCITY])
            return carry

        lax.fori_loop(0, NZ, one, 0)

    def exchange_order():
        def send_order(k, carry):
            for across, along in ((1, 1), (1, 0), (0, 1), (0, 0)):
                target = (
                    (((gy >> 5) ^ across) << 5) + (ring_z(gy, k) << 2) + ((gy & 2) ^ (2 * along))
                )
                z = (target >> 1) & 7
                send(a_up.at[z], a_land.at[gy], 0, 0, above, target)
                send(a_down.at[z], a_land.at[gy], 0, 0, below, target + 1)
            return carry

        lax.fori_loop(0, 8, send_order, 0, unroll=2)
        send_columns(0)
        load_fluid.wait()
        moments()
        parts = parts_of(units_of(0))
        wait_bytes(a_land, recv_sem.at[0, 0])
        near = slide(a_land[:, 0, :], parts)
        a_slid[:, 0, :] = near
        a_slid[:, 1, :] = slide(a_land[:, 1, :], parts)
        a_slid[:, 2, :] = rim_of(near, 1)
        a_role = 8 * is_down + a_z

        def send_slid_order(j, carry):
            block = gy ^ (16 - j)
            send(a_slid.at[block], a_ghost.at[a_role], 2, 0, sec, block)
            return carry

        lax.fori_loop(1, 16, send_slid_order, 0, unroll=5)
        pltpu.make_async_copy(a_slid.at[gy], a_ghost.at[a_role], recv_sem.at[2, 0]).start()
        put_columns(0)
        wait_bytes(a_ghost, recv_sem.at[2, 0])
        for side, near_x, far_x in outside:
            roles = pl.ds(8 * side, 8)
            field[:, 8 + near_x, own] = a_ghost[roles, 0, :]
            field[:, 8 + far_x, own] = a_ghost[roles, 1, :]
            field[:, 8 + near_x, halo] = a_ghost[roles, 2, :]
        wait_bytes(a_land, send_sem.at[0])
        wait_bytes(a_slid.at[pl.ds(0, 15)], send_sem.at[2])

    def potentials(z, carry):
        tall = lanes((32, LY))
        tiles = [field[z, :, own], field[z, :, halo]]
        ahead = [turn(tile, LY - 1) for tile in tiles]
        behind = [turn(tile, 1) for tile in tiles]
        for k in range(2):
            tile = tiles[k]
            cut = pl.ds(k * LY, LY)
            lap = (
                pltpu.roll(tile, 1, 0)
                + pltpu.roll(tile, 31, 0)
                + jnp.where(tall == LY - 1, ahead[1 - k], ahead[k])
                + jnp.where(tall == 0, behind[1 - k], behind[k])
                + field[(z + 1) & 7, :, cut]
                + field[(z + 7) & 7, :, cut]
                - 6.0 * tile
            )
            pot[z, :, cut] = tile * (COEF_A + COEF_B * tile * tile) - KAPPA_GRAD * lap
        return carry

    def collide(z, carry):
        to_left, to_right = carry
        rows = pl.ds(8, LX)
        inner = pot[z, rows, own]
        beyond = pot[z, rows, halo]
        phi = field[z, rows, own]
        half = -0.5 * phi
        force = (
            half * (pot[z, pl.ds(9, LX), own] - pot[z, pl.ds(7, LX), own]),
            half * (next_y(inner, beyond) - last_y(inner, beyond)),
            half * (pot[(z + 1) & 7, rows, own] - pot[(z + 7) & 7, rows, own]),
        )
        density = mom[0, z]
        inverse = 1.0 / density
        vel = tuple((mom[1 + k, z] + 0.5 * force[k]) * inverse for k in range(3))
        square = vel[0] * vel[0] + vel[1] * vel[1] + vel[2] * vel[2]
        drift = vel[0] * force[0] + vel[1] * force[1] + vel[2] * force[2]
        scaled = density * (1.0 / TAU_FLUID)
        base = scaled * (1.0 - 1.5 * square) - (3.0 * kick) * drift
        square_phi = phi * (1.0 / TAU_ORDER)
        base_phi = (3.0 * MOBILITY / TAU_ORDER) * inner - 1.5 * square_phi * square
        fluid = [None] * 19
        order = [None] * 19
        fluid[0] = left_f * state[0, z] + WEIGHTS[0] * base
        order[0] = left_g * state[19, z] + (
            square_phi * (1.0 - 0.5 * square) - (2.0 * MOBILITY / TAU_ORDER) * inner
        )
        for i in range(1, 19, 2):
            vector = VELOCITY[i]
            along = signed_sum(vel, vector)
            pushed = signed_sum(force, vector)
            weight = WEIGHTS[i]
            even = weight * (base + along * (4.5 * scaled * along + (9.0 * kick) * pushed))
            odd = weight * (3.0 * scaled * along + (3.0 * kick) * pushed)
            fluid[i] = left_f * state[i, z] + (even + odd)
            fluid[i + 1] = left_f * state[i + 1, z] + (even - odd)
            carried = square_phi * along
            even = weight * (base_phi + 4.5 * carried * along)
            odd = (3.0 * weight) * carried
            order[i] = left_g * state[19 + i, z] + (even + odd)
            order[i + 1] = left_g * state[20 + i, z] + (even - odd)
        for i in range(19):
            post[i, z] = fluid[i]
            post[19 + i, z] = order[i]
        going_left = jnp.zeros(plane, jnp.float32)
        going_right = jnp.zeros(plane, jnp.float32)
        for k in range(10):
            part = fluid if k < 5 else order
            going_right = jnp.where(
                lane == 8 * k, turn(part[Y_PLUS[k % 5]], 8 * k + 1), going_right
            )
            going_left = jnp.where(lane == 8 * k, turn(part[Y_MINUS[k % 5]], 8 * k), going_left)
        mine = (lane & 7) == z
        to_left = jnp.where(mine, turn(going_left, z), to_left)
        to_right = jnp.where(mine, turn(going_right, z), to_right)
        return to_left, to_right

    def pass_ghosts(step):
        member = lax.rem(b_role >> 1, 5)
        along_y = jnp.where(member == 1, -1, jnp.where(member == 2, 1, 0)) * (1 - 2 * is_down)
        parts = parts_of(units_of(step))
        slot = ROLES * is_down + b_role
        wait_bytes(b_lands[step], recv_sem.at[3, step])

        for j in range(4):
            b_slid[:, j, :] = slide(b_lands[step][:, j, :], parts, along_y)
        pass_on(step, slot)

    def pass_on(step, slot):
        def one(k, m):
            block = far_first(gy, k, m)
            send(b_slid.at[block], b_ghost.at[step, slot], 5, step, sec, block)

        def several(k, carry):
            for m in range(8):
                one(k, m)
            return carry

        lax.fori_loop(0, 7, several, 0)
        for m in range(7):
            one(7, m)
        pltpu.make_async_copy(
            b_slid.at[gy], b_ghost.at[step, slot], recv_sem.at[5, step]
        ).start()

    def pass_order(step):
        units = units_of(step)
        parts = parts_of(units)
        parts_back = parts_of((SPAN - units) & (SPAN - 1))
        parts_next = parts_of(units_of(step + 1))
        line = lanes((N_GY, LY))

        def complete(sums, crossed, j):
            forward = rows_before(turn(crossed, (LY - j) % LY) if j else crossed)
            back = rows_after(turn(crossed, j) if j else crossed)
            return sums + jnp.where(line == 0, forward, jnp.where(line == LY - 1, back, 0.0))

        wait_bytes(b_back, recv_sem.at[7, step])
        returned = slide(complete(b_back[:, 0, :], b_back[:, 1, :], 0), parts_back)
        wait_bytes(b_lands[step], recv_sem.at[6, step])
        land = b_lands[step]
        crossed = land[:, 3, :]
        near = slide(complete(land[:, 0, :], crossed, 0) + returned, parts_next)
        b_slid[:, 0, :] = near
        b_slid[:, 1, :] = slide(complete(land[:, 1, :], crossed, 1), parts_next)
        b_slid[:, 2, :] = rim_of(near, 1)
        b_slid[:, 3, :] = rim_of(slide(complete(land[:, 2, :], crossed, 2), parts), 2)
        pass_on(step, GHOSTS + 8 * is_down + group)

    def stream_level(z, carry):
        for which in range(38):
            shift_x, shift_y, shift_z = VELOCITY[which % 19]
            if shift_y == 0:
                tile = post[which, (z - shift_z) & 7]
                if shift_x:
                    tile = pltpu.roll(tile, shift_x % LX, 0)
                state[which, z] = tile
        return carry

    def stream_along_y(z, carry):
        near_left, near_right = carry
        columns = {}
        for shift_z in (-1, 0, 1):
            source = (z - shift_z) & 7
            back = (LY - source) & (LY - 1)
            columns[1, shift_z] = turn(near_left, back)
            columns[-1, shift_z] = turn(near_right, back)
        for which in range(38):
            i = which % 19
            shift_x, shift_y, shift_z = VELOCITY[i]
            if shift_y == 0:
                continue
            tile = post[which, (z - shift_z) & 7]
            if shift_y == 1:
                k = Y_PLUS.index(i) + (5 if which >= 19 else 0)
                outer = turn(columns[1, shift_z], (LY - 8 * k) % LY)
                tile = jnp.where(lane == 0, outer, turn(tile, 1))
            else:
                k = Y_MINUS.index(i) + (5 if which >= 19 else 0)
                outer = turn(columns[-1, shift_z], (LY - 1 - 8 * k) % LY)
                tile = jnp.where(lane == LY - 1, outer, turn(tile, LY - 1))
            if shift_x:
                tile = pltpu.roll(tile, shift_x % LX, 0)
            state[which, z] = tile
        return carry

    def take_ghosts(step):
        for side, members, x in incoming:
            order_sum = None
            tiles = []
            for k in range(10):
                i = members[k % 5]
                rows = b_ghost[step, pl.ds(ROLES * side + 2 * k, 2)].reshape(NZ, LY)
                if VELOCITY[i][2]:
                    rows = pltpu.roll(rows, VELOCITY[i][2] % NZ, 0)
                state[i + (19 if k >= 5 else 0), :, x, :] = rows
                if k >= 5:
                    order_sum = rows if order_sum is None else order_sum + rows
                else:
                    tiles.append(rows)
            field[:, 8 + x, own] = field[:, 8 + x, own] + order_sum
            mom[0, :, x, :] = mom[0, :, x, :] + signed_sum(tiles, (1,) * 5)
            for axis in range(3):
                mom[1 + axis, :, x, :] = mom[1 + axis, :, x, :] + signed_sum(
                    tiles, [VELOCITY[i][axis] for i in members]
                )
        for side, near_x, far_x in outside:
            roles = pl.ds(GHOSTS + 8 * side, 8)
            x = 0 if side == 0 else LX - 1
            field[:, 8 + near_x, own] = b_ghost[step, roles, 0, :]
            field[:, 8 + far_x, own] = b_ghost[step, roles, 1, :]
            field[:, 8 + near_x, halo] = b_ghost[step, roles, 2, :]
            field[:, 8 + x, halo] = field[:, 8 + x, halo] + b_ghost[step, roles, 3, :]

    def send_ghosts(step):
        for change in FAR_GROUPS:
            other = (gy >> 3) ^ change
            for place in range(2):
                role = 8 * place + other
                target = 8 * other + 2 * place
                send(b_send.at[0, role], b_lands[step].at[gy], 3, step, above, target)
                send(b_send.at[1, role], b_lands[step].at[gy], 3, step, below, target + 1)
            if change & 1 == 0:
                even = other & 6
                role = 16 + (even >> 1)
                target = 8 * even + 4
                send(b_send.at[0, role], b_lands[step].at[gy], 3, step, above, target)
                send(b_send.at[1, role], b_lands[step].at[gy], 3, step, below, target + 1)

    def send_parts(step):
        for change in FAR_GROUPS:
            z = (gy >> 3) ^ change
            target = 8 * z + 6
            send(b_part.at[0, z], b_lands[step].at[gy], 6, step, above, target)
            send(b_part.at[1, z], b_lands[step].at[gy], 6, step, below, target + 1)
            for side in (0, 1):
                to = target + 1 - side
                if change:
                    send(b_own.at[side, z], b_back.at[gy], 7, step, sec, to)
                else:

                    @pl.when(to != gy)
                    def _():
                        send(b_own.at[side, z], b_back.at[gy], 7, step, sec, to)

        @pl.when(is_phi)
        def _():
            pltpu.make_async_copy(
                b_own.at[1 - is_down, group], b_back.at[gy], recv_sem.at[7, step]
            ).start()

    exchange_order()
    for step in range(STEPS):
        last = step == STEPS - 1
        jump_up = speeds[above].astype(jnp.float32) * (-1.0 / 256.0)
        jump_down = speeds[sec].astype(jnp.float32) * (1.0 / 256.0)
        make_parts = [face_collide(0, jump_up), face_collide(1, jump_down)]
        send_ghosts(step)
        if not last:
            for make in make_parts:
                make()
            send_parts(step)

        lax.fori_loop(0, NZ, potentials, 0)
        zero = jnp.zeros(plane, jnp.float32)
        to_left, to_right = lax.fori_loop(0, NZ, collide, (zero, zero))
        b_edge[0] = to_left
        b_edge[1] = to_right
        send(b_edge.at[0], b_near.at[step, 1], 4, step, sec, left)
        send(b_edge.at[1], b_near.at[step, 0], 4, step, sec, right)
        lax.fori_loop(0, NZ, stream_level, 0)

        if step > 0:
            @pl.when(jnp.logical_or(is_owner, is_phi))
            def _():
                wait_bytes(b_slid.at[pl.ds(0, N_GY - 1)], send_sem.at[5])

        @pl.when(is_owner)
        def _():
            pass_ghosts(step)

        if not last:

            @pl.when(is_phi)
            def _():
                pass_order(step)

        wait_bytes(b_near.at[step], recv_sem.at[4, step])
        lax.fori_loop(0, NZ, stream_along_y, (b_near[step, 0], b_near[step, 1]))
        wait_bytes(a_edge, send_sem.at[1])
        if last:
            store_fluid = pltpu.make_async_copy(state.at[pl.ds(0, 19)], fluid_out, out_sem.at[0])
            store_order = pltpu.make_async_copy(state.at[pl.ds(19, 19)], order_out, out_sem.at[1])
            store_fluid.start()
            store_order.start()
        else:
            for side, members, x in incoming:
                for i in members:
                    state[i, :, x, :] = jnp.zeros((NZ, LY), jnp.float32)
                    state[19 + i, :, x, :] = jnp.zeros((NZ, LY), jnp.float32)
            order_pass()
            pack_columns()
            send_columns(step + 1)
            moments()
            put_columns(step + 1)

        wait_bytes(b_send, send_sem.at[3])
        wait_bytes(b_edge, send_sem.at[4])
        if last:
            wait_bytes(b_ghost.at[step, pl.ds(0, GHOSTS)], recv_sem.at[5, step])
            store_ghosts = pltpu.make_async_copy(
                b_ghost.at[step, pl.ds(0, GHOSTS)], ghosts_out, out_sem.at[2]
            )
            store_ghosts.start()

            @pl.when(is_owner)
            def _():
                wait_bytes(b_slid.at[pl.ds(0, N_GY - 1)], send_sem.at[5])

            store_fluid.wait()
            store_order.wait()
            store_ghosts.wait()
        else:
            wait_bytes(b_part, send_sem.at[6])
            wait_bytes(b_ghost.at[step], recv_sem.at[5, step])
            take_ghosts(step)

            @pl.when(is_phi)
            def _():
                wait_bytes(b_own.at[:, pl.ds(0, 7)], send_sem.at[7])
                wait_bytes(b_own.at[0, 0], send_sem.at[7])

            @pl.when(jnp.logical_not(is_phi))
            def _():
                wait_bytes(b_own, send_sem.at[7])


def finish(
    fluid_in, order_in, ghosts_in, fluid_out, order_out, held, ghosts, in_sem, out_sem, ghost_sem
):
    load_ghosts = pltpu.make_async_copy(ghosts_in, ghosts, ghost_sem)
    load_ghosts.start()
    loads, stores, firsts = [], [], []
    for start, size in ((0, 5), (5, 5), (10, 5), (15, 4)):
        for half, src, dst in ((0, fluid_in, fluid_out), (19, order_in, order_out)):
            k = len(loads)
            here = held.at[pl.ds(half + start, size)]
            cut = pl.ds(start, size)
            loads.append(pltpu.make_async_copy(src.at[cut], here, in_sem.at[k]))
            stores.append(pltpu.make_async_copy(here, dst.at[cut], out_sem.at[k]))
            firsts.append((half + start, size))
    for load in loads:
        load.start()
    load_ghosts.wait()
    for load, store, (first, size) in zip(loads, stores, firsts):
        load.wait()
        for side, members, x in ((0, UPWARD, 0), (1, DOWNWARD, LX - 1)):
            for k in range(10):
                i = members[k % 5]
                which = i + (19 if k >= 5 else 0)
                if first <= which < first + size:
                    rows = ghosts[pl.ds(ROLES * side + 2 * k, 2)].reshape(NZ, LY)
                    if VELOCITY[i][2]:
                        rows = pltpu.roll(rows, VELOCITY[i][2] % NZ, 0)
                    held[which, :, x, :] = rows
        store.start()
    for store in stores:
        store.wait()


def per_device(fluid_dist, order_dist, plane_offset, plane_speed):
    shape = jax.ShapeDtypeStruct((19, NZ, LX, LY), jnp.float32)
    ghosts = jax.ShapeDtypeStruct((GHOSTS, 4, LY), jnp.float32)
    hbm = pl.BlockSpec(memory_space=pl.ANY)
    dma = pltpu.SemaphoreType.DMA

    def scratch(*dims):
        return pltpu.VMEM(dims, jnp.float32)

    results = pl.pallas_call(
        kernel,
        out_shape=(shape, shape, ghosts),
        in_specs=[hbm] * 4,
        out_specs=(hbm, hbm, hbm),
        scratch_shapes=[
            pltpu.SMEM((STEPS, N_SEC), jnp.int32),
            pltpu.SMEM((N_SEC,), jnp.int32),
            scratch(38, NZ, LX, LY),
            scratch(38, NZ, LX, LY),
            scratch(NZ, 32, 2 * LY),
            scratch(NZ, 32, 2 * LY),
            scratch(4, NZ, LX, LY),
            scratch(NZ, 2, LY),
            scratch(NZ, 2, LY),
            scratch(2, LX, LY),
            scratch(N_GY, 2, LY),
            scratch(N_GY, 3, LY),
            scratch(16, 3, LY),
            scratch(STEPS, 2, LX, LY),
            scratch(2, ROLES, 4, LY),
            scratch(2, NZ, 4, LY),
            scratch(2, NZ, 2, LY),
            scratch(2, LX, LY),
            scratch(N_GY, 4, LY),
            scratch(N_GY, 4, LY),
            scratch(N_GY, 2, LY),
            scratch(N_GY, 4, LY),
            scratch(STEPS, GHOSTS + 16, 4, LY),
            scratch(STEPS, 2, LX, LY),
            dma((4,)),
            dma((3,)),
            dma((8,)),
            dma((8, STEPS)),
        ],
        compiler_params=pltpu.CompilerParams(
            collective_id=0, has_side_effects=True, vmem_limit_bytes=60 * 1024 * 1024
        ),
    )(fluid_dist, order_dist, plane_offset, plane_speed)
    return pl.pallas_call(
        finish,
        out_shape=(shape, shape),
        in_specs=[hbm] * 3,
        out_specs=(hbm, hbm),
        scratch_shapes=[
            scratch(38, NZ, LX, LY),
            scratch(GHOSTS, 4, LY),
            dma((8,)),
            dma((8,)),
            dma,
        ],
        compiler_params=pltpu.CompilerParams(vmem_limit_bytes=60 * 1024 * 1024),
    )(*results)


def solution(mesh):
    split = P(None, None, "sec", "gy")
    return jax.shard_map(
        per_device,
        mesh=mesh,
        in_specs=(split, split, P(), P()),
        out_specs=(split, split),
        check_vma=False,
    )
```

```python
import jax
import jax.numpy as jnp
from jax import lax
from jax.experimental import pallas as pl
from jax.experimental.pallas import tpu as pltpu
from jax.sharding import PartitionSpec as P

STEPS = 2
VELOCITY = (
    (0, 0, 0),
    (1, 0, 0),
    (-1, 0, 0),
    (0, 1, 0),
    (0, -1, 0),
    (0, 0, 1),
    (0, 0, -1),
    (1, 1, 0),
    (-1, -1, 0),
    (1, -1, 0),
    (-1, 1, 0),
    (1, 0, 1),
    (-1, 0, -1),
    (1, 0, -1),
    (-1, 0, 1),
    (0, 1, 1),
    (0, -1, -1),
    (0, 1, -1),
    (0, -1, 1),
)
WEIGHTS = (1.0 / 3.0,) + (1.0 / 18.0,) * 6 + (1.0 / 36.0,) * 12
UPWARD = (1, 7, 9, 11, 13)
DOWNWARD = (2, 8, 10, 12, 14)
Y_PLUS = (3, 7, 10, 15, 17)
Y_MINUS = (4, 8, 9, 16, 18)
COEF_A = -0.0625
COEF_B = 0.0625
KAPPA_GRAD = 0.04
MOBILITY = 1.0
TAU_FLUID = 0.8
TAU_ORDER = 0.9
NZ = 8
LX = 16
LY = 128
N_SEC = 4
N_GY = 64
SPAN = LY * N_GY * 256
ROLES = 32
KINDS = 17
WIDE = 2 * LY
EDGES = (0, 1, LX - 2, LX - 1)
MESH = pl.DeviceIdType.MESH
FAR_GROUPS = (6, 5, 7, 2, 4, 1, 3, 0)
ACROSS = ((1, 2), (1, 1), (1, 3), (0, 2), (1, 0), (0, 1), (0, 3), (0, 0))


def lanes(shape):
    return lax.broadcasted_iota(jnp.int32, shape, len(shape) - 1)


def turn(value, shift):
    return pltpu.roll(value, shift, value.ndim - 1)


def ring_z(gy, k):
    half = (k + 1) >> 1
    return ((gy >> 2) + 4 + jnp.where((k & 1) == 1, -half, half)) & 7


def far_first(gy, k, m):
    across, along = ACROSS[m]
    return (((gy >> 5) ^ across) << 5) + (ring_z(gy, k) << 2) + ((gy + along) & 3)


def signed_sum(terms, signs):
    total = None
    for term, sign in zip(terms, signs):
        if sign == 0:
            continue
        if total is None:
            total = term if sign > 0 else -term
        else:
            total = total + term if sign > 0 else total - term
    return total


def wait_bytes(ref, sem):
    pltpu.make_async_copy(ref, ref, sem).wait()


def parts_of(units):
    frac = (units & 255).astype(jnp.float32) * (1.0 / 256.0)
    return units >> 8, 1.0 - frac, frac


def rows_after(value):
    return pltpu.roll(value, N_GY - 1, 0)


def rows_before(value):
    return pltpu.roll(value, 1, 0)


def shifted_line(value, whole):
    inside = whole & (LY - 1)
    tile = lanes(value.shape)
    value = turn(value, (LY - inside) & (LY - 1))
    value = jnp.where(tile < LY - inside, value, rows_after(value))
    return pltpu.roll(value, (N_GY - (whole >> 7)) & (N_GY - 1), 0)


def potential_of(middle, one, other):
    lap = (
        one
        + other
        + turn(middle, 1)
        + turn(middle, WIDE - 1)
        + pltpu.roll(middle, 1, 0)
        + pltpu.roll(middle, NZ - 1, 0)
        - 6.0 * middle
    )
    return middle * (COEF_A + COEF_B * middle * middle) - KAPPA_GRAD * lap


LEFT_F = 1.0 - 1.0 / TAU_FLUID
LEFT_G = 1.0 - 1.0 / TAU_ORDER
KICK = 1.0 - 0.5 / TAU_FLUID


class Layer:
    def __init__(self, phi, low, middle, high, density, flow):
        half = -0.5 * phi
        self.phi, self.middle, self.density = phi, middle, density
        self.force = (
            half * (high - low),
            half * (turn(middle, WIDE - 1) - turn(middle, 1)),
            half * (pltpu.roll(middle, NZ - 1, 0) - pltpu.roll(middle, 1, 0)),
        )
        inverse = 1.0 / density
        self.vel = tuple((flow[k] + 0.5 * self.force[k]) * inverse for k in range(3))
        vel, force = self.vel, self.force
        self.square = vel[0] * vel[0] + vel[1] * vel[1] + vel[2] * vel[2]
        drift = vel[0] * force[0] + vel[1] * force[1] + vel[2] * force[2]
        self.scaled = density * (1.0 / TAU_FLUID)
        self.base = self.scaled * (1.0 - 1.5 * self.square) - (3.0 * KICK) * drift
        self.square_phi = phi * (1.0 / TAU_ORDER)
        self.base_phi = (
            3.0 * MOBILITY / TAU_ORDER
        ) * middle - 1.5 * self.square_phi * self.square

    def fluid(self, i, value):
        kept = LEFT_F * value
        if i == 0:
            return kept + WEIGHTS[0] * self.base
        along = signed_sum(self.vel, VELOCITY[i])
        pushed = signed_sum(self.force, VELOCITY[i])
        return kept + WEIGHTS[i] * (
            self.base
            + along * (4.5 * self.scaled * along + (9.0 * KICK) * pushed)
            + (3.0 * self.scaled * along + (3.0 * KICK) * pushed)
        )

    def order(self, i, value):
        kept = LEFT_G * value
        if i == 0:
            return kept + (
                self.square_phi * (1.0 - 0.5 * self.square)
                - (2.0 * MOBILITY / TAU_ORDER) * self.middle
            )
        along = signed_sum(self.vel, VELOCITY[i])
        carried = self.square_phi * along
        return kept + WEIGHTS[i] * (self.base_phi + 4.5 * carried * along + 3.0 * carried)

    def change(self, i, jump):
        moved = self.vel[1] + jump
        along = signed_sum(self.vel, VELOCITY[i])
        after = signed_sum((self.vel[0], moved, self.vel[2]), VELOCITY[i])
        return WEIGHTS[i] * (
            3.0 * (after - along)
            + 4.5 * (after * after - along * along)
            - 1.5 * (moved * moved - self.vel[1] * self.vel[1])
        )


def streamed(value, i):
    _, shift_y, shift_z = VELOCITY[i]
    if shift_y:
        value = turn(value, shift_y % WIDE)
    if shift_z:
        value = pltpu.roll(value, shift_z % NZ, 0)
    return value[:, :LY]


def kernel(
    fluid_in, order_in, offsets_in, speeds_in, fluid_out, order_out,
    offsets, speeds, state, post, field, pot, mom, kept,
    a_edge, a_near,
    r_send, r_land_0, r_land_1, r_slid, r_ghost,
    in_sem, out_sem, send_sem, recv_sem,
):
    lands = (r_land_0, r_land_1)
    sec = lax.axis_index("sec")
    gy = lax.axis_index("gy")
    above = (sec + 1) & (N_SEC - 1)
    below = (sec + N_SEC - 1) & (N_SEC - 1)
    left = (gy + N_GY - 1) & (N_GY - 1)
    right = (gy + 1) & (N_GY - 1)
    is_down = gy & 1
    slot = ROLES * (gy & 1) + (gy >> 1)
    load_order = pltpu.make_async_copy(order_in, state.at[pl.ds(19, 19)], in_sem.at[0])
    load_order.start()
    load_offsets = pltpu.make_async_copy(offsets_in, offsets, in_sem.at[2])
    load_offsets.start()
    load_speeds = pltpu.make_async_copy(speeds_in, speeds, in_sem.at[3])
    load_speeds.start()
    load_fluid = pltpu.make_async_copy(fluid_in, state.at[pl.ds(0, 19)], in_sem.at[1])
    load_fluid.start()

    barrier = pltpu.get_barrier_semaphore()
    source_sec = jnp.where(is_down == 0, below, above)

    def greet(k, carry):
        for m in range(8):
            other = far_first(gy, k, m)
            pl.semaphore_signal(
                barrier, inc=1, device_id=(source_sec, other), device_id_type=MESH
            )
            if m < 7:
                pl.semaphore_signal(barrier, inc=1, device_id=(sec, other), device_id_type=MESH)
        return carry

    def greet_rest(k, carry):
        pl.semaphore_signal(
            barrier, inc=1, device_id=(sec, far_first(gy, k, 7)), device_id_type=MESH
        )
        return carry

    lax.fori_loop(0, 8, greet, 0)
    lax.fori_loop(0, 7, greet_rest, 0)

    plane = (LX, LY)
    lane = lanes(plane)
    rim = lanes((NZ, LY))
    level = lax.broadcasted_iota(jnp.int32, (NZ, LY), 0) & 3
    field[...] = jnp.zeros_like(field)
    r_send[...] = jnp.zeros_like(r_send)

    def order_pass():
        def one(z, carry):
            phi = state[19, z]
            for i in range(1, 19):
                phi = phi + state[19 + i, z]
            field[z, pl.ds(8, LX), pl.ds(0, LY)] = phi
            return carry

        lax.fori_loop(0, NZ, one, 0)

    def prepare_faces():
        for side, members, x, inward in ((0, UPWARD, LX - 1, -1), (1, DOWNWARD, 0, 1)):
            fluid = [state[i, :, x, :] for i in range(19)]
            tiles = [fluid[i] for i in members] + [state[19 + i, :, x, :] for i in members]
            tiles.append(signed_sum(fluid, (1,) * 19))
            for axis in range(3):
                tiles.append(signed_sum(fluid, [vector[axis] for vector in VELOCITY]))
            for depth in range(3):
                layer = [state[19 + i, :, x + depth * inward, :] for i in range(19)]
                tiles.append(signed_sum(layer, (1,) * 19))
            for k in range(KINDS - 1):
                r_send[side, 2 * k, pl.ds(0, 4), :] = tiles[k][:4]
                r_send[side, 2 * k + 1, pl.ds(0, 4), :] = tiles[k][4:]
            r_send[side, pl.ds(0, NZ), 4, :] = tiles[KINDS - 1]

    def send_faces(step):
        for change in FAR_GROUPS:
            for place in range(4):
                role = 4 * ((gy >> 3) ^ change) + place
                send(r_send.at[0, role], lands[step].at[gy], 0, step, above, 2 * role)
                send(r_send.at[1, role], lands[step].at[gy], 0, step, below, 2 * role + 1)

    def pack_columns():
        to_left = jnp.zeros(plane, jnp.float32)
        to_right = to_left
        for z in range(NZ):
            phi = field[z, pl.ds(8, LX), pl.ds(0, LY)]
            mine = (lane >> 2) == z
            to_left = jnp.where(mine, turn(phi, 4 * z), to_left)
            to_right = jnp.where(mine, turn(phi, 4 * z + 4), to_right)
        a_edge[0, pl.ds(0, LX), :] = to_left
        a_edge[1, pl.ds(0, LX), :] = to_right
        for side, rows in ((0, Y_MINUS), (1, Y_PLUS)):
            packed = jnp.zeros((NZ, LY), jnp.float32)
            for n, x in enumerate(EDGES):
                tiles = [kept[i, n] for i in rows] + [kept[19 + i, n] for i in rows]
                tiles += [mom[k, :, x, :] for k in range(4)]
                for k, tile in enumerate(tiles):
                    at = 32 * n + k
                    packed = jnp.where(rim == at, turn(tile, (at + side) % LY), packed)
            a_edge[side, pl.ds(LX, NZ), :] = packed

        def pack(z, carry):
            result = []
            for side, rows in ((0, Y_MINUS), (1, Y_PLUS)):
                tiles = [state[i, z] for i in rows] + [state[19 + i, z] for i in rows]
                tiles += [mom[k, z] for k in range(4)]
                going = jnp.zeros(plane, jnp.float32)
                for k, tile in enumerate(tiles):
                    going = jnp.where(lane == 8 * k, turn(tile, 8 * k + side), going)
                result.append(jnp.where((lane & 7) == z, turn(going, z), carry[side]))
            return tuple(result)

        zero = jnp.zeros(plane, jnp.float32)
        packed = lax.fori_loop(0, NZ, pack, (zero, zero))
        for side in range(2):
            a_edge[side, pl.ds(LX + NZ, LX), :] = packed[side]

    def keep_edges():
        for which in range(38):
            for n, x in enumerate(EDGES):
                kept[which, n] = state[which, :, x, :]

    def next_y(near, far):
        tile = lanes(near.shape)
        return jnp.where(tile == LY - 1, turn(far, LY - 1), turn(near, LY - 1))

    def last_y(near, far):
        tile = lanes(near.shape)
        return jnp.where(tile == 0, turn(far, 1), turn(near, 1))

    left_f, left_g, kick = LEFT_F, LEFT_G, KICK

    def send(src, dst, which, slot, to_sec, to_gy):
        pltpu.make_async_remote_copy(
            src_ref=src,
            dst_ref=dst,
            send_sem=send_sem.at[which],
            recv_sem=recv_sem.at[which, slot],
            device_id=(to_sec, to_gy),
            device_id_type=MESH,
        ).start()

    def moments():
        def one(z, carry):
            tiles = [state[i, z] for i in range(19)]
            mom[0, z] = signed_sum(tiles, (1,) * 19)
            for axis in range(3):
                mom[1 + axis, z] = signed_sum(tiles, [vector[axis] for vector in VELOCITY])
            return carry

        lax.fori_loop(0, NZ, one, 0)

    load_order.wait()
    order_pass()
    load_fluid.wait()
    prepare_faces()
    moments()
    keep_edges()
    pack_columns()
    load_offsets.wait()
    load_speeds.wait()
    pl.semaphore_wait(barrier, 2 * N_GY - 1)

    own = pl.ds(0, LY)
    halo = pl.ds(LY, LY)
    def units_of(step):
        return jnp.where(
            is_down == 0, offsets[step, sec], (SPAN - offsets[step, above]) & (SPAN - 1)
        )

    def send_columns(step):
        send(a_edge.at[0], a_near.at[step, 1], 1, step, sec, left)
        send(a_edge.at[1], a_near.at[step, 0], 1, step, sec, right)

    def put_columns(step):
        wait_bytes(a_near.at[step], recv_sem.at[1, step])
        from_left = a_near[step, 0, pl.ds(0, LX), :]
        from_right = a_near[step, 1, pl.ds(0, LX), :]

        def one(z, carry):
            field[z, pl.ds(8, LX), halo] = jnp.where(
                lane < 4,
                turn(from_right, (LY - 4 * z) & (LY - 1)),
                jnp.where(lane >= LY - 4, turn(from_left, (LY - 4 - 4 * z) & (LY - 1)), 0.0),
            )
            return carry

        lax.fori_loop(0, NZ, one, 0)

    def potentials(z, carry):
        tall = lanes((32, LY))
        tiles = [field[z, :, own], field[z, :, halo]]
        ahead = [turn(tile, LY - 1) for tile in tiles]
        behind = [turn(tile, 1) for tile in tiles]
        for k in range(2):
            tile = tiles[k]
            cut = pl.ds(k * LY, LY)
            lap = (
                pltpu.roll(tile, 1, 0)
                + pltpu.roll(tile, 31, 0)
                + jnp.where(tall == LY - 1, ahead[1 - k], ahead[k])
                + jnp.where(tall == 0, behind[1 - k], behind[k])
                + field[(z + 1) & 7, :, cut]
                + field[(z + 7) & 7, :, cut]
                - 6.0 * tile
            )
            pot[z, :, cut] = tile * (COEF_A + COEF_B * tile * tile) - KAPPA_GRAD * lap
        return carry

    def collide(z, carry):
        rows = pl.ds(8, LX)
        inner = pot[z, rows, own]
        beyond = pot[z, rows, halo]
        phi = field[z, rows, own]
        half = -0.5 * phi
        force = (
            half * (pot[z, pl.ds(9, LX), own] - pot[z, pl.ds(7, LX), own]),
            half * (next_y(inner, beyond) - last_y(inner, beyond)),
            half * (pot[(z + 1) & 7, rows, own] - pot[(z + 7) & 7, rows, own]),
        )
        density = mom[0, z]
        inverse = 1.0 / density
        vel = tuple((mom[1 + k, z] + 0.5 * force[k]) * inverse for k in range(3))
        square = vel[0] * vel[0] + vel[1] * vel[1] + vel[2] * vel[2]
        drift = vel[0] * force[0] + vel[1] * force[1] + vel[2] * force[2]
        scaled = density * (1.0 / TAU_FLUID)
        base = scaled * (1.0 - 1.5 * square) - (3.0 * kick) * drift
        square_phi = phi * (1.0 / TAU_ORDER)
        base_phi = (3.0 * MOBILITY / TAU_ORDER) * inner - 1.5 * square_phi * square
        fluid = [None] * 19
        order = [None] * 19
        fluid[0] = left_f * state[0, z] + WEIGHTS[0] * base
        order[0] = left_g * state[19, z] + (
            square_phi * (1.0 - 0.5 * square) - (2.0 * MOBILITY / TAU_ORDER) * inner
        )
        for i in range(1, 19, 2):
            vector = VELOCITY[i]
            along = signed_sum(vel, vector)
            pushed = signed_sum(force, vector)
            weight = WEIGHTS[i]
            even = weight * (base + along * (4.5 * scaled * along + (9.0 * kick) * pushed))
            odd = weight * (3.0 * scaled * along + (3.0 * kick) * pushed)
            fluid[i] = left_f * state[i, z] + (even + odd)
            fluid[i + 1] = left_f * state[i + 1, z] + (even - odd)
            carried = square_phi * along
            even = weight * (base_phi + 4.5 * carried * along)
            odd = (3.0 * weight) * carried
            order[i] = left_g * state[19 + i, z] + (even + odd)
            order[i + 1] = left_g * state[20 + i, z] + (even - odd)
        for i in range(19):
            post[i, z] = fluid[i]
            post[19 + i, z] = order[i]
        return carry

    def collide_beyond(step):
        from_left = a_near[step, 0, pl.ds(LX + NZ, LX), :]
        from_right = a_near[step, 1, pl.ds(LX + NZ, LX), :]
        at_left = lane < LY // 2

        def both(k):
            return jnp.where(
                at_left, turn(from_left, (LY - 8 * k) % LY), turn(from_right, (LY // 2 - 8 * k) % LY)
            )

        def gathered(left_tile, left_lane, right_tile, right_lane, height):
            result = jnp.zeros((height, LY), jnp.float32)
            tall = lanes((height, LY))
            for z in range(NZ):
                moved_left = turn(left_tile(z), (z - left_lane) % LY)
                moved_right = turn(right_tile(z), (LY // 2 + z - right_lane) % LY)
                result = jnp.where(
                    tall == z, moved_left, jnp.where(tall == LY // 2 + z, moved_right, result)
                )
            return result

        rows = pl.ds(8, LX)
        before = gathered(lambda z: pot[z, rows, halo], LY - 2, lambda z: pot[z, rows, own], LY - 1, LX)
        after = gathered(lambda z: pot[z, rows, own], 0, lambda z: pot[z, rows, halo], 1, LX)
        middle = gathered(lambda z: pot[z, :, halo], LY - 1, lambda z: pot[z, :, halo], 0, 32)
        phi = gathered(lambda z: field[z, rows, halo], LY - 1, lambda z: field[z, rows, halo], 0, LX)
        inner = middle[8:24]
        half = -0.5 * phi
        next_z = jnp.where((lane & 7) == 7, turn(inner, 7), turn(inner, LY - 1))
        last_z = jnp.where((lane & 7) == 0, turn(inner, LY - 7), turn(inner, 1))
        force = (half * (middle[9:25] - middle[7:23]), half * (after - before), half * (next_z - last_z))
        density = both(10)
        inverse = 1.0 / density
        vel = tuple((both(11 + k) + 0.5 * force[k]) * inverse for k in range(3))
        square = vel[0] * vel[0] + vel[1] * vel[1] + vel[2] * vel[2]
        drift = vel[0] * force[0] + vel[1] * force[1] + vel[2] * force[2]
        scaled = density * (1.0 / TAU_FLUID)
        base = scaled * (1.0 - 1.5 * square) - (3.0 * kick) * drift
        square_phi = phi * (1.0 / TAU_ORDER)
        base_phi = (3.0 * MOBILITY / TAU_ORDER) * inner - 1.5 * square_phi * square
        sign = jnp.where(at_left, 1.0, -1.0)
        to_left = jnp.zeros(plane, jnp.float32)
        to_right = to_left
        for k, i in enumerate(Y_PLUS):
            weight = WEIGHTS[i]
            along = sign * signed_sum(vel, VELOCITY[i])
            pushed = sign * signed_sum(force, VELOCITY[i])
            carried = square_phi * along
            fluid = left_f * both(k) + weight * (
                base
                + along * (4.5 * scaled * along + (9.0 * kick) * pushed)
                + (3.0 * scaled * along + (3.0 * kick) * pushed)
            )
            order = left_g * both(5 + k) + weight * (
                base_phi + 4.5 * carried * along + 3.0 * carried
            )
            for at, value in ((k, fluid), (5 + k, order)):
                to_left = jnp.where((lane >> 3) == at, turn(value, 8 * at), to_left)
                to_right = jnp.where(
                    (lane >> 3) == at, turn(value, (8 * at + LY // 2) % LY), to_right
                )
        return to_left, to_right

    def pass_faces(step):
        whole = units_of(step) >> 8
        wait_bytes(lands[step], recv_sem.at[0, step])
        tall = lanes((N_GY, LY))
        ends = jnp.zeros((N_GY, LY), jnp.float32)
        for j in range(5):
            line = shifted_line(lands[step][:, j, :], whole)
            r_slid[:, j, :] = line
            ends = jnp.where(
                (tall >> 2) == 2 * j,
                turn(rows_after(line), 8 * j) if j else rows_after(line),
                jnp.where((tall >> 2) == 2 * j + 1, turn(rows_before(line), 8 * j + 8), ends),
            )
        r_slid[:, 5, :] = ends

        def one(k, m):
            block = far_first(gy, k, m)
            send(r_slid.at[block], r_ghost.at[step, slot], 2, step, sec, block)

        def several(k, carry):
            for m in range(8):
                one(k, m)
            return carry

        lax.fori_loop(0, 7, several, 0)
        for m in range(7):
            one(7, m)
        pltpu.make_async_copy(
            r_slid.at[gy], r_ghost.at[step, slot], recv_sem.at[2, step]
        ).start()

    def stream_level(z, carry):
        for which in range(38):
            shift_x, shift_y, shift_z = VELOCITY[which % 19]
            if shift_y == 0:
                tile = post[which, (z - shift_z) & 7]
                if shift_x:
                    tile = pltpu.roll(tile, shift_x % LX, 0)
                state[which, z] = tile
        return carry

    def stream_along_y(z, carry):
        near_left, near_right = carry
        columns = {}
        for shift_z in (-1, 0, 1):
            source = (z - shift_z) & 7
            back = (LY - source) & (LY - 1)
            columns[1, shift_z] = turn(near_left, back)
            columns[-1, shift_z] = turn(near_right, back)
        for which in range(38):
            i = which % 19
            shift_x, shift_y, shift_z = VELOCITY[i]
            if shift_y == 0:
                continue
            tile = post[which, (z - shift_z) & 7]
            if shift_y == 1:
                k = Y_PLUS.index(i) + (5 if which >= 19 else 0)
                outer = turn(columns[1, shift_z], (LY - 8 * k) % LY)
                tile = jnp.where(lane == 0, outer, turn(tile, 1))
            else:
                k = Y_MINUS.index(i) + (5 if which >= 19 else 0)
                outer = turn(columns[-1, shift_z], (LY - 1 - 8 * k) % LY)
                tile = jnp.where(lane == LY - 1, outer, turn(tile, LY - 1))
            if shift_x:
                tile = pltpu.roll(tile, shift_x % LX, 0)
            state[which, z] = tile
        return carry

    def take_faces(step, side):
        members, (x, second, third, fourth), units, jump = (
            (UPWARD, (0, 1, 2, 3), offsets[step, sec], -1.0 * speeds[sec].astype(jnp.float32)),
            (
                DOWNWARD,
                (LX - 1, LX - 2, LX - 3, LX - 4),
                (SPAN - offsets[step, above]) & (SPAN - 1),
                speeds[above].astype(jnp.float32),
            ),
        )[side]
        jump = jump * (1.0 / 256.0)
        _, keep, frac = parts_of(units)
        first = ROLES * side

        def ordered(outer, inner):
            return (outer, inner) if side == 0 else (inner, outer)

        def unpacked(tile, crossed):
            ends = crossed
            for j in (1, 2, 3):
                ends = jnp.where(level == j, turn(crossed, LY - 8 * j), ends)
            return widened(tile, ends)

        def widened(tile, ends):
            ends = jnp.where(rim < 4, ends, jnp.where(rim >= LY - 4, turn(ends, LY - 8), 0.0))
            return jnp.concatenate([tile, ends], axis=1)

        def kind(k):
            if k == KINDS - 1:
                roles = pl.ds(first, NZ)
                return widened(
                    r_ghost[step, roles, 4, :], turn(r_ghost[step, roles, 5, :], LY - 32)
                )
            pair = r_ghost[step, pl.ds(first + 2 * k, 2), pl.ds(0, 4), :].reshape(NZ, LY)
            ends = [
                jnp.broadcast_to(r_ghost[step, first + 2 * k + j, pl.ds(5, 1), :], (4, LY))
                for j in range(2)
            ]
            return unpacked(pair, jnp.concatenate(ends, axis=0))

        kinds = [kind(k) for k in range(KINDS)]
        density, flow = kinds[10], kinds[11:14]
        beyond, beyond2, beyond3 = kinds[14:]
        own0, own1, own2, own3 = [field[:, 8 + at, :] for at in (x, second, third, fourth)]

        seen0 = keep * own0 + frac * turn(own0, 1)
        seen1 = keep * own1 + frac * turn(own1, 1)
        inner = potential_of(beyond2, beyond3, beyond)
        middle = potential_of(beyond, beyond2, seen0)
        outer = potential_of(seen0, beyond, seen1)
        low, high = ordered(inner, outer)
        layer = Layer(beyond, low, middle, high, density, flow)
        for k, i in enumerate(members):
            change = layer.change(i, jump)
            sent = (
                layer.fluid(i, kinds[k]) + density * change,
                layer.order(i, kinds[5 + k]) + beyond * change,
            )
            for lift, value in zip((0, 19), sent):
                ghost = keep * value + frac * turn(value, WIDE - 1)
                state[lift + i, :, x, :] = streamed(ghost, i)

        near = keep * beyond + frac * turn(beyond, WIDE - 1)
        far = keep * beyond2 + frac * turn(beyond2, WIDE - 1)
        pots = [
            potential_of(near, far, own0),
            potential_of(own0, near, own1),
            potential_of(own1, own0, own2),
            potential_of(own2, own1, own3),
        ]
        columns = [a_near[step, j, pl.ds(LX, NZ), :] for j in range(2)]
        for depth, (at, phi) in enumerate(((x, own0), (second, own1))):
            n = EDGES.index(at)

            def from_left(k):
                return turn(columns[0], LY - 1 - (32 * n + k))

            def from_right(k):
                return turn(columns[1], (LY - (32 * n + k)) % LY)

            def wide_moment(k):
                ends = jnp.where(rim == 0, from_right(10 + k), from_left(10 + k))
                return jnp.concatenate([mom[k, :, at, :], ends], axis=1)

            low, high = ordered(pots[depth], pots[depth + 2])
            layer = Layer(
                phi, low, pots[depth + 1], high, wide_moment(0), [wide_moment(k) for k in (1, 2, 3)]
            )
            for i in range(19):
                shift_x, shift_y, _ = VELOCITY[i]
                target = at + shift_x
                if target < 0 or target >= LX:
                    continue
                for lift, function, k in ((0, layer.fluid, 0), (19, layer.order, 5)):
                    tile = kept[lift + i, n]
                    if shift_y == 1:
                        ends = from_left(Y_PLUS.index(i) + k)
                    elif shift_y == -1:
                        ends = from_right(Y_MINUS.index(i) + k)
                    else:
                        ends = tile
                    value = function(i, jnp.concatenate([tile, ends], axis=1))
                    state[lift + i, :, target, :] = streamed(value, i)

    for step in range(STEPS):
        last = step == STEPS - 1
        send_faces(step)
        if step > 0:
            order_pass()
            moments()
            keep_edges()
            pack_columns()
        send_columns(step)
        put_columns(step)
        if step == 0:
            lax.fori_loop(0, NZ, potentials, 0)
            pass_faces(step)
        else:
            pass_faces(step)
            lax.fori_loop(0, NZ, potentials, 0)
        lax.fori_loop(0, NZ, collide, 0)
        lax.fori_loop(0, NZ, stream_level, 0)
        lax.fori_loop(0, NZ, stream_along_y, collide_beyond(step))

        wait_bytes(r_send, send_sem.at[0])
        wait_bytes(a_edge, send_sem.at[1])
        wait_bytes(r_ghost.at[step], recv_sem.at[2, step])
        for side in range(2):
            take_faces(step, side)
        if not last:
            prepare_faces()
            wait_bytes(r_slid.at[pl.ds(0, N_GY - 1)], send_sem.at[2])

    store_fluid = pltpu.make_async_copy(state.at[pl.ds(0, 19)], fluid_out, out_sem.at[0])
    store_order = pltpu.make_async_copy(state.at[pl.ds(19, 19)], order_out, out_sem.at[1])
    store_fluid.start()
    store_order.start()
    wait_bytes(r_slid.at[pl.ds(0, N_GY - 1)], send_sem.at[2])
    store_fluid.wait()
    store_order.wait()


def finish(fluid_in, order_in, fluid_out, order_out, held, in_sem, out_sem):
    loads, stores = [], []
    for start, size in ((0, 5), (5, 5), (10, 5), (15, 4)):
        for half, src, dst in ((0, fluid_in, fluid_out), (19, order_in, order_out)):
            k = len(loads)
            here = held.at[pl.ds(half + start, size)]
            cut = pl.ds(start, size)
            loads.append(pltpu.make_async_copy(src.at[cut], here, in_sem.at[k]))
            stores.append(pltpu.make_async_copy(here, dst.at[cut], out_sem.at[k]))
    for load in loads:
        load.start()
    for load, store in zip(loads, stores):
        load.wait()
        store.start()
    for store in stores:
        store.wait()


def per_device(fluid_dist, order_dist, plane_offset, plane_speed):
    shape = jax.ShapeDtypeStruct((19, NZ, LX, LY), jnp.float32)
    hbm = pl.BlockSpec(memory_space=pl.ANY)
    dma = pltpu.SemaphoreType.DMA

    def scratch(*dims):
        return pltpu.VMEM(dims, jnp.float32)

    results = pl.pallas_call(
        kernel,
        out_shape=(shape, shape),
        in_specs=[hbm] * 4,
        out_specs=(hbm, hbm),
        scratch_shapes=[
            pltpu.SMEM((STEPS, N_SEC), jnp.int32),
            pltpu.SMEM((N_SEC,), jnp.int32),
            scratch(38, NZ, LX, LY),
            scratch(38, NZ, LX, LY),
            scratch(NZ, 32, 2 * LY),
            scratch(NZ, 32, 2 * LY),
            scratch(4, NZ, LX, LY),
            scratch(38, 4, NZ, LY),
            scratch(2, 2 * LX + NZ, LY),
            scratch(STEPS, 2, 2 * LX + NZ, LY),
            scratch(2, ROLES, 5, LY),
            scratch(N_GY, 5, LY),
            scratch(N_GY, 5, LY),
            scratch(N_GY, 6, LY),
            scratch(STEPS, 2 * ROLES, 6, LY),
            dma((4,)),
            dma((2,)),
            dma((3,)),
            dma((3, STEPS)),
        ],
        compiler_params=pltpu.CompilerParams(
            collective_id=0, has_side_effects=True, vmem_limit_bytes=60 * 1024 * 1024
        ),
    )(fluid_dist, order_dist, plane_offset, plane_speed)
    return pl.pallas_call(
        finish,
        out_shape=(shape, shape),
        in_specs=[hbm] * 2,
        out_specs=(hbm, hbm),
        scratch_shapes=[scratch(38, NZ, LX, LY), dma((8,)), dma((8,))],
        compiler_params=pltpu.CompilerParams(vmem_limit_bytes=60 * 1024 * 1024),
    )(*results)


def solution(mesh):
    split = P(None, None, "sec", "gy")
    return jax.shard_map(
        per_device,
        mesh=mesh,
        in_specs=(split, split, P(), P()),
        out_specs=(split, split),
        check_vma=False,
    )
```

```python
import jax
import jax.numpy as jnp
from jax import lax
from jax.experimental import pallas as pl
from jax.experimental.pallas import tpu as pltpu
from jax.sharding import PartitionSpec as P

STEPS = 2
VELOCITY = (
    (0, 0, 0),
    (1, 0, 0),
    (-1, 0, 0),
    (0, 1, 0),
    (0, -1, 0),
    (0, 0, 1),
    (0, 0, -1),
    (1, 1, 0),
    (-1, -1, 0),
    (1, -1, 0),
    (-1, 1, 0),
    (1, 0, 1),
    (-1, 0, -1),
    (1, 0, -1),
    (-1, 0, 1),
    (0, 1, 1),
    (0, -1, -1),
    (0, 1, -1),
    (0, -1, 1),
)
WEIGHTS = (1.0 / 3.0,) + (1.0 / 18.0,) * 6 + (1.0 / 36.0,) * 12
UPWARD = (1, 7, 9, 11, 13)
DOWNWARD = (2, 8, 10, 12, 14)
Y_PLUS = (3, 7, 10, 15, 17)
Y_MINUS = (4, 8, 9, 16, 18)
COEF_A = -0.0625
COEF_B = 0.0625
KAPPA_GRAD = 0.04
MOBILITY = 1.0
TAU_FLUID = 0.8
TAU_ORDER = 0.9
NZ = 8
LX = 16
LY = 128
N_SEC = 4
N_GY = 64
SPAN = LY * N_GY * 256
ROLES = 32
KINDS = 17
WIDE = 2 * LY
EDGES = (0, 1, LX - 2, LX - 1)
MESH = pl.DeviceIdType.MESH
FAR_GROUPS = (6, 5, 7, 2, 4, 1, 3, 0)
ACROSS = ((1, 2), (1, 1), (1, 3), (0, 2), (1, 0), (0, 1), (0, 3), (0, 0))


def lanes(shape):
    return lax.broadcasted_iota(jnp.int32, shape, len(shape) - 1)


def turn(value, shift):
    return pltpu.roll(value, shift, value.ndim - 1)


def ring_z(gy, k):
    half = (k + 1) >> 1
    return ((gy >> 2) + 4 + jnp.where((k & 1) == 1, -half, half)) & 7


def far_first(gy, k, m):
    across, along = ACROSS[m]
    return (((gy >> 5) ^ across) << 5) + (ring_z(gy, k) << 2) + ((gy + along) & 3)


def signed_sum(terms, signs):
    total = None
    for term, sign in zip(terms, signs):
        if sign == 0:
            continue
        if total is None:
            total = term if sign > 0 else -term
        else:
            total = total + term if sign > 0 else total - term
    return total


def wait_bytes(ref, sem):
    pltpu.make_async_copy(ref, ref, sem).wait()


def parts_of(units):
    frac = (units & 255).astype(jnp.float32) * (1.0 / 256.0)
    return units >> 8, 1.0 - frac, frac


def rows_after(value):
    return pltpu.roll(value, N_GY - 1, 0)


def rows_before(value):
    return pltpu.roll(value, 1, 0)


def shifted_line(value, whole):
    inside = whole & (LY - 1)
    tile = lanes(value.shape)
    value = turn(value, (LY - inside) & (LY - 1))
    value = jnp.where(tile < LY - inside, value, rows_after(value))
    return pltpu.roll(value, (N_GY - (whole >> 7)) & (N_GY - 1), 0)


def potential_of(middle, one, other):
    lap = (
        one
        + other
        + turn(middle, 1)
        + turn(middle, WIDE - 1)
        + pltpu.roll(middle, 1, 0)
        + pltpu.roll(middle, NZ - 1, 0)
        - 6.0 * middle
    )
    return middle * (COEF_A + COEF_B * middle * middle) - KAPPA_GRAD * lap


LEFT_F = 1.0 - 1.0 / TAU_FLUID
LEFT_G = 1.0 - 1.0 / TAU_ORDER
KICK = 1.0 - 0.5 / TAU_FLUID


class Layer:
    def __init__(self, phi, low, middle, high, density, flow):
        half = -0.5 * phi
        self.phi, self.middle, self.density = phi, middle, density
        self.force = (
            half * (high - low),
            half * (turn(middle, WIDE - 1) - turn(middle, 1)),
            half * (pltpu.roll(middle, NZ - 1, 0) - pltpu.roll(middle, 1, 0)),
        )
        inverse = 1.0 / density
        self.vel = tuple((flow[k] + 0.5 * self.force[k]) * inverse for k in range(3))
        vel, force = self.vel, self.force
        self.square = vel[0] * vel[0] + vel[1] * vel[1] + vel[2] * vel[2]
        drift = vel[0] * force[0] + vel[1] * force[1] + vel[2] * force[2]
        self.scaled = density * (1.0 / TAU_FLUID)
        self.base = self.scaled * (1.0 - 1.5 * self.square) - (3.0 * KICK) * drift
        self.square_phi = phi * (1.0 / TAU_ORDER)
        self.base_phi = (
            3.0 * MOBILITY / TAU_ORDER
        ) * middle - 1.5 * self.square_phi * self.square

    def own(self):
        part = object.__new__(Layer)
        for name, value in vars(self).items():
            if isinstance(value, tuple):
                value = tuple(tile[:, :LY] for tile in value)
            else:
                value = value[:, :LY]
            setattr(part, name, value)
        return part

    def rest(self, fluid, order):
        return (
            LEFT_F * fluid + WEIGHTS[0] * self.base,
            LEFT_G * order
            + (
                self.square_phi * (1.0 - 0.5 * self.square)
                - (2.0 * MOBILITY / TAU_ORDER) * self.middle
            ),
        )

    def terms(self, i):
        along = signed_sum(self.vel, VELOCITY[i])
        pushed = signed_sum(self.force, VELOCITY[i])
        weight = WEIGHTS[i]
        dense = self.scaled * along
        carried = self.square_phi * along
        return (
            weight * (self.base + along * (4.5 * dense + (9.0 * KICK) * pushed)),
            weight * (3.0 * dense + (3.0 * KICK) * pushed),
            weight * (self.base_phi + 4.5 * carried * along),
            (3.0 * weight) * carried,
        )

    def change(self, i, jump):
        moved = self.vel[1] + jump
        along = signed_sum(self.vel, VELOCITY[i])
        after = signed_sum((self.vel[0], moved, self.vel[2]), VELOCITY[i])
        return WEIGHTS[i] * (
            3.0 * (after - along)
            + 4.5 * (after * after - along * along)
            - 1.5 * (moved * moved - self.vel[1] * self.vel[1])
        )


def streamed(tile, ends, i):
    _, shift_y, shift_z = VELOCITY[i]
    if shift_y:
        tile = next_to(tile, ends, -shift_y)
    if shift_z:
        tile = pltpu.roll(tile, shift_z % NZ, 0)
    return tile


def next_to(tile, ends, step):
    lane, shift = (LY - 1, LY - 1) if step == 1 else (0, 1)
    return jnp.where(lanes(tile.shape) == lane, turn(ends, shift), turn(tile, shift))


def kernel(
    fluid_in, order_in, offsets_in, speeds_in, fluid_out, order_out,
    offsets, speeds, state, post, field, pot, mom, kept,
    a_edge, a_near,
    r_send, r_land_0, r_land_1, r_slid, r_ghost, wide, pots,
    in_sem, out_sem, send_sem, recv_sem,
):
    lands = (r_land_0, r_land_1)
    sec = lax.axis_index("sec")
    gy = lax.axis_index("gy")
    above = (sec + 1) & (N_SEC - 1)
    below = (sec + N_SEC - 1) & (N_SEC - 1)
    left = (gy + N_GY - 1) & (N_GY - 1)
    right = (gy + 1) & (N_GY - 1)
    is_down = gy & 1
    slot = ROLES * (gy & 1) + (gy >> 1)
    load_order = pltpu.make_async_copy(order_in, state.at[pl.ds(19, 19)], in_sem.at[0])
    load_order.start()
    load_offsets = pltpu.make_async_copy(offsets_in, offsets, in_sem.at[2])
    load_offsets.start()
    load_speeds = pltpu.make_async_copy(speeds_in, speeds, in_sem.at[3])
    load_speeds.start()
    load_fluid = pltpu.make_async_copy(fluid_in, state.at[pl.ds(0, 19)], in_sem.at[1])
    load_fluid.start()

    barrier = pltpu.get_barrier_semaphore()
    source_sec = jnp.where(is_down == 0, below, above)

    def greet(k, carry):
        for m in range(8):
            other = far_first(gy, k, m)
            pl.semaphore_signal(
                barrier, inc=1, device_id=(source_sec, other), device_id_type=MESH
            )
            if m < 7:
                pl.semaphore_signal(barrier, inc=1, device_id=(sec, other), device_id_type=MESH)
        return carry

    def greet_rest(k, carry):
        pl.semaphore_signal(
            barrier, inc=1, device_id=(sec, far_first(gy, k, 7)), device_id_type=MESH
        )
        return carry

    lax.fori_loop(0, 8, greet, 0)
    lax.fori_loop(0, 7, greet_rest, 0)

    plane = (LX, LY)
    lane = lanes(plane)
    rim = lanes((NZ, LY))
    level = lax.broadcasted_iota(jnp.int32, (NZ, LY), 0) & 3
    field[...] = jnp.zeros_like(field)
    r_send[...] = jnp.zeros_like(r_send)

    def order_pass():
        def one(z, carry):
            phi = state[19, z]
            for i in range(1, 19):
                phi = phi + state[19 + i, z]
            field[z, pl.ds(8, LX), pl.ds(0, LY)] = phi
            return carry

        lax.fori_loop(0, NZ, one, 0)

    def prepare_faces():
        for side, members, x, inward in ((0, UPWARD, LX - 1, -1), (1, DOWNWARD, 0, 1)):
            fluid = [state[i, :, x, :] for i in range(19)]
            tiles = [fluid[i] for i in members] + [state[19 + i, :, x, :] for i in members]
            tiles.append(signed_sum(fluid, (1,) * 19))
            for axis in range(3):
                tiles.append(signed_sum(fluid, [vector[axis] for vector in VELOCITY]))
            for depth in range(3):
                layer = [state[19 + i, :, x + depth * inward, :] for i in range(19)]
                tiles.append(signed_sum(layer, (1,) * 19))
            for k in range(KINDS - 1):
                r_send[side, 2 * k, pl.ds(0, 4), :] = tiles[k][:4]
                r_send[side, 2 * k + 1, pl.ds(0, 4), :] = tiles[k][4:]
            for z in range(NZ):
                r_send[side, 4 * z, pl.ds(4, 1), :] = tiles[KINDS - 1][z : z + 1]

    def send_faces(step):
        for change in FAR_GROUPS:
            for place in range(4):
                role = 4 * ((gy >> 3) ^ change) + place
                rows = pl.ds(0, 5 if place == 0 else 4)
                land = lands[step].at[gy, rows]
                send(r_send.at[0, role, rows], land, 0, step, above, 2 * role)
                send(r_send.at[1, role, rows], land, 0, step, below, 2 * role + 1)

    def pack_columns():
        to_left = jnp.zeros(plane, jnp.float32)
        to_right = to_left
        for z in range(NZ):
            phi = field[z, pl.ds(8, LX), pl.ds(0, LY)]
            mine = (lane >> 2) == z
            to_left = jnp.where(mine, turn(phi, 4 * z), to_left)
            to_right = jnp.where(mine, turn(phi, 4 * z + 4), to_right)
        a_edge[0, pl.ds(0, LX), :] = to_left
        a_edge[1, pl.ds(0, LX), :] = to_right
        for side, rows in ((0, Y_MINUS), (1, Y_PLUS)):
            packed = jnp.zeros((NZ, LY), jnp.float32)
            for n, x in enumerate(EDGES):
                tiles = [kept[i, n] for i in rows] + [kept[19 + i, n] for i in rows]
                tiles += [mom[k, :, x, :] for k in range(4)]
                for k, tile in enumerate(tiles):
                    at = 32 * n + k
                    packed = jnp.where(rim == at, turn(tile, (at + side) % LY), packed)
            a_edge[side, pl.ds(LX, NZ), :] = packed

        def pack(z, carry):
            result = []
            for side, rows in ((0, Y_MINUS), (1, Y_PLUS)):
                tiles = [state[i, z] for i in rows] + [state[19 + i, z] for i in rows]
                tiles += [mom[k, z] for k in range(4)]
                going = jnp.zeros(plane, jnp.float32)
                for k, tile in enumerate(tiles):
                    going = jnp.where(lane == 8 * k, turn(tile, 8 * k + side), going)
                result.append(jnp.where((lane & 7) == z, turn(going, z), carry[side]))
            return tuple(result)

        zero = jnp.zeros(plane, jnp.float32)
        packed = lax.fori_loop(0, NZ, pack, (zero, zero))
        for side in range(2):
            a_edge[side, pl.ds(LX + NZ, LX), :] = packed[side]

    def keep_edges():
        for which in range(38):
            for n, x in enumerate(EDGES):
                kept[which, n] = state[which, :, x, :]

    def next_y(near, far):
        tile = lanes(near.shape)
        return jnp.where(tile == LY - 1, turn(far, LY - 1), turn(near, LY - 1))

    def last_y(near, far):
        tile = lanes(near.shape)
        return jnp.where(tile == 0, turn(far, 1), turn(near, 1))

    left_f, left_g, kick = LEFT_F, LEFT_G, KICK

    def send(src, dst, which, slot, to_sec, to_gy):
        pltpu.make_async_remote_copy(
            src_ref=src,
            dst_ref=dst,
            send_sem=send_sem.at[which],
            recv_sem=recv_sem.at[which, slot],
            device_id=(to_sec, to_gy),
            device_id_type=MESH,
        ).start()

    def moments():
        def one(z, carry):
            tiles = [state[i, z] for i in range(19)]
            mom[0, z] = signed_sum(tiles, (1,) * 19)
            for axis in range(3):
                mom[1 + axis, z] = signed_sum(tiles, [vector[axis] for vector in VELOCITY])
            return carry

        lax.fori_loop(0, NZ, one, 0)

    load_order.wait()
    order_pass()
    load_fluid.wait()
    prepare_faces()
    moments()
    keep_edges()
    pack_columns()
    load_offsets.wait()
    load_speeds.wait()
    pl.semaphore_wait(barrier, 2 * N_GY - 1)

    own = pl.ds(0, LY)
    halo = pl.ds(LY, LY)
    def units_of(step):
        return jnp.where(
            is_down == 0, offsets[step, sec], (SPAN - offsets[step, above]) & (SPAN - 1)
        )

    def send_columns(step):
        send(a_edge.at[0], a_near.at[step, 1], 1, step, sec, left)
        send(a_edge.at[1], a_near.at[step, 0], 1, step, sec, right)

    def put_columns(step):
        wait_bytes(a_near.at[step], recv_sem.at[1, step])
        from_left = a_near[step, 0, pl.ds(0, LX), :]
        from_right = a_near[step, 1, pl.ds(0, LX), :]

        def one(z, carry):
            field[z, pl.ds(8, LX), halo] = jnp.where(
                lane < 4,
                turn(from_right, (LY - 4 * z) & (LY - 1)),
                jnp.where(lane >= LY - 4, turn(from_left, (LY - 4 - 4 * z) & (LY - 1)), 0.0),
            )
            return carry

        lax.fori_loop(0, NZ, one, 0)

    def potentials(z, carry):
        tall = lanes((32, LY))
        tiles = [field[z, :, own], field[z, :, halo]]
        ahead = [turn(tile, LY - 1) for tile in tiles]
        behind = [turn(tile, 1) for tile in tiles]
        for k in range(2):
            tile = tiles[k]
            cut = pl.ds(k * LY, LY)
            lap = (
                pltpu.roll(tile, 1, 0)
                + pltpu.roll(tile, 31, 0)
                + jnp.where(tall == LY - 1, ahead[1 - k], ahead[k])
                + jnp.where(tall == 0, behind[1 - k], behind[k])
                + field[(z + 1) & 7, :, cut]
                + field[(z + 7) & 7, :, cut]
                - 6.0 * tile
            )
            pot[z, :, cut] = tile * (COEF_A + COEF_B * tile * tile) - KAPPA_GRAD * lap
        return carry

    def collide(z, carry):
        rows = pl.ds(8, LX)
        inner = pot[z, rows, own]
        beyond = pot[z, rows, halo]
        phi = field[z, rows, own]
        half = -0.5 * phi
        force = (
            half * (pot[z, pl.ds(9, LX), own] - pot[z, pl.ds(7, LX), own]),
            half * (next_y(inner, beyond) - last_y(inner, beyond)),
            half * (pot[(z + 1) & 7, rows, own] - pot[(z + 7) & 7, rows, own]),
        )
        density = mom[0, z]
        inverse = 1.0 / density
        vel = tuple((mom[1 + k, z] + 0.5 * force[k]) * inverse for k in range(3))
        square = vel[0] * vel[0] + vel[1] * vel[1] + vel[2] * vel[2]
        drift = vel[0] * force[0] + vel[1] * force[1] + vel[2] * force[2]
        scaled = density * (1.0 / TAU_FLUID)
        base = scaled * (1.0 - 1.5 * square) - (3.0 * kick) * drift
        square_phi = phi * (1.0 / TAU_ORDER)
        base_phi = (3.0 * MOBILITY / TAU_ORDER) * inner - 1.5 * square_phi * square
        fluid = [None] * 19
        order = [None] * 19
        fluid[0] = left_f * state[0, z] + WEIGHTS[0] * base
        order[0] = left_g * state[19, z] + (
            square_phi * (1.0 - 0.5 * square) - (2.0 * MOBILITY / TAU_ORDER) * inner
        )
        for i in range(1, 19, 2):
            vector = VELOCITY[i]
            along = signed_sum(vel, vector)
            pushed = signed_sum(force, vector)
            weight = WEIGHTS[i]
            even = weight * (base + along * (4.5 * scaled * along + (9.0 * kick) * pushed))
            odd = weight * (3.0 * scaled * along + (3.0 * kick) * pushed)
            fluid[i] = left_f * state[i, z] + (even + odd)
            fluid[i + 1] = left_f * state[i + 1, z] + (even - odd)
            carried = square_phi * along
            even = weight * (base_phi + 4.5 * carried * along)
            odd = (3.0 * weight) * carried
            order[i] = left_g * state[19 + i, z] + (even + odd)
            order[i + 1] = left_g * state[20 + i, z] + (even - odd)
        for i in range(19):
            post[i, z] = fluid[i]
            post[19 + i, z] = order[i]
        return carry

    def collide_beyond(step):
        from_left = a_near[step, 0, pl.ds(LX + NZ, LX), :]
        from_right = a_near[step, 1, pl.ds(LX + NZ, LX), :]
        at_left = lane < LY // 2

        def both(k):
            return jnp.where(
                at_left, turn(from_left, (LY - 8 * k) % LY), turn(from_right, (LY // 2 - 8 * k) % LY)
            )

        def gathered(left_tile, left_lane, right_tile, right_lane, height):
            result = jnp.zeros((height, LY), jnp.float32)
            tall = lanes((height, LY))
            for z in range(NZ):
                moved_left = turn(left_tile(z), (z - left_lane) % LY)
                moved_right = turn(right_tile(z), (LY // 2 + z - right_lane) % LY)
                result = jnp.where(
                    tall == z, moved_left, jnp.where(tall == LY // 2 + z, moved_right, result)
                )
            return result

        rows = pl.ds(8, LX)
        before = gathered(lambda z: pot[z, rows, halo], LY - 2, lambda z: pot[z, rows, own], LY - 1, LX)
        after = gathered(lambda z: pot[z, rows, own], 0, lambda z: pot[z, rows, halo], 1, LX)
        middle = gathered(lambda z: pot[z, :, halo], LY - 1, lambda z: pot[z, :, halo], 0, 32)
        phi = gathered(lambda z: field[z, rows, halo], LY - 1, lambda z: field[z, rows, halo], 0, LX)
        inner = middle[8:24]
        half = -0.5 * phi
        next_z = jnp.where((lane & 7) == 7, turn(inner, 7), turn(inner, LY - 1))
        last_z = jnp.where((lane & 7) == 0, turn(inner, LY - 7), turn(inner, 1))
        force = (half * (middle[9:25] - middle[7:23]), half * (after - before), half * (next_z - last_z))
        density = both(10)
        inverse = 1.0 / density
        vel = tuple((both(11 + k) + 0.5 * force[k]) * inverse for k in range(3))
        square = vel[0] * vel[0] + vel[1] * vel[1] + vel[2] * vel[2]
        drift = vel[0] * force[0] + vel[1] * force[1] + vel[2] * force[2]
        scaled = density * (1.0 / TAU_FLUID)
        base = scaled * (1.0 - 1.5 * square) - (3.0 * kick) * drift
        square_phi = phi * (1.0 / TAU_ORDER)
        base_phi = (3.0 * MOBILITY / TAU_ORDER) * inner - 1.5 * square_phi * square
        sign = jnp.where(at_left, 1.0, -1.0)
        to_left = jnp.zeros(plane, jnp.float32)
        to_right = to_left
        for k, i in enumerate(Y_PLUS):
            weight = WEIGHTS[i]
            along = sign * signed_sum(vel, VELOCITY[i])
            pushed = sign * signed_sum(force, VELOCITY[i])
            carried = square_phi * along
            fluid = left_f * both(k) + weight * (
                base
                + along * (4.5 * scaled * along + (9.0 * kick) * pushed)
                + (3.0 * scaled * along + (3.0 * kick) * pushed)
            )
            order = left_g * both(5 + k) + weight * (
                base_phi + 4.5 * carried * along + 3.0 * carried
            )
            for at, value in ((k, fluid), (5 + k, order)):
                to_left = jnp.where((lane >> 3) == at, turn(value, 8 * at), to_left)
                to_right = jnp.where(
                    (lane >> 3) == at, turn(value, (8 * at + LY // 2) % LY), to_right
                )
        return to_left, to_right

    def pass_faces(step):
        whole = units_of(step) >> 8
        has_extra = ((gy >> 1) & 3) == 0

        @pl.when(has_extra)
        def _():
            wait_bytes(lands[step], recv_sem.at[0, step])

        @pl.when(jnp.logical_not(has_extra))
        def _():
            wait_bytes(lands[step].at[:, pl.ds(0, 4)], recv_sem.at[0, step])

        tall = lanes((N_GY, LY))
        ends = jnp.zeros((N_GY, LY), jnp.float32)
        for j in range(5):
            line = shifted_line(lands[step][:, j, :], whole)
            r_slid[:, j if j < 4 else 5, :] = line
            ends = jnp.where(
                (tall >> 2) == 2 * j,
                turn(rows_after(line), 8 * j) if j else rows_after(line),
                jnp.where((tall >> 2) == 2 * j + 1, turn(rows_before(line), 8 * j + 8), ends),
            )
        r_slid[:, 4, :] = ends

        def pass_on(rows):
            def one(k, m):
                block = far_first(gy, k, m)
                send(r_slid.at[block, rows], r_ghost.at[step, slot, rows], 2, step, sec, block)

            def several(k, carry):
                for m in range(8):
                    one(k, m)
                return carry

            lax.fori_loop(0, 7, several, 0)
            for m in range(7):
                one(7, m)
            pltpu.make_async_copy(
                r_slid.at[gy, rows], r_ghost.at[step, slot, rows], recv_sem.at[2, step]
            ).start()

        @pl.when(has_extra)
        def _():
            pass_on(pl.ds(0, 6))

        @pl.when(jnp.logical_not(has_extra))
        def _():
            pass_on(pl.ds(0, 5))

    def stream_level(z, carry):
        for which in range(38):
            shift_x, shift_y, shift_z = VELOCITY[which % 19]
            if shift_y == 0:
                tile = post[which, (z - shift_z) & 7]
                if shift_x:
                    tile = pltpu.roll(tile, shift_x % LX, 0)
                state[which, z] = tile
        return carry

    def stream_along_y(z, carry):
        near_left, near_right = carry
        columns = {}
        for shift_z in (-1, 0, 1):
            source = (z - shift_z) & 7
            back = (LY - source) & (LY - 1)
            columns[1, shift_z] = turn(near_left, back)
            columns[-1, shift_z] = turn(near_right, back)
        for which in range(38):
            i = which % 19
            shift_x, shift_y, shift_z = VELOCITY[i]
            if shift_y == 0:
                continue
            tile = post[which, (z - shift_z) & 7]
            if shift_y == 1:
                k = Y_PLUS.index(i) + (5 if which >= 19 else 0)
                outer = turn(columns[1, shift_z], (LY - 8 * k) % LY)
                tile = jnp.where(lane == 0, outer, turn(tile, 1))
            else:
                k = Y_MINUS.index(i) + (5 if which >= 19 else 0)
                outer = turn(columns[-1, shift_z], (LY - 1 - 8 * k) % LY)
                tile = jnp.where(lane == LY - 1, outer, turn(tile, LY - 1))
            if shift_x:
                tile = pltpu.roll(tile, shift_x % LX, 0)
            state[which, z] = tile
        return carry

    def take_faces(step, side):
        members, (x, second, third, fourth), units, jump = (
            (UPWARD, (0, 1, 2, 3), offsets[step, sec], -1.0 * speeds[sec].astype(jnp.float32)),
            (
                DOWNWARD,
                (LX - 1, LX - 2, LX - 3, LX - 4),
                (SPAN - offsets[step, above]) & (SPAN - 1),
                speeds[above].astype(jnp.float32),
            ),
        )[side]
        jump = jump * (1.0 / 256.0)
        _, keep, frac = parts_of(units)
        first = ROLES * side

        def ordered(outer, inner):
            return (outer, inner) if side == 0 else (inner, outer)

        def unpacked(tile, crossed):
            ends = crossed
            for j in (1, 2, 3):
                ends = jnp.where(level == j, turn(crossed, LY - 8 * j), ends)
            return widened(tile, ends)

        def widened(tile, ends):
            ends = jnp.where(rim < 4, ends, jnp.where(rim >= LY - 4, turn(ends, LY - 8), 0.0))
            return jnp.concatenate([tile, ends], axis=1)

        def kind(k):
            if k == KINDS - 1:
                rows = [
                    jnp.concatenate(
                        [r_ghost[step, first + 4 * z, pl.ds(j, 1), :] for z in range(NZ)], axis=0
                    )
                    for j in (5, 4)
                ]
                return widened(rows[0], turn(rows[1], LY - 32))
            pair = r_ghost[step, pl.ds(first + 2 * k, 2), pl.ds(0, 4), :].reshape(NZ, LY)
            ends = [
                jnp.broadcast_to(r_ghost[step, first + 2 * k + j, pl.ds(4, 1), :], (4, LY))
                for j in range(2)
            ]
            return unpacked(pair, jnp.concatenate(ends, axis=0))

        @pl.when(gy >= 0)
        def _():
            for k in range(KINDS):
                wide[k] = kind(k)

        @pl.when(gy >= 0)
        def _():
            kinds = [wide[k] for k in range(KINDS)]
            density, flow = kinds[10], kinds[11:14]
            beyond, beyond2, beyond3 = kinds[14:]
            own0, own1 = [field[:, 8 + at, :] for at in (x, second)]

            seen0 = keep * own0 + frac * turn(own0, 1)
            seen1 = keep * own1 + frac * turn(own1, 1)
            inner = potential_of(beyond2, beyond3, beyond)
            middle = potential_of(beyond, beyond2, seen0)
            outer = potential_of(seen0, beyond, seen1)
            low, high = ordered(inner, outer)
            layer = Layer(beyond, low, middle, high, density, flow)
            for k, i in enumerate(members):
                change = layer.change(i, jump)
                even_f, odd_f, even_g, odd_g = layer.terms(i)
                sent = (
                    LEFT_F * kinds[k] + (even_f + odd_f) + density * change,
                    LEFT_G * kinds[5 + k] + (even_g + odd_g) + beyond * change,
                )
                for lift, value in zip((0, 19), sent):
                    if VELOCITY[i][1]:
                        ghost = keep * value + frac * turn(value, WIDE - 1)
                        tile, ends = ghost[:, :LY], ghost[:, LY:]
                    else:
                        tile, ends = value[:, :LY], value[:, LY:]
                        tile = keep * tile + frac * next_to(tile, ends, 1)
                    state[lift + i, :, x, :] = streamed(tile, ends, i)

        @pl.when(gy >= 0)
        def _():
            beyond, beyond2 = wide[14], wide[15]
            own0, own1, own2, own3 = [field[:, 8 + at, :] for at in (x, second, third, fourth)]
            near = keep * beyond + frac * turn(beyond, WIDE - 1)
            far = keep * beyond2 + frac * turn(beyond2, WIDE - 1)
            made = [
                potential_of(near, far, own0),
                potential_of(own0, near, own1),
                potential_of(own1, own0, own2),
                potential_of(own2, own1, own3),
            ]
            for k in range(4):
                pots[k] = made[k]

        for depth, at in enumerate((x, second)):

            @pl.when(gy >= 0)
            def _():
                columns = [a_near[step, j, pl.ds(LX, NZ), :] for j in range(2)]
                phi = field[:, 8 + at, :]
                n = EDGES.index(at)

                def from_left(k):
                    return turn(columns[0], LY - 1 - (32 * n + k))

                def from_right(k):
                    return turn(columns[1], (LY - (32 * n + k)) % LY)

                def wide_moment(k):
                    ends = jnp.where(rim == 0, from_right(10 + k), from_left(10 + k))
                    return jnp.concatenate([mom[k, :, at, :], ends], axis=1)

                low, high = ordered(pots[depth], pots[depth + 2])
                layer = Layer(
                    phi, low, pots[depth + 1], high, wide_moment(0), [wide_moment(k) for k in (1, 2, 3)]
                )
                narrow = layer.own()

                def put(which, target, tile, ends, i):
                    if 0 <= target < LX:
                        state[which, :, target, :] = streamed(tile, ends, i)

                fluid, order = narrow.rest(kept[0, n], kept[19, n])
                put(0, at, fluid, None, 0)
                put(19, at, order, None, 0)
                for i in range(1, 19, 2):
                    shift_x, shift_y, _ = VELOCITY[i]
                    even_f, odd_f, even_g, odd_g = (layer if shift_y else narrow).terms(i)
                    for sign, member in ((1, i), (-1, i + 1)):
                        target = at + sign * shift_x
                        if target < 0 or target >= LX:
                            continue
                        for lift, left, even, odd, k in (
                            (0, LEFT_F, even_f, odd_f, 0),
                            (19, LEFT_G, even_g, odd_g, 5),
                        ):
                            gain = even + odd if sign == 1 else even - odd
                            tile = left * kept[lift + member, n] + gain[:, :LY]
                            ends = None
                            if sign * shift_y == 1:
                                ends = left * from_left(Y_PLUS.index(member) + k) + gain[:, LY:]
                            elif sign * shift_y == -1:
                                ends = left * from_right(Y_MINUS.index(member) + k) + gain[:, LY:]
                            put(lift + member, target, tile, ends, member)

    def wait_slid():
        has_extra = ((gy >> 1) & 3) == 0

        @pl.when(has_extra)
        def _():
            wait_bytes(r_slid.at[pl.ds(0, N_GY - 1)], send_sem.at[2])

        @pl.when(jnp.logical_not(has_extra))
        def _():
            wait_bytes(r_slid.at[pl.ds(0, N_GY - 1), pl.ds(0, 5)], send_sem.at[2])

    for step in range(STEPS):
        last = step == STEPS - 1
        send_faces(step)
        if step > 0:
            order_pass()
            moments()
            keep_edges()
            pack_columns()
        send_columns(step)
        put_columns(step)
        if step == 0:
            lax.fori_loop(0, NZ, potentials, 0)
            pass_faces(step)
        else:
            pass_faces(step)
            lax.fori_loop(0, NZ, potentials, 0)
        lax.fori_loop(0, NZ, collide, 0)
        lax.fori_loop(0, NZ, stream_level, 0)
        lax.fori_loop(0, NZ, stream_along_y, collide_beyond(step))

        wait_bytes(r_send.at[:, :, pl.ds(0, 4)], send_sem.at[0])
        wait_bytes(r_send.at[:, pl.ds(0, NZ), 4], send_sem.at[0])
        wait_bytes(a_edge, send_sem.at[1])
        wait_bytes(r_ghost.at[step, pl.ds(0, 56)], recv_sem.at[2, step])
        for side in range(2):
            take_faces(step, side)
        if not last:
            prepare_faces()
            wait_slid()

    store_fluid = pltpu.make_async_copy(state.at[pl.ds(0, 19)], fluid_out, out_sem.at[0])
    store_order = pltpu.make_async_copy(state.at[pl.ds(19, 19)], order_out, out_sem.at[1])
    store_fluid.start()
    store_order.start()
    wait_slid()
    store_fluid.wait()
    store_order.wait()


def finish(fluid_in, order_in, fluid_out, order_out, held, in_sem, out_sem):
    loads, stores = [], []
    for start, size in ((0, 5), (5, 5), (10, 5), (15, 4)):
        for half, src, dst in ((0, fluid_in, fluid_out), (19, order_in, order_out)):
            k = len(loads)
            here = held.at[pl.ds(half + start, size)]
            cut = pl.ds(start, size)
            loads.append(pltpu.make_async_copy(src.at[cut], here, in_sem.at[k]))
            stores.append(pltpu.make_async_copy(here, dst.at[cut], out_sem.at[k]))
    for load in loads:
        load.start()
    for load, store in zip(loads, stores):
        load.wait()
        store.start()
    for store in stores:
        store.wait()


def per_device(fluid_dist, order_dist, plane_offset, plane_speed):
    shape = jax.ShapeDtypeStruct((19, NZ, LX, LY), jnp.float32)
    hbm = pl.BlockSpec(memory_space=pl.ANY)
    dma = pltpu.SemaphoreType.DMA

    def scratch(*dims):
        return pltpu.VMEM(dims, jnp.float32)

    results = pl.pallas_call(
        kernel,
        out_shape=(shape, shape),
        in_specs=[hbm] * 4,
        out_specs=(hbm, hbm),
        scratch_shapes=[
            pltpu.SMEM((STEPS, N_SEC), jnp.int32),
            pltpu.SMEM((N_SEC,), jnp.int32),
            scratch(38, NZ, LX, LY),
            scratch(38, NZ, LX, LY),
            scratch(NZ, 32, 2 * LY),
            scratch(NZ, 32, 2 * LY),
            scratch(4, NZ, LX, LY),
            scratch(38, 4, NZ, LY),
            scratch(2, 2 * LX + NZ, LY),
            scratch(STEPS, 2, 2 * LX + NZ, LY),
            scratch(2, ROLES, 5, LY),
            scratch(N_GY, 5, LY),
            scratch(N_GY, 5, LY),
            scratch(N_GY, 6, LY),
            scratch(STEPS, 2 * ROLES, 6, LY),
            scratch(KINDS, NZ, WIDE),
            scratch(4, NZ, WIDE),
            dma((4,)),
            dma((2,)),
            dma((3,)),
            dma((3, STEPS)),
        ],
        compiler_params=pltpu.CompilerParams(
            collective_id=0, has_side_effects=True, vmem_limit_bytes=60 * 1024 * 1024
        ),
    )(fluid_dist, order_dist, plane_offset, plane_speed)
    return pl.pallas_call(
        finish,
        out_shape=(shape, shape),
        in_specs=[hbm] * 2,
        out_specs=(hbm, hbm),
        scratch_shapes=[scratch(38, NZ, LX, LY), dma((8,)), dma((8,))],
        compiler_params=pltpu.CompilerParams(vmem_limit_bytes=60 * 1024 * 1024),
    )(*results)


def solution(mesh):
    split = P(None, None, "sec", "gy")
    return jax.shard_map(
        per_device,
        mesh=mesh,
        in_specs=(split, split, P(), P()),
        out_specs=(split, split),
        check_vma=False,
    )
```

```python
import jax
import jax.numpy as jnp
from jax import lax
from jax.experimental import pallas as pl
from jax.experimental.pallas import tpu as pltpu
from jax.sharding import PartitionSpec as P

STEPS = 2
VELOCITY = (
    (0, 0, 0),
    (1, 0, 0),
    (-1, 0, 0),
    (0, 1, 0),
    (0, -1, 0),
    (0, 0, 1),
    (0, 0, -1),
    (1, 1, 0),
    (-1, -1, 0),
    (1, -1, 0),
    (-1, 1, 0),
    (1, 0, 1),
    (-1, 0, -1),
    (1, 0, -1),
    (-1, 0, 1),
    (0, 1, 1),
    (0, -1, -1),
    (0, 1, -1),
    (0, -1, 1),
)
WEIGHTS = (1.0 / 3.0,) + (1.0 / 18.0,) * 6 + (1.0 / 36.0,) * 12
UPWARD = (1, 7, 9, 11, 13)
DOWNWARD = (2, 8, 10, 12, 14)
Y_PLUS = (3, 7, 10, 15, 17)
Y_MINUS = (4, 8, 9, 16, 18)
COEF_A = -0.0625
COEF_B = 0.0625
KAPPA_GRAD = 0.04
MOBILITY = 1.0
TAU_FLUID = 0.8
TAU_ORDER = 0.9
NZ = 8
LX = 16
LY = 128
N_SEC = 4
N_GY = 64
SPAN = LY * N_GY * 256
ROLES = 32
KINDS = 17
WIDE = 2 * LY
EDGES = (0, 1, LX - 2, LX - 1)
MESH = pl.DeviceIdType.MESH
FAR_GROUPS = (6, 5, 7, 2, 4, 1, 3, 0)
ACROSS = ((1, 2), (1, 1), (1, 3), (0, 2), (1, 0), (0, 1), (0, 3), (0, 0))


def lanes(shape):
    return lax.broadcasted_iota(jnp.int32, shape, len(shape) - 1)


def turn(value, shift):
    return pltpu.roll(value, shift, value.ndim - 1)


def ring_z(gy, k):
    half = (k + 1) >> 1
    return ((gy >> 2) + 4 + jnp.where((k & 1) == 1, -half, half)) & 7


def far_first(gy, k, m):
    across, along = ACROSS[m]
    return (((gy >> 5) ^ across) << 5) + (ring_z(gy, k) << 2) + ((gy + along) & 3)


def signed_sum(terms, signs):
    total = None
    for term, sign in zip(terms, signs):
        if sign == 0:
            continue
        if total is None:
            total = term if sign > 0 else -term
        else:
            total = total + term if sign > 0 else total - term
    return total


def wait_bytes(ref, sem):
    pltpu.make_async_copy(ref, ref, sem).wait()


def parts_of(units):
    frac = (units & 255).astype(jnp.float32) * (1.0 / 256.0)
    return units >> 8, 1.0 - frac, frac


def rows_after(value):
    return pltpu.roll(value, N_GY - 1, 0)


def rows_before(value):
    return pltpu.roll(value, 1, 0)


def shifted_line(value, whole):
    inside = whole & (LY - 1)
    tile = lanes(value.shape)
    value = turn(value, (LY - inside) & (LY - 1))
    value = jnp.where(tile < LY - inside, value, rows_after(value))
    return pltpu.roll(value, (N_GY - (whole >> 7)) & (N_GY - 1), 0)


def potential_of(middle, one, other):
    lap = (
        one
        + other
        + turn(middle, 1)
        + turn(middle, WIDE - 1)
        + pltpu.roll(middle, 1, 0)
        + pltpu.roll(middle, NZ - 1, 0)
        - 6.0 * middle
    )
    return middle * (COEF_A + COEF_B * middle * middle) - KAPPA_GRAD * lap


LEFT_F = 1.0 - 1.0 / TAU_FLUID
LEFT_G = 1.0 - 1.0 / TAU_ORDER
KICK = 1.0 - 0.5 / TAU_FLUID


class Layer:
    def __init__(self, phi, low, middle, high, density, flow):
        half = -0.5 * phi
        self.phi, self.middle, self.density = phi, middle, density
        self.force = (
            half * (high - low),
            half * (turn(middle, WIDE - 1) - turn(middle, 1)),
            half * (pltpu.roll(middle, NZ - 1, 0) - pltpu.roll(middle, 1, 0)),
        )
        inverse = 1.0 / density
        self.vel = tuple((flow[k] + 0.5 * self.force[k]) * inverse for k in range(3))
        vel, force = self.vel, self.force
        self.square = vel[0] * vel[0] + vel[1] * vel[1] + vel[2] * vel[2]
        drift = vel[0] * force[0] + vel[1] * force[1] + vel[2] * force[2]
        self.scaled = density * (1.0 / TAU_FLUID)
        self.base = self.scaled * (1.0 - 1.5 * self.square) - (3.0 * KICK) * drift
        self.square_phi = phi * (1.0 / TAU_ORDER)
        self.base_phi = (
            3.0 * MOBILITY / TAU_ORDER
        ) * middle - 1.5 * self.square_phi * self.square

    def save(self, ref):
        tiles = (self.phi, self.middle, self.density, self.square, self.scaled, self.base)
        tiles += (self.square_phi, self.base_phi) + self.force + self.vel
        for k, tile in enumerate(tiles):
            ref[k] = tile

    @staticmethod
    def saved(ref, columns):
        part = object.__new__(Layer)
        tiles = [ref[k, :, columns] for k in range(14)]
        part.phi, part.middle, part.density, part.square, part.scaled, part.base = tiles[:6]
        part.square_phi, part.base_phi = tiles[6:8]
        part.force, part.vel = tuple(tiles[8:11]), tuple(tiles[11:])
        return part

    def rest(self, fluid, order):
        return (
            LEFT_F * fluid + WEIGHTS[0] * self.base,
            LEFT_G * order
            + (
                self.square_phi * (1.0 - 0.5 * self.square)
                - (2.0 * MOBILITY / TAU_ORDER) * self.middle
            ),
        )

    def terms(self, i):
        along = signed_sum(self.vel, VELOCITY[i])
        pushed = signed_sum(self.force, VELOCITY[i])
        weight = WEIGHTS[i]
        dense = self.scaled * along
        carried = self.square_phi * along
        return (
            weight * (self.base + along * (4.5 * dense + (9.0 * KICK) * pushed)),
            weight * (3.0 * dense + (3.0 * KICK) * pushed),
            weight * (self.base_phi + 4.5 * carried * along),
            (3.0 * weight) * carried,
        )

    def change(self, i, jump):
        moved = self.vel[1] + jump
        along = signed_sum(self.vel, VELOCITY[i])
        after = signed_sum((self.vel[0], moved, self.vel[2]), VELOCITY[i])
        return WEIGHTS[i] * (
            3.0 * (after - along)
            + 4.5 * (after * after - along * along)
            - 1.5 * (moved * moved - self.vel[1] * self.vel[1])
        )


def streamed(tile, ends, i):
    _, shift_y, shift_z = VELOCITY[i]
    if shift_y:
        tile = next_to(tile, ends, -shift_y)
    if shift_z:
        tile = pltpu.roll(tile, shift_z % NZ, 0)
    return tile


def next_to(tile, ends, step):
    lane, shift = (LY - 1, LY - 1) if step == 1 else (0, 1)
    return jnp.where(lanes(tile.shape) == lane, turn(ends, shift), turn(tile, shift))


def kernel(
    fluid_in, order_in, offsets_in, speeds_in, fluid_out, order_out,
    offsets, speeds, state, post, field, pot, mom, kept,
    a_edge, a_near,
    r_send, r_land_0, r_land_1, r_slid, r_ghost, wide, pots, held,
    in_sem, out_sem, send_sem, recv_sem,
):
    lands = (r_land_0, r_land_1)
    sec = lax.axis_index("sec")
    gy = lax.axis_index("gy")
    above = (sec + 1) & (N_SEC - 1)
    below = (sec + N_SEC - 1) & (N_SEC - 1)
    left = (gy + N_GY - 1) & (N_GY - 1)
    right = (gy + 1) & (N_GY - 1)
    is_down = gy & 1
    slot = ROLES * (gy & 1) + (gy >> 1)
    load_order = pltpu.make_async_copy(order_in, state.at[pl.ds(19, 19)], in_sem.at[0])
    load_order.start()
    load_offsets = pltpu.make_async_copy(offsets_in, offsets, in_sem.at[2])
    load_offsets.start()
    load_speeds = pltpu.make_async_copy(speeds_in, speeds, in_sem.at[3])
    load_speeds.start()
    load_fluid = pltpu.make_async_copy(fluid_in, state.at[pl.ds(0, 19)], in_sem.at[1])
    load_fluid.start()

    barrier = pltpu.get_barrier_semaphore()
    source_sec = jnp.where(is_down == 0, below, above)

    def greet(k, carry):
        for m in range(8):
            other = far_first(gy, k, m)
            pl.semaphore_signal(
                barrier, inc=1, device_id=(source_sec, other), device_id_type=MESH
            )
            if m < 7:
                pl.semaphore_signal(barrier, inc=1, device_id=(sec, other), device_id_type=MESH)
        return carry

    def greet_rest(k, carry):
        pl.semaphore_signal(
            barrier, inc=1, device_id=(sec, far_first(gy, k, 7)), device_id_type=MESH
        )
        return carry

    lax.fori_loop(0, 8, greet, 0)
    lax.fori_loop(0, 7, greet_rest, 0)

    plane = (LX, LY)
    lane = lanes(plane)
    rim = lanes((NZ, LY))
    level = lax.broadcasted_iota(jnp.int32, (NZ, LY), 0) & 3
    field[...] = jnp.zeros_like(field)
    r_send[...] = jnp.zeros_like(r_send)

    def order_pass():
        def one(z, carry):
            phi = state[19, z]
            for i in range(1, 19):
                phi = phi + state[19 + i, z]
            field[z, pl.ds(8, LX), pl.ds(0, LY)] = phi
            return carry

        lax.fori_loop(0, NZ, one, 0)

    def prepare_faces():
        for side, members, x, inward in ((0, UPWARD, LX - 1, -1), (1, DOWNWARD, 0, 1)):
            fluid = [state[i, :, x, :] for i in range(19)]
            tiles = [fluid[i] for i in members] + [state[19 + i, :, x, :] for i in members]
            tiles.append(signed_sum(fluid, (1,) * 19))
            for axis in range(3):
                tiles.append(signed_sum(fluid, [vector[axis] for vector in VELOCITY]))
            for depth in range(3):
                layer = [state[19 + i, :, x + depth * inward, :] for i in range(19)]
                tiles.append(signed_sum(layer, (1,) * 19))
            for k in range(KINDS - 1):
                r_send[side, 2 * k, pl.ds(0, 4), :] = tiles[k][:4]
                r_send[side, 2 * k + 1, pl.ds(0, 4), :] = tiles[k][4:]
            for z in range(NZ):
                r_send[side, 4 * z, pl.ds(4, 1), :] = tiles[KINDS - 1][z : z + 1]

    def send_faces(step):
        for change in FAR_GROUPS:
            for place in range(4):
                role = 4 * ((gy >> 3) ^ change) + place
                rows = pl.ds(0, 5 if place == 0 else 4)
                land = lands[step].at[gy, rows]
                send(r_send.at[0, role, rows], land, 0, step, above, 2 * role)
                send(r_send.at[1, role, rows], land, 0, step, below, 2 * role + 1)

    def pack_columns():
        to_left = jnp.zeros(plane, jnp.float32)
        to_right = to_left
        for z in range(NZ):
            phi = field[z, pl.ds(8, LX), pl.ds(0, LY)]
            mine = (lane >> 2) == z
            to_left = jnp.where(mine, turn(phi, 4 * z), to_left)
            to_right = jnp.where(mine, turn(phi, 4 * z + 4), to_right)
        a_edge[0, pl.ds(0, LX), :] = to_left
        a_edge[1, pl.ds(0, LX), :] = to_right
        for side, rows in ((0, Y_MINUS), (1, Y_PLUS)):
            packed = jnp.zeros((NZ, LY), jnp.float32)
            for n, x in enumerate(EDGES):
                tiles = [kept[i, n] for i in rows] + [kept[19 + i, n] for i in rows]
                tiles += [mom[k, :, x, :] for k in range(4)]
                for k, tile in enumerate(tiles):
                    at = 32 * n + k
                    packed = jnp.where(rim == at, turn(tile, (at + side) % LY), packed)
            a_edge[side, pl.ds(LX, NZ), :] = packed

        def pack(z, carry):
            result = []
            for side, rows in ((0, Y_MINUS), (1, Y_PLUS)):
                tiles = [state[i, z] for i in rows] + [state[19 + i, z] for i in rows]
                tiles += [mom[k, z] for k in range(4)]
                going = jnp.zeros(plane, jnp.float32)
                for k, tile in enumerate(tiles):
                    going = jnp.where(lane == 8 * k, turn(tile, 8 * k + side), going)
                result.append(jnp.where((lane & 7) == z, turn(going, z), carry[side]))
            return tuple(result)

        zero = jnp.zeros(plane, jnp.float32)
        packed = lax.fori_loop(0, NZ, pack, (zero, zero))
        for side in range(2):
            a_edge[side, pl.ds(LX + NZ, LX), :] = packed[side]

    def keep_edges():
        for which in range(38):
            for n, x in enumerate(EDGES):
                kept[which, n] = state[which, :, x, :]

    def next_y(near, far):
        tile = lanes(near.shape)
        return jnp.where(tile == LY - 1, turn(far, LY - 1), turn(near, LY - 1))

    def last_y(near, far):
        tile = lanes(near.shape)
        return jnp.where(tile == 0, turn(far, 1), turn(near, 1))

    left_f, left_g, kick = LEFT_F, LEFT_G, KICK

    def send(src, dst, which, slot, to_sec, to_gy):
        pltpu.make_async_remote_copy(
            src_ref=src,
            dst_ref=dst,
            send_sem=send_sem.at[which],
            recv_sem=recv_sem.at[which, slot],
            device_id=(to_sec, to_gy),
            device_id_type=MESH,
        ).start()

    def moments():
        def one(z, carry):
            tiles = [state[i, z] for i in range(19)]
            mom[0, z] = signed_sum(tiles, (1,) * 19)
            for axis in range(3):
                mom[1 + axis, z] = signed_sum(tiles, [vector[axis] for vector in VELOCITY])
            return carry

        lax.fori_loop(0, NZ, one, 0)

    load_order.wait()
    order_pass()
    load_fluid.wait()
    prepare_faces()
    moments()
    keep_edges()
    pack_columns()
    load_offsets.wait()
    load_speeds.wait()
    pl.semaphore_wait(barrier, 2 * N_GY - 1)

    own = pl.ds(0, LY)
    halo = pl.ds(LY, LY)
    def units_of(step):
        return jnp.where(
            is_down == 0, offsets[step, sec], (SPAN - offsets[step, above]) & (SPAN - 1)
        )

    def send_columns(step):
        send(a_edge.at[0], a_near.at[step, 1], 1, step, sec, left)
        send(a_edge.at[1], a_near.at[step, 0], 1, step, sec, right)

    def put_columns(step):
        wait_bytes(a_near.at[step], recv_sem.at[1, step])
        from_left = a_near[step, 0, pl.ds(0, LX), :]
        from_right = a_near[step, 1, pl.ds(0, LX), :]

        def one(z, carry):
            field[z, pl.ds(8, LX), halo] = jnp.where(
                lane < 4,
                turn(from_right, (LY - 4 * z) & (LY - 1)),
                jnp.where(lane >= LY - 4, turn(from_left, (LY - 4 - 4 * z) & (LY - 1)), 0.0),
            )
            return carry

        lax.fori_loop(0, NZ, one, 0)

    def potentials(z, carry):
        tall = lanes((32, LY))
        tiles = [field[z, :, own], field[z, :, halo]]
        ahead = [turn(tile, LY - 1) for tile in tiles]
        behind = [turn(tile, 1) for tile in tiles]
        for k in range(2):
            tile = tiles[k]
            cut = pl.ds(k * LY, LY)
            lap = (
                pltpu.roll(tile, 1, 0)
                + pltpu.roll(tile, 31, 0)
                + jnp.where(tall == LY - 1, ahead[1 - k], ahead[k])
                + jnp.where(tall == 0, behind[1 - k], behind[k])
                + field[(z + 1) & 7, :, cut]
                + field[(z + 7) & 7, :, cut]
                - 6.0 * tile
            )
            pot[z, :, cut] = tile * (COEF_A + COEF_B * tile * tile) - KAPPA_GRAD * lap
        return carry

    def collide(z, carry):
        rows = pl.ds(8, LX)
        inner = pot[z, rows, own]
        beyond = pot[z, rows, halo]
        phi = field[z, rows, own]
        half = -0.5 * phi
        force = (
            half * (pot[z, pl.ds(9, LX), own] - pot[z, pl.ds(7, LX), own]),
            half * (next_y(inner, beyond) - last_y(inner, beyond)),
            half * (pot[(z + 1) & 7, rows, own] - pot[(z + 7) & 7, rows, own]),
        )
        density = mom[0, z]
        inverse = 1.0 / density
        vel = tuple((mom[1 + k, z] + 0.5 * force[k]) * inverse for k in range(3))
        square = vel[0] * vel[0] + vel[1] * vel[1] + vel[2] * vel[2]
        drift = vel[0] * force[0] + vel[1] * force[1] + vel[2] * force[2]
        scaled = density * (1.0 / TAU_FLUID)
        base = scaled * (1.0 - 1.5 * square) - (3.0 * kick) * drift
        square_phi = phi * (1.0 / TAU_ORDER)
        base_phi = (3.0 * MOBILITY / TAU_ORDER) * inner - 1.5 * square_phi * square
        fluid = [None] * 19
        order = [None] * 19
        fluid[0] = left_f * state[0, z] + WEIGHTS[0] * base
        order[0] = left_g * state[19, z] + (
            square_phi * (1.0 - 0.5 * square) - (2.0 * MOBILITY / TAU_ORDER) * inner
        )
        for i in range(1, 19, 2):
            vector = VELOCITY[i]
            along = signed_sum(vel, vector)
            pushed = signed_sum(force, vector)
            weight = WEIGHTS[i]
            even = weight * (base + along * (4.5 * scaled * along + (9.0 * kick) * pushed))
            odd = weight * (3.0 * scaled * along + (3.0 * kick) * pushed)
            fluid[i] = left_f * state[i, z] + (even + odd)
            fluid[i + 1] = left_f * state[i + 1, z] + (even - odd)
            carried = square_phi * along
            even = weight * (base_phi + 4.5 * carried * along)
            odd = (3.0 * weight) * carried
            order[i] = left_g * state[19 + i, z] + (even + odd)
            order[i + 1] = left_g * state[20 + i, z] + (even - odd)
        for i in range(19):
            post[i, z] = fluid[i]
            post[19 + i, z] = order[i]
        return carry

    def collide_beyond(step):
        from_left = a_near[step, 0, pl.ds(LX + NZ, LX), :]
        from_right = a_near[step, 1, pl.ds(LX + NZ, LX), :]
        at_left = lane < LY // 2

        def both(k):
            return jnp.where(
                at_left, turn(from_left, (LY - 8 * k) % LY), turn(from_right, (LY // 2 - 8 * k) % LY)
            )

        def gathered(left_tile, left_lane, right_tile, right_lane, height):
            result = jnp.zeros((height, LY), jnp.float32)
            tall = lanes((height, LY))
            for z in range(NZ):
                moved_left = turn(left_tile(z), (z - left_lane) % LY)
                moved_right = turn(right_tile(z), (LY // 2 + z - right_lane) % LY)
                result = jnp.where(
                    tall == z, moved_left, jnp.where(tall == LY // 2 + z, moved_right, result)
                )
            return result

        rows = pl.ds(8, LX)
        before = gathered(lambda z: pot[z, rows, halo], LY - 2, lambda z: pot[z, rows, own], LY - 1, LX)
        after = gathered(lambda z: pot[z, rows, own], 0, lambda z: pot[z, rows, halo], 1, LX)
        middle = gathered(lambda z: pot[z, :, halo], LY - 1, lambda z: pot[z, :, halo], 0, 32)
        phi = gathered(lambda z: field[z, rows, halo], LY - 1, lambda z: field[z, rows, halo], 0, LX)
        inner = middle[8:24]
        half = -0.5 * phi
        next_z = jnp.where((lane & 7) == 7, turn(inner, 7), turn(inner, LY - 1))
        last_z = jnp.where((lane & 7) == 0, turn(inner, LY - 7), turn(inner, 1))
        force = (half * (middle[9:25] - middle[7:23]), half * (after - before), half * (next_z - last_z))
        density = both(10)
        inverse = 1.0 / density
        vel = tuple((both(11 + k) + 0.5 * force[k]) * inverse for k in range(3))
        square = vel[0] * vel[0] + vel[1] * vel[1] + vel[2] * vel[2]
        drift = vel[0] * force[0] + vel[1] * force[1] + vel[2] * force[2]
        scaled = density * (1.0 / TAU_FLUID)
        base = scaled * (1.0 - 1.5 * square) - (3.0 * kick) * drift
        square_phi = phi * (1.0 / TAU_ORDER)
        base_phi = (3.0 * MOBILITY / TAU_ORDER) * inner - 1.5 * square_phi * square
        sign = jnp.where(at_left, 1.0, -1.0)
        to_left = jnp.zeros(plane, jnp.float32)
        to_right = to_left
        for k, i in enumerate(Y_PLUS):
            weight = WEIGHTS[i]
            along = sign * signed_sum(vel, VELOCITY[i])
            pushed = sign * signed_sum(force, VELOCITY[i])
            carried = square_phi * along
            fluid = left_f * both(k) + weight * (
                base
                + along * (4.5 * scaled * along + (9.0 * kick) * pushed)
                + (3.0 * scaled * along + (3.0 * kick) * pushed)
            )
            order = left_g * both(5 + k) + weight * (
                base_phi + 4.5 * carried * along + 3.0 * carried
            )
            for at, value in ((k, fluid), (5 + k, order)):
                to_left = jnp.where((lane >> 3) == at, turn(value, 8 * at), to_left)
                to_right = jnp.where(
                    (lane >> 3) == at, turn(value, (8 * at + LY // 2) % LY), to_right
                )
        return to_left, to_right

    def pass_faces(step):
        whole = units_of(step) >> 8
        has_extra = ((gy >> 1) & 3) == 0

        @pl.when(has_extra)
        def _():
            wait_bytes(lands[step], recv_sem.at[0, step])

        @pl.when(jnp.logical_not(has_extra))
        def _():
            wait_bytes(lands[step].at[:, pl.ds(0, 4)], recv_sem.at[0, step])

        tall = lanes((N_GY, LY))
        ends = jnp.zeros((N_GY, LY), jnp.float32)
        for j in range(5):
            line = shifted_line(lands[step][:, j, :], whole)
            r_slid[:, j if j < 4 else 5, :] = line
            ends = jnp.where(
                (tall >> 2) == 2 * j,
                turn(rows_after(line), 8 * j) if j else rows_after(line),
                jnp.where((tall >> 2) == 2 * j + 1, turn(rows_before(line), 8 * j + 8), ends),
            )
        r_slid[:, 4, :] = ends

        def pass_on(rows):
            def one(k, m):
                block = far_first(gy, k, m)
                send(r_slid.at[block, rows], r_ghost.at[step, slot, rows], 2, step, sec, block)

            def several(k, carry):
                for m in range(8):
                    one(k, m)
                return carry

            lax.fori_loop(0, 7, several, 0)
            for m in range(7):
                one(7, m)
            pltpu.make_async_copy(
                r_slid.at[gy, rows], r_ghost.at[step, slot, rows], recv_sem.at[2, step]
            ).start()

        @pl.when(has_extra)
        def _():
            pass_on(pl.ds(0, 6))

        @pl.when(jnp.logical_not(has_extra))
        def _():
            pass_on(pl.ds(0, 5))

    def stream_level(z, carry):
        for which in range(38):
            shift_x, shift_y, shift_z = VELOCITY[which % 19]
            if shift_y == 0:
                tile = post[which, (z - shift_z) & 7]
                if shift_x:
                    tile = pltpu.roll(tile, shift_x % LX, 0)
                state[which, z] = tile
        return carry

    def stream_along_y(z, carry):
        near_left, near_right = carry
        columns = {}
        for shift_z in (-1, 0, 1):
            source = (z - shift_z) & 7
            back = (LY - source) & (LY - 1)
            columns[1, shift_z] = turn(near_left, back)
            columns[-1, shift_z] = turn(near_right, back)
        for which in range(38):
            i = which % 19
            shift_x, shift_y, shift_z = VELOCITY[i]
            if shift_y == 0:
                continue
            tile = post[which, (z - shift_z) & 7]
            if shift_y == 1:
                k = Y_PLUS.index(i) + (5 if which >= 19 else 0)
                outer = turn(columns[1, shift_z], (LY - 8 * k) % LY)
                tile = jnp.where(lane == 0, outer, turn(tile, 1))
            else:
                k = Y_MINUS.index(i) + (5 if which >= 19 else 0)
                outer = turn(columns[-1, shift_z], (LY - 1 - 8 * k) % LY)
                tile = jnp.where(lane == LY - 1, outer, turn(tile, LY - 1))
            if shift_x:
                tile = pltpu.roll(tile, shift_x % LX, 0)
            state[which, z] = tile
        return carry

    def take_faces(step, side):
        members, (x, second, third, fourth), units, jump = (
            (UPWARD, (0, 1, 2, 3), offsets[step, sec], -1.0 * speeds[sec].astype(jnp.float32)),
            (
                DOWNWARD,
                (LX - 1, LX - 2, LX - 3, LX - 4),
                (SPAN - offsets[step, above]) & (SPAN - 1),
                speeds[above].astype(jnp.float32),
            ),
        )[side]
        jump = jump * (1.0 / 256.0)
        _, keep, frac = parts_of(units)
        first = ROLES * side

        def ordered(outer, inner):
            return (outer, inner) if side == 0 else (inner, outer)

        def unpacked(tile, crossed):
            ends = crossed
            for j in (1, 2, 3):
                ends = jnp.where(level == j, turn(crossed, LY - 8 * j), ends)
            return widened(tile, ends)

        def widened(tile, ends):
            ends = jnp.where(rim < 4, ends, jnp.where(rim >= LY - 4, turn(ends, LY - 8), 0.0))
            return jnp.concatenate([tile, ends], axis=1)

        def kind(k):
            if k == KINDS - 1:
                rows = [
                    jnp.concatenate(
                        [r_ghost[step, first + 4 * z, pl.ds(j, 1), :] for z in range(NZ)], axis=0
                    )
                    for j in (5, 4)
                ]
                return widened(rows[0], turn(rows[1], LY - 32))
            pair = r_ghost[step, pl.ds(first + 2 * k, 2), pl.ds(0, 4), :].reshape(NZ, LY)
            ends = [
                jnp.broadcast_to(r_ghost[step, first + 2 * k + j, pl.ds(4, 1), :], (4, LY))
                for j in range(2)
            ]
            return unpacked(pair, jnp.concatenate(ends, axis=0))

        @pl.when(gy >= 0)
        def _():
            for k in range(KINDS):
                wide[k] = kind(k)

        @pl.when(gy >= 0)
        def _():
            kinds = [wide[k] for k in range(KINDS)]
            density, flow = kinds[10], kinds[11:14]
            beyond, beyond2, beyond3 = kinds[14:]
            own0, own1 = [field[:, 8 + at, :] for at in (x, second)]

            seen0 = keep * own0 + frac * turn(own0, 1)
            seen1 = keep * own1 + frac * turn(own1, 1)
            inner = potential_of(beyond2, beyond3, beyond)
            middle = potential_of(beyond, beyond2, seen0)
            outer = potential_of(seen0, beyond, seen1)
            low, high = ordered(inner, outer)
            layer = Layer(beyond, low, middle, high, density, flow)
            for k, i in enumerate(members):
                change = layer.change(i, jump)
                even_f, odd_f, even_g, odd_g = layer.terms(i)
                sent = (
                    LEFT_F * kinds[k] + (even_f + odd_f) + density * change,
                    LEFT_G * kinds[5 + k] + (even_g + odd_g) + beyond * change,
                )
                for lift, value in zip((0, 19), sent):
                    if VELOCITY[i][1]:
                        ghost = keep * value + frac * turn(value, WIDE - 1)
                        tile, ends = ghost[:, :LY], ghost[:, LY:]
                    else:
                        tile, ends = value[:, :LY], value[:, LY:]
                        tile = keep * tile + frac * next_to(tile, ends, 1)
                    state[lift + i, :, x, :] = streamed(tile, ends, i)

        @pl.when(gy >= 0)
        def _():
            beyond, beyond2 = wide[14], wide[15]
            own0, own1, own2, own3 = [field[:, 8 + at, :] for at in (x, second, third, fourth)]
            near = keep * beyond + frac * turn(beyond, WIDE - 1)
            far = keep * beyond2 + frac * turn(beyond2, WIDE - 1)
            made = [
                potential_of(near, far, own0),
                potential_of(own0, near, own1),
                potential_of(own1, own0, own2),
                potential_of(own2, own1, own3),
            ]
            for k in range(4):
                pots[k] = made[k]

        for depth, at in enumerate((x, second)):

            @pl.when(gy >= 0)
            def _():
                columns = [a_near[step, j, pl.ds(LX, NZ), :] for j in range(2)]
                phi = field[:, 8 + at, :]
                n = EDGES.index(at)

                def from_left(k):
                    return turn(columns[0], LY - 1 - (32 * n + k))

                def from_right(k):
                    return turn(columns[1], (LY - (32 * n + k)) % LY)

                def wide_moment(k):
                    ends = jnp.where(rim == 0, from_right(10 + k), from_left(10 + k))
                    return jnp.concatenate([mom[k, :, at, :], ends], axis=1)

                low, high = ordered(pots[depth], pots[depth + 2])
                layer = Layer(
                    phi, low, pots[depth + 1], high, wide_moment(0), [wide_moment(k) for k in (1, 2, 3)]
                )
                layer.save(held)

            both = pl.ds(0, WIDE)
            for cut, pairs in (
                (own, (1, 5)), (own, (11, 13)), (both, (3, 7, 9)), (both, (15, 17))
            ):

                @pl.when(gy >= 0)
                def _():
                    layer = Layer.saved(held, cut)
                    columns = [a_near[step, j, pl.ds(LX, NZ), :] for j in range(2)]
                    n = EDGES.index(at)

                    def from_left(k):
                        return turn(columns[0], LY - 1 - (32 * n + k))

                    def from_right(k):
                        return turn(columns[1], (LY - (32 * n + k)) % LY)

                    def put(which, target, tile, ends, i):
                        if 0 <= target < LX:
                            state[which, :, target, :] = streamed(tile, ends, i)

                    if pairs[0] == 1:
                        fluid, order = layer.rest(kept[0, n], kept[19, n])
                        put(0, at, fluid, None, 0)
                        put(19, at, order, None, 0)
                    for i in pairs:
                        shift_x, shift_y, _ = VELOCITY[i]
                        even_f, odd_f, even_g, odd_g = layer.terms(i)
                        for sign, member in ((1, i), (-1, i + 1)):
                            target = at + sign * shift_x
                            if target < 0 or target >= LX:
                                continue
                            for lift, left, even, odd, k in (
                                (0, LEFT_F, even_f, odd_f, 0),
                                (19, LEFT_G, even_g, odd_g, 5),
                            ):
                                gain = even + odd if sign == 1 else even - odd
                                tile = left * kept[lift + member, n] + gain[:, :LY]
                                ends = None
                                if sign * shift_y == 1:
                                    ends = left * from_left(Y_PLUS.index(member) + k) + gain[:, LY:]
                                elif sign * shift_y == -1:
                                    ends = left * from_right(Y_MINUS.index(member) + k) + gain[:, LY:]
                                put(lift + member, target, tile, ends, member)

    def wait_slid():
        has_extra = ((gy >> 1) & 3) == 0

        @pl.when(has_extra)
        def _():
            wait_bytes(r_slid.at[pl.ds(0, N_GY - 1)], send_sem.at[2])

        @pl.when(jnp.logical_not(has_extra))
        def _():
            wait_bytes(r_slid.at[pl.ds(0, N_GY - 1), pl.ds(0, 5)], send_sem.at[2])

    stores = []
    for step in range(STEPS):
        last = step == STEPS - 1
        send_faces(step)
        if step > 0:
            order_pass()
            moments()
            keep_edges()
            pack_columns()
        send_columns(step)
        pass_faces(step)
        put_columns(step)
        lax.fori_loop(0, NZ, potentials, 0)
        lax.fori_loop(0, NZ, collide, 0)
        lax.fori_loop(0, NZ, stream_level, 0)
        lax.fori_loop(0, NZ, stream_along_y, collide_beyond(step))

        wait_bytes(r_send.at[:, :, pl.ds(0, 4)], send_sem.at[0])
        wait_bytes(r_send.at[:, pl.ds(0, NZ), 4], send_sem.at[0])
        wait_bytes(a_edge, send_sem.at[1])
        wait_bytes(r_ghost.at[step, pl.ds(0, 56)], recv_sem.at[2, step])
        for side in range(2):
            take_faces(step, side)
            if last:
                half = pl.ds(8 * side, 8)
                for k, (first, out) in enumerate(((0, fluid_out), (19, order_out))):
                    store = pltpu.make_async_copy(
                        state.at[pl.ds(first, 19), :, half], out.at[:, :, half], out_sem.at[k, side]
                    )
                    store.start()
                    stores.append(store)
        if not last:
            prepare_faces()
            wait_slid()

    wait_slid()
    for store in stores:
        store.wait()


def finish(fluid_in, order_in, fluid_out, order_out, held, in_sem, out_sem):
    loads, stores = [], []
    for start, size in ((0, 5), (5, 5), (10, 5), (15, 4)):
        for half, src, dst in ((0, fluid_in, fluid_out), (19, order_in, order_out)):
            k = len(loads)
            here = held.at[pl.ds(half + start, size)]
            cut = pl.ds(start, size)
            loads.append(pltpu.make_async_copy(src.at[cut], here, in_sem.at[k]))
            stores.append(pltpu.make_async_copy(here, dst.at[cut], out_sem.at[k]))
    for load in loads:
        load.start()
    for load, store in zip(loads, stores):
        load.wait()
        store.start()
    for store in stores:
        store.wait()


def per_device(fluid_dist, order_dist, plane_offset, plane_speed):
    shape = jax.ShapeDtypeStruct((19, NZ, LX, LY), jnp.float32)
    hbm = pl.BlockSpec(memory_space=pl.ANY)
    dma = pltpu.SemaphoreType.DMA

    def scratch(*dims):
        return pltpu.VMEM(dims, jnp.float32)

    results = pl.pallas_call(
        kernel,
        out_shape=(shape, shape),
        in_specs=[hbm] * 4,
        out_specs=(hbm, hbm),
        scratch_shapes=[
            pltpu.SMEM((STEPS, N_SEC), jnp.int32),
            pltpu.SMEM((N_SEC,), jnp.int32),
            scratch(38, NZ, LX, LY),
            scratch(38, NZ, LX, LY),
            scratch(NZ, 32, 2 * LY),
            scratch(NZ, 32, 2 * LY),
            scratch(4, NZ, LX, LY),
            scratch(38, 4, NZ, LY),
            scratch(2, 2 * LX + NZ, LY),
            scratch(STEPS, 2, 2 * LX + NZ, LY),
            scratch(2, ROLES, 5, LY),
            scratch(N_GY, 5, LY),
            scratch(N_GY, 5, LY),
            scratch(N_GY, 6, LY),
            scratch(STEPS, 2 * ROLES, 6, LY),
            scratch(KINDS, NZ, WIDE),
            scratch(4, NZ, WIDE),
            scratch(14, NZ, WIDE),
            dma((4,)),
            dma((2, 2)),
            dma((3,)),
            dma((3, STEPS)),
        ],
        compiler_params=pltpu.CompilerParams(
            collective_id=0, has_side_effects=True, vmem_limit_bytes=60 * 1024 * 1024
        ),
    )(fluid_dist, order_dist, plane_offset, plane_speed)
    return pl.pallas_call(
        finish,
        out_shape=(shape, shape),
        in_specs=[hbm] * 2,
        out_specs=(hbm, hbm),
        scratch_shapes=[scratch(38, NZ, LX, LY), dma((8,)), dma((8,))],
        compiler_params=pltpu.CompilerParams(vmem_limit_bytes=60 * 1024 * 1024),
    )(*results)


def solution(mesh):
    split = P(None, None, "sec", "gy")
    return jax.shard_map(
        per_device,
        mesh=mesh,
        in_specs=(split, split, P(), P()),
        out_specs=(split, split),
        check_vma=False,
    )
```

```python
import jax
import jax.numpy as jnp
from jax import lax
from jax.experimental import pallas as pl
from jax.experimental.pallas import tpu as pltpu
from jax.sharding import PartitionSpec as P

STEPS = 2
VELOCITY = (
    (0, 0, 0),
    (1, 0, 0),
    (-1, 0, 0),
    (0, 1, 0),
    (0, -1, 0),
    (0, 0, 1),
    (0, 0, -1),
    (1, 1, 0),
    (-1, -1, 0),
    (1, -1, 0),
    (-1, 1, 0),
    (1, 0, 1),
    (-1, 0, -1),
    (1, 0, -1),
    (-1, 0, 1),
    (0, 1, 1),
    (0, -1, -1),
    (0, 1, -1),
    (0, -1, 1),
)
WEIGHTS = (1.0 / 3.0,) + (1.0 / 18.0,) * 6 + (1.0 / 36.0,) * 12
UPWARD = (1, 7, 9, 11, 13)
DOWNWARD = (2, 8, 10, 12, 14)
Y_PLUS = (3, 7, 10, 15, 17)
Y_MINUS = (4, 8, 9, 16, 18)
COEF_A = -0.0625
COEF_B = 0.0625
KAPPA_GRAD = 0.04
MOBILITY = 1.0
TAU_FLUID = 0.8
TAU_ORDER = 0.9
NZ = 8
LX = 16
LY = 128
N_SEC = 4
N_GY = 64
SPAN = LY * N_GY * 256
ROLES = 32
KINDS = 17
WIDE = 2 * LY
EDGES = (0, 1, LX - 2, LX - 1)
MESH = pl.DeviceIdType.MESH
FAR_GROUPS = (6, 5, 7, 2, 4, 1, 3, 0)
ACROSS = ((1, 2), (1, 1), (1, 3), (0, 2), (1, 0), (0, 1), (0, 3), (0, 0))


def lanes(shape):
    return lax.broadcasted_iota(jnp.int32, shape, len(shape) - 1)


def turn(value, shift):
    return pltpu.roll(value, shift, value.ndim - 1)


def ring_z(gy, k):
    half = (k + 1) >> 1
    return ((gy >> 2) + 4 + jnp.where((k & 1) == 1, -half, half)) & 7


def far_first(gy, k, m):
    across, along = ACROSS[m]
    return (((gy >> 5) ^ across) << 5) + (ring_z(gy, k) << 2) + ((gy + along) & 3)


def signed_sum(terms, signs):
    total = None
    for term, sign in zip(terms, signs):
        if sign == 0:
            continue
        if total is None:
            total = term if sign > 0 else -term
        else:
            total = total + term if sign > 0 else total - term
    return total


def wait_bytes(ref, sem):
    pltpu.make_async_copy(ref, ref, sem).wait()


def parts_of(units):
    frac = (units & 255).astype(jnp.float32) * (1.0 / 256.0)
    return units >> 8, 1.0 - frac, frac


def rows_after(value):
    return pltpu.roll(value, N_GY - 1, 0)


def rows_before(value):
    return pltpu.roll(value, 1, 0)


def shifted_line(value, whole):
    inside = whole & (LY - 1)
    tile = lanes(value.shape)
    value = turn(value, (LY - inside) & (LY - 1))
    value = jnp.where(tile < LY - inside, value, rows_after(value))
    return pltpu.roll(value, (N_GY - (whole >> 7)) & (N_GY - 1), 0)


def potential_of(middle, one, other):
    lap = (
        one
        + other
        + turn(middle, 1)
        + turn(middle, WIDE - 1)
        + pltpu.roll(middle, 1, 0)
        + pltpu.roll(middle, NZ - 1, 0)
        - 6.0 * middle
    )
    return middle * (COEF_A + COEF_B * middle * middle) - KAPPA_GRAD * lap


LEFT_F = 1.0 - 1.0 / TAU_FLUID
LEFT_G = 1.0 - 1.0 / TAU_ORDER
KICK = 1.0 - 0.5 / TAU_FLUID


class Layer:
    def __init__(self, phi, low, middle, high, density, flow):
        half = -0.5 * phi
        self.phi, self.middle, self.density = phi, middle, density
        self.force = (
            half * (high - low),
            half * (turn(middle, WIDE - 1) - turn(middle, 1)),
            half * (pltpu.roll(middle, NZ - 1, 0) - pltpu.roll(middle, 1, 0)),
        )
        inverse = 1.0 / density
        self.vel = tuple((flow[k] + 0.5 * self.force[k]) * inverse for k in range(3))
        vel, force = self.vel, self.force
        self.square = vel[0] * vel[0] + vel[1] * vel[1] + vel[2] * vel[2]
        drift = vel[0] * force[0] + vel[1] * force[1] + vel[2] * force[2]
        self.scaled = density * (1.0 / TAU_FLUID)
        self.base = self.scaled * (1.0 - 1.5 * self.square) - (3.0 * KICK) * drift
        self.square_phi = phi * (1.0 / TAU_ORDER)
        self.base_phi = (
            3.0 * MOBILITY / TAU_ORDER
        ) * middle - 1.5 * self.square_phi * self.square

    def save(self, ref):
        tiles = (self.phi, self.middle, self.density, self.square, self.scaled, self.base)
        tiles += (self.square_phi, self.base_phi) + self.force + self.vel
        for k, tile in enumerate(tiles):
            ref[k] = tile

    @staticmethod
    def saved(ref, columns):
        part = object.__new__(Layer)
        tiles = [ref[k, :, columns] for k in range(14)]
        part.phi, part.middle, part.density, part.square, part.scaled, part.base = tiles[:6]
        part.square_phi, part.base_phi = tiles[6:8]
        part.force, part.vel = tuple(tiles[8:11]), tuple(tiles[11:])
        return part

    def rest(self, fluid, order):
        return (
            LEFT_F * fluid + WEIGHTS[0] * self.base,
            LEFT_G * order
            + (
                self.square_phi * (1.0 - 0.5 * self.square)
                - (2.0 * MOBILITY / TAU_ORDER) * self.middle
            ),
        )

    def terms(self, i):
        along = signed_sum(self.vel, VELOCITY[i])
        pushed = signed_sum(self.force, VELOCITY[i])
        weight = WEIGHTS[i]
        dense = self.scaled * along
        carried = self.square_phi * along
        return (
            weight * (self.base + along * (4.5 * dense + (9.0 * KICK) * pushed)),
            weight * (3.0 * dense + (3.0 * KICK) * pushed),
            weight * (self.base_phi + 4.5 * carried * along),
            (3.0 * weight) * carried,
        )

    def change(self, i, jump):
        moved = self.vel[1] + jump
        along = signed_sum(self.vel, VELOCITY[i])
        after = signed_sum((self.vel[0], moved, self.vel[2]), VELOCITY[i])
        return WEIGHTS[i] * (
            3.0 * (after - along)
            + 4.5 * (after * after - along * along)
            - 1.5 * (moved * moved - self.vel[1] * self.vel[1])
        )


def streamed(tile, ends, i):
    _, shift_y, shift_z = VELOCITY[i]
    if shift_y:
        tile = next_to(tile, ends, -shift_y)
    if shift_z:
        tile = pltpu.roll(tile, shift_z % NZ, 0)
    return tile


def next_to(tile, ends, step):
    lane, shift = (LY - 1, LY - 1) if step == 1 else (0, 1)
    return jnp.where(lanes(tile.shape) == lane, turn(ends, shift), turn(tile, shift))


def kernel(
    fluid_in, order_in, offsets_in, speeds_in, fluid_out, order_out,
    offsets, speeds, state, post, field, pot, mom, kept,
    a_edge, a_near,
    r_send, r_land_0, r_land_1, r_slid, r_ghost, wide, pots, held,
    in_sem, out_sem, send_sem, recv_sem,
):
    lands = (r_land_0, r_land_1)
    sec = lax.axis_index("sec")
    gy = lax.axis_index("gy")
    above = (sec + 1) & (N_SEC - 1)
    below = (sec + N_SEC - 1) & (N_SEC - 1)
    left = (gy + N_GY - 1) & (N_GY - 1)
    right = (gy + 1) & (N_GY - 1)
    is_down = gy & 1
    slot = ROLES * (gy & 1) + (gy >> 1)
    load_order = pltpu.make_async_copy(order_in, state.at[pl.ds(19, 19)], in_sem.at[0])
    load_order.start()
    load_offsets = pltpu.make_async_copy(offsets_in, offsets, in_sem.at[2])
    load_offsets.start()
    load_speeds = pltpu.make_async_copy(speeds_in, speeds, in_sem.at[3])
    load_speeds.start()
    load_fluid = pltpu.make_async_copy(fluid_in, state.at[pl.ds(0, 19)], in_sem.at[1])
    load_fluid.start()

    barrier = pltpu.get_barrier_semaphore()
    source_sec = jnp.where(is_down == 0, below, above)

    def greet(k, carry):
        for m in range(8):
            other = far_first(gy, k, m)
            pl.semaphore_signal(
                barrier, inc=1, device_id=(source_sec, other), device_id_type=MESH
            )
            if m < 7:
                pl.semaphore_signal(barrier, inc=1, device_id=(sec, other), device_id_type=MESH)
        return carry

    def greet_rest(k, carry):
        pl.semaphore_signal(
            barrier, inc=1, device_id=(sec, far_first(gy, k, 7)), device_id_type=MESH
        )
        return carry

    lax.fori_loop(0, 8, greet, 0)
    lax.fori_loop(0, 7, greet_rest, 0)

    plane = (LX, LY)
    lane = lanes(plane)
    rim = lanes((NZ, LY))
    level = lax.broadcasted_iota(jnp.int32, (NZ, LY), 0) & 3
    field[...] = jnp.zeros_like(field)
    r_send[...] = jnp.zeros_like(r_send)

    def order_pass():
        def one(z, carry):
            phi = state[19, z]
            for i in range(1, 19):
                phi = phi + state[19 + i, z]
            field[z, pl.ds(8, LX), pl.ds(0, LY)] = phi
            return carry

        lax.fori_loop(0, NZ, one, 0)

    def prepare_faces():
        for side, members, x, inward in ((0, UPWARD, LX - 1, -1), (1, DOWNWARD, 0, 1)):
            fluid = [state[i, :, x, :] for i in range(19)]
            tiles = [fluid[i] for i in members] + [state[19 + i, :, x, :] for i in members]
            tiles.append(signed_sum(fluid, (1,) * 19))
            for axis in range(3):
                tiles.append(signed_sum(fluid, [vector[axis] for vector in VELOCITY]))
            for depth in range(3):
                layer = [state[19 + i, :, x + depth * inward, :] for i in range(19)]
                tiles.append(signed_sum(layer, (1,) * 19))
            for k in range(KINDS - 1):
                r_send[side, 2 * k, pl.ds(0, 4), :] = tiles[k][:4]
                r_send[side, 2 * k + 1, pl.ds(0, 4), :] = tiles[k][4:]
            for z in range(NZ):
                r_send[side, 4 * z, pl.ds(4, 1), :] = tiles[KINDS - 1][z : z + 1]

    def send_faces(step):
        for change in FAR_GROUPS:
            for place in range(4):
                role = 4 * ((gy >> 3) ^ change) + place
                rows = pl.ds(0, 5 if place == 0 else 4)
                land = lands[step].at[gy, rows]
                send(r_send.at[0, role, rows], land, 0, step, above, 2 * role)
                send(r_send.at[1, role, rows], land, 0, step, below, 2 * role + 1)

    def pack_columns():
        to_left = jnp.zeros(plane, jnp.float32)
        to_right = to_left
        for z in range(NZ):
            phi = field[z, pl.ds(8, LX), pl.ds(0, LY)]
            mine = (lane >> 2) == z
            to_left = jnp.where(mine, turn(phi, 4 * z), to_left)
            to_right = jnp.where(mine, turn(phi, 4 * z + 4), to_right)
        a_edge[0, pl.ds(0, LX), :] = to_left
        a_edge[1, pl.ds(0, LX), :] = to_right
        for side, rows in ((0, Y_MINUS), (1, Y_PLUS)):
            packed = jnp.zeros((NZ, LY), jnp.float32)
            for n, x in enumerate(EDGES):
                tiles = [kept[i, n] for i in rows] + [kept[19 + i, n] for i in rows]
                tiles += [mom[k, :, x, :] for k in range(4)]
                for k, tile in enumerate(tiles):
                    at = 32 * n + k
                    packed = jnp.where(rim == at, turn(tile, (at + side) % LY), packed)
            a_edge[side, pl.ds(LX, NZ), :] = packed

        def pack(z, carry):
            result = []
            for side, rows in ((0, Y_MINUS), (1, Y_PLUS)):
                tiles = [state[i, z] for i in rows] + [state[19 + i, z] for i in rows]
                tiles += [mom[k, z] for k in range(4)]
                going = jnp.zeros(plane, jnp.float32)
                for k, tile in enumerate(tiles):
                    going = jnp.where(lane == 8 * k, turn(tile, 8 * k + side), going)
                result.append(jnp.where((lane & 7) == z, turn(going, z), carry[side]))
            return tuple(result)

        zero = jnp.zeros(plane, jnp.float32)
        packed = lax.fori_loop(0, NZ, pack, (zero, zero))
        for side in range(2):
            a_edge[side, pl.ds(LX + NZ, LX), :] = packed[side]

    def keep_edges():
        for which in range(38):
            for n, x in enumerate(EDGES):
                kept[which, n] = state[which, :, x, :]

    def next_y(near, far):
        tile = lanes(near.shape)
        return jnp.where(tile == LY - 1, turn(far, LY - 1), turn(near, LY - 1))

    def last_y(near, far):
        tile = lanes(near.shape)
        return jnp.where(tile == 0, turn(far, 1), turn(near, 1))

    left_f, left_g, kick = LEFT_F, LEFT_G, KICK

    def send(src, dst, which, slot, to_sec, to_gy, arrival=None):
        pltpu.make_async_remote_copy(
            src_ref=src,
            dst_ref=dst,
            send_sem=send_sem.at[which],
            recv_sem=recv_sem.at[which if arrival is None else arrival, slot],
            device_id=(to_sec, to_gy),
            device_id_type=MESH,
        ).start()

    def moments():
        def one(z, carry):
            tiles = [state[i, z] for i in range(19)]
            mom[0, z] = signed_sum(tiles, (1,) * 19)
            for axis in range(3):
                mom[1 + axis, z] = signed_sum(tiles, [vector[axis] for vector in VELOCITY])
            return carry

        lax.fori_loop(0, NZ, one, 0)

    load_order.wait()
    order_pass()
    load_fluid.wait()
    prepare_faces()
    moments()
    keep_edges()
    pack_columns()
    load_offsets.wait()
    load_speeds.wait()
    pl.semaphore_wait(barrier, 2 * N_GY - 1)

    own = pl.ds(0, LY)
    halo = pl.ds(LY, LY)
    def units_of(step):
        return jnp.where(
            is_down == 0, offsets[step, sec], (SPAN - offsets[step, above]) & (SPAN - 1)
        )

    def send_columns(step):
        send(a_edge.at[0], a_near.at[step, 1], 1, step, sec, left)
        send(a_edge.at[1], a_near.at[step, 0], 1, step, sec, right)

    def put_columns(step):
        wait_bytes(a_near.at[step], recv_sem.at[1, step])
        from_left = a_near[step, 0, pl.ds(0, LX), :]
        from_right = a_near[step, 1, pl.ds(0, LX), :]

        def one(z, carry):
            field[z, pl.ds(8, LX), halo] = jnp.where(
                lane < 4,
                turn(from_right, (LY - 4 * z) & (LY - 1)),
                jnp.where(lane >= LY - 4, turn(from_left, (LY - 4 - 4 * z) & (LY - 1)), 0.0),
            )
            return carry

        lax.fori_loop(0, NZ, one, 0)

    def potentials(z, carry):
        tall = lanes((32, LY))
        tiles = [field[z, :, own], field[z, :, halo]]
        ahead = [turn(tile, LY - 1) for tile in tiles]
        behind = [turn(tile, 1) for tile in tiles]
        for k in range(2):
            tile = tiles[k]
            cut = pl.ds(k * LY, LY)
            lap = (
                pltpu.roll(tile, 1, 0)
                + pltpu.roll(tile, 31, 0)
                + jnp.where(tall == LY - 1, ahead[1 - k], ahead[k])
                + jnp.where(tall == 0, behind[1 - k], behind[k])
                + field[(z + 1) & 7, :, cut]
                + field[(z + 7) & 7, :, cut]
                - 6.0 * tile
            )
            pot[z, :, cut] = tile * (COEF_A + COEF_B * tile * tile) - KAPPA_GRAD * lap
        return carry

    def collide(z, carry):
        rows = pl.ds(8, LX)
        inner = pot[z, rows, own]
        beyond = pot[z, rows, halo]
        phi = field[z, rows, own]
        half = -0.5 * phi
        force = (
            half * (pot[z, pl.ds(9, LX), own] - pot[z, pl.ds(7, LX), own]),
            half * (next_y(inner, beyond) - last_y(inner, beyond)),
            half * (pot[(z + 1) & 7, rows, own] - pot[(z + 7) & 7, rows, own]),
        )
        density = mom[0, z]
        inverse = 1.0 / density
        vel = tuple((mom[1 + k, z] + 0.5 * force[k]) * inverse for k in range(3))
        square = vel[0] * vel[0] + vel[1] * vel[1] + vel[2] * vel[2]
        drift = vel[0] * force[0] + vel[1] * force[1] + vel[2] * force[2]
        scaled = density * (1.0 / TAU_FLUID)
        base = scaled * (1.0 - 1.5 * square) - (3.0 * kick) * drift
        square_phi = phi * (1.0 / TAU_ORDER)
        base_phi = (3.0 * MOBILITY / TAU_ORDER) * inner - 1.5 * square_phi * square
        fluid = [None] * 19
        order = [None] * 19
        fluid[0] = left_f * state[0, z] + WEIGHTS[0] * base
        order[0] = left_g * state[19, z] + (
            square_phi * (1.0 - 0.5 * square) - (2.0 * MOBILITY / TAU_ORDER) * inner
        )
        for i in range(1, 19, 2):
            vector = VELOCITY[i]
            along = signed_sum(vel, vector)
            pushed = signed_sum(force, vector)
            weight = WEIGHTS[i]
            even = weight * (base + along * (4.5 * scaled * along + (9.0 * kick) * pushed))
            odd = weight * (3.0 * scaled * along + (3.0 * kick) * pushed)
            fluid[i] = left_f * state[i, z] + (even + odd)
            fluid[i + 1] = left_f * state[i + 1, z] + (even - odd)
            carried = square_phi * along
            even = weight * (base_phi + 4.5 * carried * along)
            odd = (3.0 * weight) * carried
            order[i] = left_g * state[19 + i, z] + (even + odd)
            order[i + 1] = left_g * state[20 + i, z] + (even - odd)
        for i in range(19):
            post[i, z] = fluid[i]
            post[19 + i, z] = order[i]
        return carry

    def collide_beyond(step):
        from_left = a_near[step, 0, pl.ds(LX + NZ, LX), :]
        from_right = a_near[step, 1, pl.ds(LX + NZ, LX), :]
        at_left = lane < LY // 2

        def both(k):
            return jnp.where(
                at_left, turn(from_left, (LY - 8 * k) % LY), turn(from_right, (LY // 2 - 8 * k) % LY)
            )

        def gathered(left_tile, left_lane, right_tile, right_lane, height):
            result = jnp.zeros((height, LY), jnp.float32)
            tall = lanes((height, LY))
            for z in range(NZ):
                moved_left = turn(left_tile(z), (z - left_lane) % LY)
                moved_right = turn(right_tile(z), (LY // 2 + z - right_lane) % LY)
                result = jnp.where(
                    tall == z, moved_left, jnp.where(tall == LY // 2 + z, moved_right, result)
                )
            return result

        rows = pl.ds(8, LX)
        before = gathered(lambda z: pot[z, rows, halo], LY - 2, lambda z: pot[z, rows, own], LY - 1, LX)
        after = gathered(lambda z: pot[z, rows, own], 0, lambda z: pot[z, rows, halo], 1, LX)
        middle = gathered(lambda z: pot[z, :, halo], LY - 1, lambda z: pot[z, :, halo], 0, 32)
        phi = gathered(lambda z: field[z, rows, halo], LY - 1, lambda z: field[z, rows, halo], 0, LX)
        inner = middle[8:24]
        half = -0.5 * phi
        next_z = jnp.where((lane & 7) == 7, turn(inner, 7), turn(inner, LY - 1))
        last_z = jnp.where((lane & 7) == 0, turn(inner, LY - 7), turn(inner, 1))
        force = (half * (middle[9:25] - middle[7:23]), half * (after - before), half * (next_z - last_z))
        density = both(10)
        inverse = 1.0 / density
        vel = tuple((both(11 + k) + 0.5 * force[k]) * inverse for k in range(3))
        square = vel[0] * vel[0] + vel[1] * vel[1] + vel[2] * vel[2]
        drift = vel[0] * force[0] + vel[1] * force[1] + vel[2] * force[2]
        scaled = density * (1.0 / TAU_FLUID)
        base = scaled * (1.0 - 1.5 * square) - (3.0 * kick) * drift
        square_phi = phi * (1.0 / TAU_ORDER)
        base_phi = (3.0 * MOBILITY / TAU_ORDER) * inner - 1.5 * square_phi * square
        sign = jnp.where(at_left, 1.0, -1.0)
        to_left = jnp.zeros(plane, jnp.float32)
        to_right = to_left
        for k, i in enumerate(Y_PLUS):
            weight = WEIGHTS[i]
            along = sign * signed_sum(vel, VELOCITY[i])
            pushed = sign * signed_sum(force, VELOCITY[i])
            carried = square_phi * along
            fluid = left_f * both(k) + weight * (
                base
                + along * (4.5 * scaled * along + (9.0 * kick) * pushed)
                + (3.0 * scaled * along + (3.0 * kick) * pushed)
            )
            order = left_g * both(5 + k) + weight * (
                base_phi + 4.5 * carried * along + 3.0 * carried
            )
            for at, value in ((k, fluid), (5 + k, order)):
                to_left = jnp.where((lane >> 3) == at, turn(value, 8 * at), to_left)
                to_right = jnp.where(
                    (lane >> 3) == at, turn(value, (8 * at + LY // 2) % LY), to_right
                )
        return to_left, to_right

    def pass_faces(step):
        whole = units_of(step) >> 8
        has_extra = ((gy >> 1) & 3) == 0

        @pl.when(has_extra)
        def _():
            wait_bytes(lands[step], recv_sem.at[0, step])

        @pl.when(jnp.logical_not(has_extra))
        def _():
            wait_bytes(lands[step].at[:, pl.ds(0, 4)], recv_sem.at[0, step])

        tall = lanes((N_GY, LY))
        ends = jnp.zeros((N_GY, LY), jnp.float32)
        for j in range(5):
            line = shifted_line(lands[step][:, j, :], whole)
            r_slid[:, j if j < 4 else 5, :] = line
            ends = jnp.where(
                (tall >> 2) == 2 * j,
                turn(rows_after(line), 8 * j) if j else rows_after(line),
                jnp.where((tall >> 2) == 2 * j + 1, turn(rows_before(line), 8 * j + 8), ends),
            )
        r_slid[:, 4, :] = ends

        arrival = 2 + is_down

        def pass_on(rows):
            def one(k, m):
                block = far_first(gy, k, m)
                send(
                    r_slid.at[block, rows], r_ghost.at[step, slot, rows], 2, step, sec, block, arrival
                )

            def several(k, carry):
                for m in range(8):
                    one(k, m)
                return carry

            lax.fori_loop(0, 7, several, 0)
            for m in range(7):
                one(7, m)
            pltpu.make_async_copy(
                r_slid.at[gy, rows], r_ghost.at[step, slot, rows], recv_sem.at[arrival, step]
            ).start()

        @pl.when(has_extra)
        def _():
            pass_on(pl.ds(0, 6))

        @pl.when(jnp.logical_not(has_extra))
        def _():
            pass_on(pl.ds(0, 5))

    def stream_level(z, carry):
        for which in range(38):
            shift_x, shift_y, shift_z = VELOCITY[which % 19]
            if shift_y == 0:
                tile = post[which, (z - shift_z) & 7]
                if shift_x:
                    tile = pltpu.roll(tile, shift_x % LX, 0)
                state[which, z] = tile
        return carry

    def stream_along_y(z, carry):
        near_left, near_right = carry
        columns = {}
        for shift_z in (-1, 0, 1):
            source = (z - shift_z) & 7
            back = (LY - source) & (LY - 1)
            columns[1, shift_z] = turn(near_left, back)
            columns[-1, shift_z] = turn(near_right, back)
        for which in range(38):
            i = which % 19
            shift_x, shift_y, shift_z = VELOCITY[i]
            if shift_y == 0:
                continue
            tile = post[which, (z - shift_z) & 7]
            if shift_y == 1:
                k = Y_PLUS.index(i) + (5 if which >= 19 else 0)
                outer = turn(columns[1, shift_z], (LY - 8 * k) % LY)
                tile = jnp.where(lane == 0, outer, turn(tile, 1))
            else:
                k = Y_MINUS.index(i) + (5 if which >= 19 else 0)
                outer = turn(columns[-1, shift_z], (LY - 1 - 8 * k) % LY)
                tile = jnp.where(lane == LY - 1, outer, turn(tile, LY - 1))
            if shift_x:
                tile = pltpu.roll(tile, shift_x % LX, 0)
            state[which, z] = tile
        return carry

    def take_faces(step, side):
        members, (x, second, third, fourth), units, jump = (
            (UPWARD, (0, 1, 2, 3), offsets[step, sec], -1.0 * speeds[sec].astype(jnp.float32)),
            (
                DOWNWARD,
                (LX - 1, LX - 2, LX - 3, LX - 4),
                (SPAN - offsets[step, above]) & (SPAN - 1),
                speeds[above].astype(jnp.float32),
            ),
        )[side]
        jump = jump * (1.0 / 256.0)
        _, keep, frac = parts_of(units)
        first = ROLES * side

        def ordered(outer, inner):
            return (outer, inner) if side == 0 else (inner, outer)

        def unpacked(tile, crossed):
            ends = crossed
            for j in (1, 2, 3):
                ends = jnp.where(level == j, turn(crossed, LY - 8 * j), ends)
            return widened(tile, ends)

        def widened(tile, ends):
            ends = jnp.where(rim < 4, ends, jnp.where(rim >= LY - 4, turn(ends, LY - 8), 0.0))
            return jnp.concatenate([tile, ends], axis=1)

        def kind(k):
            if k == KINDS - 1:
                rows = [
                    jnp.concatenate(
                        [r_ghost[step, first + 4 * z, pl.ds(j, 1), :] for z in range(NZ)], axis=0
                    )
                    for j in (5, 4)
                ]
                return widened(rows[0], turn(rows[1], LY - 32))
            pair = r_ghost[step, pl.ds(first + 2 * k, 2), pl.ds(0, 4), :].reshape(NZ, LY)
            ends = [
                jnp.broadcast_to(r_ghost[step, first + 2 * k + j, pl.ds(4, 1), :], (4, LY))
                for j in range(2)
            ]
            return unpacked(pair, jnp.concatenate(ends, axis=0))

        @pl.when(gy >= 0)
        def _():
            for k in range(KINDS):
                wide[k] = kind(k)

        @pl.when(gy >= 0)
        def _():
            kinds = [wide[k] for k in range(KINDS)]
            density, flow = kinds[10], kinds[11:14]
            beyond, beyond2, beyond3 = kinds[14:]
            own0, own1 = [field[:, 8 + at, :] for at in (x, second)]

            seen0 = keep * own0 + frac * turn(own0, 1)
            seen1 = keep * own1 + frac * turn(own1, 1)
            inner = potential_of(beyond2, beyond3, beyond)
            middle = potential_of(beyond, beyond2, seen0)
            outer = potential_of(seen0, beyond, seen1)
            low, high = ordered(inner, outer)
            layer = Layer(beyond, low, middle, high, density, flow)
            for k, i in enumerate(members):
                change = layer.change(i, jump)
                even_f, odd_f, even_g, odd_g = layer.terms(i)
                sent = (
                    LEFT_F * kinds[k] + (even_f + odd_f) + density * change,
                    LEFT_G * kinds[5 + k] + (even_g + odd_g) + beyond * change,
                )
                for lift, value in zip((0, 19), sent):
                    if VELOCITY[i][1]:
                        ghost = keep * value + frac * turn(value, WIDE - 1)
                        tile, ends = ghost[:, :LY], ghost[:, LY:]
                    else:
                        tile, ends = value[:, :LY], value[:, LY:]
                        tile = keep * tile + frac * next_to(tile, ends, 1)
                    state[lift + i, :, x, :] = streamed(tile, ends, i)

        @pl.when(gy >= 0)
        def _():
            beyond, beyond2 = wide[14], wide[15]
            own0, own1, own2, own3 = [field[:, 8 + at, :] for at in (x, second, third, fourth)]
            near = keep * beyond + frac * turn(beyond, WIDE - 1)
            far = keep * beyond2 + frac * turn(beyond2, WIDE - 1)
            made = [
                potential_of(near, far, own0),
                potential_of(own0, near, own1),
                potential_of(own1, own0, own2),
                potential_of(own2, own1, own3),
            ]
            for k in range(4):
                pots[k] = made[k]

        for depth, at in enumerate((x, second)):

            @pl.when(gy >= 0)
            def _():
                columns = [a_near[step, j, pl.ds(LX, NZ), :] for j in range(2)]
                phi = field[:, 8 + at, :]
                n = EDGES.index(at)

                def from_left(k):
                    return turn(columns[0], LY - 1 - (32 * n + k))

                def from_right(k):
                    return turn(columns[1], (LY - (32 * n + k)) % LY)

                def wide_moment(k):
                    ends = jnp.where(rim == 0, from_right(10 + k), from_left(10 + k))
                    return jnp.concatenate([mom[k, :, at, :], ends], axis=1)

                low, high = ordered(pots[depth], pots[depth + 2])
                layer = Layer(
                    phi, low, pots[depth + 1], high, wide_moment(0), [wide_moment(k) for k in (1, 2, 3)]
                )
                layer.save(held)

            both = pl.ds(0, WIDE)
            for cut, pairs in (
                (own, (1, 5)), (own, (11, 13)), (both, (3, 7, 9)), (both, (15, 17))
            ):

                @pl.when(gy >= 0)
                def _():
                    layer = Layer.saved(held, cut)
                    columns = [a_near[step, j, pl.ds(LX, NZ), :] for j in range(2)]
                    n = EDGES.index(at)

                    def from_left(k):
                        return turn(columns[0], LY - 1 - (32 * n + k))

                    def from_right(k):
                        return turn(columns[1], (LY - (32 * n + k)) % LY)

                    def put(which, target, tile, ends, i):
                        if 0 <= target < LX:
                            state[which, :, target, :] = streamed(tile, ends, i)

                    if pairs[0] == 1:
                        fluid, order = layer.rest(kept[0, n], kept[19, n])
                        put(0, at, fluid, None, 0)
                        put(19, at, order, None, 0)
                    for i in pairs:
                        shift_x, shift_y, _ = VELOCITY[i]
                        even_f, odd_f, even_g, odd_g = layer.terms(i)
                        for sign, member in ((1, i), (-1, i + 1)):
                            target = at + sign * shift_x
                            if target < 0 or target >= LX:
                                continue
                            for lift, left, even, odd, k in (
                                (0, LEFT_F, even_f, odd_f, 0),
                                (19, LEFT_G, even_g, odd_g, 5),
                            ):
                                gain = even + odd if sign == 1 else even - odd
                                tile = left * kept[lift + member, n] + gain[:, :LY]
                                ends = None
                                if sign * shift_y == 1:
                                    ends = left * from_left(Y_PLUS.index(member) + k) + gain[:, LY:]
                                elif sign * shift_y == -1:
                                    ends = left * from_right(Y_MINUS.index(member) + k) + gain[:, LY:]
                                put(lift + member, target, tile, ends, member)

    def wait_slid():
        has_extra = ((gy >> 1) & 3) == 0

        @pl.when(has_extra)
        def _():
            wait_bytes(r_slid.at[pl.ds(0, N_GY - 1)], send_sem.at[2])

        @pl.when(jnp.logical_not(has_extra))
        def _():
            wait_bytes(r_slid.at[pl.ds(0, N_GY - 1), pl.ds(0, 5)], send_sem.at[2])

    stores = []
    for step in range(STEPS):
        last = step == STEPS - 1
        send_faces(step)
        if step > 0:
            order_pass()
            moments()
            keep_edges()
            pack_columns()
        send_columns(step)
        pass_faces(step)
        put_columns(step)
        lax.fori_loop(0, NZ, potentials, 0)
        lax.fori_loop(0, NZ, collide, 0)
        lax.fori_loop(0, NZ, stream_level, 0)
        lax.fori_loop(0, NZ, stream_along_y, collide_beyond(step))

        wait_bytes(r_send.at[:, :, pl.ds(0, 4)], send_sem.at[0])
        wait_bytes(r_send.at[:, pl.ds(0, NZ), 4], send_sem.at[0])
        wait_bytes(a_edge, send_sem.at[1])
        for side in range(2):
            wait_bytes(r_ghost.at[step, pl.ds(ROLES * side, 28)], recv_sem.at[2 + side, step])
            take_faces(step, side)
            if last:
                half = pl.ds(8 * side, 8)
                for k, (first, out) in enumerate(((0, fluid_out), (19, order_out))):
                    store = pltpu.make_async_copy(
                        state.at[pl.ds(first, 19), :, half], out.at[:, :, half], out_sem.at[k, side]
                    )
                    store.start()
                    stores.append(store)
        if not last:
            prepare_faces()
            wait_slid()

    wait_slid()
    for store in stores:
        store.wait()


def finish(fluid_in, order_in, fluid_out, order_out, held, in_sem, out_sem):
    loads, stores = [], []
    for start, size in ((0, 5), (5, 5), (10, 5), (15, 4)):
        for half, src, dst in ((0, fluid_in, fluid_out), (19, order_in, order_out)):
            k = len(loads)
            here = held.at[pl.ds(half + start, size)]
            cut = pl.ds(start, size)
            loads.append(pltpu.make_async_copy(src.at[cut], here, in_sem.at[k]))
            stores.append(pltpu.make_async_copy(here, dst.at[cut], out_sem.at[k]))
    for load in loads:
        load.start()
    for load, store in zip(loads, stores):
        load.wait()
        store.start()
    for store in stores:
        store.wait()


def per_device(fluid_dist, order_dist, plane_offset, plane_speed):
    shape = jax.ShapeDtypeStruct((19, NZ, LX, LY), jnp.float32)
    hbm = pl.BlockSpec(memory_space=pl.ANY)
    dma = pltpu.SemaphoreType.DMA

    def scratch(*dims):
        return pltpu.VMEM(dims, jnp.float32)

    results = pl.pallas_call(
        kernel,
        out_shape=(shape, shape),
        in_specs=[hbm] * 4,
        out_specs=(hbm, hbm),
        scratch_shapes=[
            pltpu.SMEM((STEPS, N_SEC), jnp.int32),
            pltpu.SMEM((N_SEC,), jnp.int32),
            scratch(38, NZ, LX, LY),
            scratch(38, NZ, LX, LY),
            scratch(NZ, 32, 2 * LY),
            scratch(NZ, 32, 2 * LY),
            scratch(4, NZ, LX, LY),
            scratch(38, 4, NZ, LY),
            scratch(2, 2 * LX + NZ, LY),
            scratch(STEPS, 2, 2 * LX + NZ, LY),
            scratch(2, ROLES, 5, LY),
            scratch(N_GY, 5, LY),
            scratch(N_GY, 5, LY),
            scratch(N_GY, 6, LY),
            scratch(STEPS, 2 * ROLES, 6, LY),
            scratch(KINDS, NZ, WIDE),
            scratch(4, NZ, WIDE),
            scratch(14, NZ, WIDE),
            dma((4,)),
            dma((2, 2)),
            dma((3,)),
            dma((4, STEPS)),
        ],
        compiler_params=pltpu.CompilerParams(
            collective_id=0, has_side_effects=True, vmem_limit_bytes=60 * 1024 * 1024
        ),
    )(fluid_dist, order_dist, plane_offset, plane_speed)
    return pl.pallas_call(
        finish,
        out_shape=(shape, shape),
        in_specs=[hbm] * 2,
        out_specs=(hbm, hbm),
        scratch_shapes=[scratch(38, NZ, LX, LY), dma((8,)), dma((8,))],
        compiler_params=pltpu.CompilerParams(vmem_limit_bytes=60 * 1024 * 1024),
    )(*results)


def solution(mesh):
    split = P(None, None, "sec", "gy")
    return jax.shard_map(
        per_device,
        mesh=mesh,
        in_specs=(split, split, P(), P()),
        out_specs=(split, split),
        check_vma=False,
    )
```
